32 devices in a mesh: ctx: 2 (over core), head: 16 (over z, y, x).
Axes of the slice: x: 2, y: 2, z: 4, core: 2. Of those that a mesh axis runs over, the one named last changes fastest.
Arguments:
- queries: bfloat16 [32, 24576], P('ctx', 'head'), may hold values from -8 to 8
- cache: bfloat16 [2048, 576], P(('ctx', 'head')), may hold values from -8 to 8
- key_up_weight: bfloat16 [128, 128, 512], P('head', None, 'ctx'), may hold values from -0.5 to 0.5
- value_up_weight: bfloat16 [128, 128, 512], P('head', None, 'ctx'), may hold values from -1.5 to 1.5
- prior_len: int32 [1], replicated, may hold values from 0 to 2016
Outputs:
- attended: bfloat16 [32, 16384], P('ctx', 'head')
The draws below stay inside these ranges and needn't reach their ends.
All inputs are finite; a program needn't handle non-finite values.
Results may differ from the reference program's by a relative error of at most 0.02.
Values may be sent and summed in bfloat16 or wider, within the bound.
A program may use at most 128 MiB of HBM per device.

```python
import jax
import jax.numpy as jnp
from jax import lax

HEAD_TOTAL = 128
PLAIN_WIDTH = 128
ROTARY_WIDTH = 64
LATENT_WIDTH = 512
VALUE_WIDTH = 128
QTOK = 32
CACHE = 2048


def draw_cache(key, part):
    latent_row_width = LATENT_WIDTH + ROTARY_WIDTH
    sampled_inputs = jnp.clip(jax.random.normal(jax.random.fold_in(key, 1), (CACHE, latent_row_width), jnp.float32), -6.0, 6.0)
    return sampled_inputs.astype(jnp.bfloat16)


def draw_queries(key, part):
    sampled_inputs = jnp.clip(jax.random.normal(jax.random.fold_in(key, 21), (QTOK, HEAD_TOTAL, PLAIN_WIDTH + ROTARY_WIDTH), jnp.float32), -6.0, 6.0)
    return sampled_inputs.reshape(QTOK, HEAD_TOTAL * (PLAIN_WIDTH + ROTARY_WIDTH)).astype(jnp.bfloat16)


def level_of(key, extent, shards, smallest, largest):
    factor_of = 1.0
    for axis_at, blocks in shards:
        draws = jax.random.uniform(jax.random.fold_in(jax.random.fold_in(key, 6), axis_at), (blocks,), jnp.float32, smallest / len(shards), largest / len(shards))
        factor_of = factor_of * jnp.repeat(jnp.exp(draws), extent[axis_at] // blocks).reshape((-1,) + (1,) * (len(extent) - 1 - axis_at))
    return factor_of


def centred(own_key, shape, width, bound, pieces=(), kind=jnp.bfloat16):
    entries = width * jax.random.normal(own_key, shape, jnp.float32)
    if pieces:
        entries = entries * level_of(own_key, shape, pieces, -0.22, 0.18)
    return jnp.clip(entries, -bound, bound).astype(kind)


def setup_inputs(seed: int = 0) -> dict:
    arg_keys = jax.random.split(jax.random.key(seed), 6)
    return {
        "queries": draw_queries(jax.random.fold_in(arg_keys[5], 71), 0),
        "cache": draw_cache(jax.random.fold_in(arg_keys[5], 71), 0),
        "key_up_weight": centred(arg_keys[2], (HEAD_TOTAL, PLAIN_WIDTH, LATENT_WIDTH), PLAIN_WIDTH ** -0.5, 0.5, ((0, 16), (2, 2))),
        "value_up_weight": centred(arg_keys[3], (HEAD_TOTAL, VALUE_WIDTH, LATENT_WIDTH), 0.25, 1.5, ((0, 16), (2, 2))),
        "prior_len": jax.random.randint(arg_keys[4], (1,), 0, CACHE - QTOK + 1).astype(jnp.int32),
    }


def reference(queries, cache, key_up_weight, value_up_weight, prior_len):
    split_rows = queries.reshape(QTOK, HEAD_TOTAL, PLAIN_WIDTH + ROTARY_WIDTH)
    query_place = prior_len[0] + jnp.arange(QTOK, dtype=jnp.int32)
    key_place = jnp.arange(CACHE, dtype=jnp.int32)
    visible = key_place[None, :] <= query_place[:, None]
    key_matrix = cache.astype(jnp.float32)
    value_matrix = key_matrix[:, :LATENT_WIDTH]
    score_scale = (PLAIN_WIDTH + ROTARY_WIDTH) ** -0.5

    def one_head(inputs):
        head_rows, key_panel, value_panel = inputs
        latent = jnp.dot(head_rows[:, :PLAIN_WIDTH], key_panel, preferred_element_type=jnp.float32).astype(jnp.bfloat16)
        joined = jnp.concatenate([latent, head_rows[:, PLAIN_WIDTH:]], axis=1).astype(jnp.float32)
        scores = jnp.dot(joined, key_matrix.T, precision=lax.Precision.HIGHEST) * score_scale
        scores = jnp.where(visible, scores, jnp.float32(-1e30))
        row_peak = jnp.max(scores, axis=1)
        probabilities = jnp.where(visible, jnp.exp(scores - row_peak[:, None]), jnp.float32(0.0))
        row_total = jnp.sum(probabilities, axis=1)
        rounded = probabilities.astype(jnp.bfloat16).astype(jnp.float32)
        latent_out = jnp.dot(rounded, value_matrix, precision=lax.Precision.HIGHEST)
        projected = jnp.dot(latent_out, value_panel.astype(jnp.float32).T, precision=lax.Precision.HIGHEST)
        return (projected / row_total[:, None]).astype(jnp.bfloat16)

    per_head = lax.map(one_head, (jnp.transpose(split_rows, (1, 0, 2)), key_up_weight, value_up_weight))
    return jnp.transpose(per_head, (1, 0, 2)).reshape(QTOK, HEAD_TOTAL * VALUE_WIDTH)
```

```python
import jax
import jax.numpy as jnp
from jax import lax
from jax.experimental import pallas as pl
from jax.experimental.pallas import tpu as pltpu
from jax.sharding import PartitionSpec as P

PLAIN_WIDTH = 128
ROTARY_WIDTH = 64
LATENT_WIDTH = 512
VALUE_WIDTH = 128


def per_device(queries, cache, key_up_weight, value_up_weight, prior_len):
    heads_number = key_up_weight.shape[0]
    block_rows = queries.shape[0]
    combined_width = LATENT_WIDTH + ROTARY_WIDTH
    key_panel, value_panel = (
        lax.all_gather(key_up_weight, "ctx", axis=2, tiled=True),
        lax.all_gather(value_up_weight, "ctx", axis=2, tiled=True),
    )
    gathered = lax.all_gather(queries, "ctx", axis=0, tiled=True)
    split_rows = gathered.reshape(gathered.shape[0], heads_number, PLAIN_WIDTH + ROTARY_WIDTH)
    latent = jnp.einsum(
        "thn,hnc->thc",
        split_rows[:, :, :PLAIN_WIDTH],
        key_panel,
        preferred_element_type=jnp.float32,
    ).astype(jnp.bfloat16)
    flat_queries = jnp.concatenate([latent, split_rows[:, :, PLAIN_WIDTH:]], axis=2).reshape(
        -1, combined_width
    )
    flat_rows = flat_queries.shape[0]
    query_number = flat_rows // heads_number
    query_place = prior_len[0] + jnp.arange(flat_rows, dtype=jnp.int32) // heads_number
    group_slots = cache.shape[0] * lax.axis_size("head")
    block_base = lax.axis_index("ctx") * group_slots
    score_scale = (PLAIN_WIDTH + ROTARY_WIDTH) ** (-0.5)
    key_section = lax.all_gather(cache, "head", axis=0, tiled=True)
    row_peak = jnp.full((flat_rows,), -1e30, jnp.float32)
    key_count = key_section.shape[0]
    scores = (
        jnp.einsum("rc,nc->rn", flat_queries, key_section, preferred_element_type=jnp.float32)
        * score_scale
    )
    key_place = block_base + jnp.arange(key_count, dtype=jnp.int32)
    visible = key_place[None, :] <= query_place[:, None]
    scores = jnp.where(visible, scores, jnp.float32(-1e30))
    new_peak = jnp.maximum(row_peak, jnp.max(scores, axis=1))
    probabilities = jnp.where(visible, jnp.exp(scores - new_peak[:, None]), jnp.float32(0.0))
    row_total = jnp.sum(probabilities, axis=1)
    weighted_values = jnp.dot(
        probabilities.astype(jnp.bfloat16),
        key_section[:, :LATENT_WIDTH],
        preferred_element_type=jnp.float32,
    )
    row_peak, row_total, weighted_values = (new_peak, row_total, weighted_values)
    global_peak = lax.pmax(row_peak, "ctx")
    softmax_scale = jnp.exp(row_peak - global_peak)
    scaled_sums = (row_total * softmax_scale).reshape(query_number, heads_number)
    latent_scaled = (weighted_values * softmax_scale[:, None]).reshape(
        query_number, heads_number * LATENT_WIDTH
    )
    block_latent, own_totals = (
        lax.psum_scatter(
            latent_scaled.astype(jnp.bfloat16), "ctx", scatter_dimension=0, tiled=True
        ).astype(jnp.float32),
        lax.psum_scatter(
            scaled_sums.astype(jnp.bfloat16), "ctx", scatter_dimension=0, tiled=True
        ).astype(jnp.float32),
    )
    reshaped_queries = block_latent.reshape(block_rows, heads_number, LATENT_WIDTH)
    projected = jnp.einsum(
        "thc,hvc->thv",
        reshaped_queries,
        value_panel.astype(jnp.float32),
        precision=lax.Precision.HIGHEST,
    )
    result = projected / own_totals[:, :, None]
    return result.reshape(block_rows, heads_number * VALUE_WIDTH).astype(jnp.bfloat16)


MESH = pl.DeviceIdType.MESH
HEAD_WIDTH = PLAIN_WIDTH + ROTARY_WIDTH
Z_CHIPS, Y_CHIPS, X_CHIPS = 4, 2, 2
LANES = 128


def fused_kernel(
    queries_ref, cache_ref, key_hbm, value_hbm, prior_ref, out_ref,
    mine, other, key_panel, value_panel, query_low, query_high, numerator,
    mine_recv, half_recv, other_recv, other_half_recv, send_sem, panel_sem, local_sem,
):
    core = lax.axis_index("ctx")
    place = lax.axis_index("head")
    z = place // (Y_CHIPS * X_CHIPS)
    y = (place // X_CHIPS) % Y_CHIPS
    x = place % X_CHIPS
    heads = key_hbm.shape[0]
    tokens = queries_ref.shape[0]
    slots = cache_ref.shape[0]
    half_slots = slots // 2
    tiles = LATENT_WIDTH // LANES
    half_rows = mine.shape[2] // 2

    def chip(zz, yy, xx):
        return (zz * Y_CHIPS + yy) * X_CHIPS + xx

    z_of = [z, z + 1 - 2 * (z % 2), (z + 2) % 4, 3 - z]
    x_peer = (core, chip(z, y, 1 - x))
    y_peer = (core, chip(z, 1 - y, x))
    core_peer = (1 - core, place)
    z_peer = [None] + [(core, chip(z_of[k], y, x)) for k in (1, 2, 3)]
    partners = [x_peer, y_peer, core_peer] + z_peer[1:]

    barrier = pltpu.get_barrier_semaphore()
    for partner in partners:
        pl.semaphore_signal(barrier, inc=1, device_id=partner, device_id_type=MESH)

    local = [
        pltpu.make_async_copy(key_hbm, key_panel.at[core], local_sem.at[0]),
        pltpu.make_async_copy(value_hbm, value_panel.at[core], local_sem.at[1]),
    ]
    for copy in local:
        copy.start()
    for c in range(tiles):
        mine[0, 0, c * slots:(c + 1) * slots, :] = cache_ref[:, c * LANES:(c + 1) * LANES]
    rotary = cache_ref[:, LATENT_WIDTH:]
    mine[0, 0, tiles * slots:, :] = jnp.concatenate(
        [rotary[:half_slots], rotary[half_slots:]], axis=1
    )
    pl.semaphore_wait(barrier, len(partners))

    sends = []

    def send(src, dst, recv, to):
        copy = pltpu.make_async_remote_copy(
            src_ref=src, dst_ref=dst, send_sem=send_sem.at[len(sends)], recv_sem=recv,
            device_id=to, device_id_type=MESH,
        )
        copy.start()
        sends.append(copy)

    def arrived(ref, sem):
        pltpu.make_async_copy(ref, ref, sem).wait()

    def rows(ref, k, p, half):
        return ref.at[k, p, pl.ds(half * half_rows, half_rows)]

    def share_column(k):
        block = mine.at[k, 0]
        send(block, mine.at[k, 1], mine_recv.at[k, 1], x_peer)
        send(block, mine.at[k, 2], mine_recv.at[k, 2], y_peer)
        if k == 0:
            for j in (1, 2, 3):
                send(block, mine.at[j, 0], mine_recv.at[j, 0], z_peer[j])
        send(block, other.at[k, 0], other_recv.at[k, 0], core_peer)

    def column_step(k):
        arrived(mine.at[k, 0], mine_recv.at[k, 0])
        share_column(k)

    def plane_step(k):
        arrived(mine.at[k, 1], mine_recv.at[k, 1])
        send(rows(mine, k, 1, 1), rows(mine, k, 3, 1), half_recv.at[k, 1], y_peer)
        send(mine.at[k, 1], other.at[k, 1], other_recv.at[k, 1], core_peer)
        arrived(mine.at[k, 2], mine_recv.at[k, 2])
        send(rows(mine, k, 2, 0), rows(mine, k, 3, 0), half_recv.at[k, 0], x_peer)
        send(mine.at[k, 2], other.at[k, 2], other_recv.at[k, 2], core_peer)

    def diagonal_step(k):
        for half in (0, 1):
            arrived(rows(mine, k, 3, half), half_recv.at[k, half])
            send(rows(mine, k, 3, half), rows(other, k, 3, half), other_half_recv.at[k, half], core_peer)

    def other_arrived(k, p):
        if p < 3:
            arrived(other.at[k, p], other_recv.at[k, p])
        else:
            for half in (0, 1):
                arrived(rows(other, k, 3, half), other_half_recv.at[k, half])

    share_column(0)
    send(key_hbm, key_panel.at[core], panel_sem.at[0], core_peer)
    send(value_hbm, value_panel.at[core], panel_sem.at[1], core_peer)

    def project_queries():
        local[0].wait()
        arrived(key_panel.at[1 - core], panel_sem.at[0])
        zeros = jnp.zeros((tokens, ROTARY_WIDTH), jnp.bfloat16)
        for h in range(heads):
            here = slice(h * tokens, (h + 1) * tokens)
            plain = queries_ref[:, h * HEAD_WIDTH:h * HEAD_WIDTH + PLAIN_WIDTH]
            rotary = queries_ref[:, h * HEAD_WIDTH + PLAIN_WIDTH:(h + 1) * HEAD_WIDTH]
            for c in (0, 1):
                latent = jnp.dot(
                    plain, key_panel[c, h], preferred_element_type=jnp.float32
                ).astype(jnp.bfloat16)
                width = latent.shape[1]
                query_low[here, c * width:(c + 1) * width] = latent
                query_high[here, c * width:(c + 1) * width] = latent
            query_low[here, LATENT_WIDTH:] = jnp.concatenate([rotary, zeros], axis=1)
            query_high[here, LATENT_WIDTH:] = jnp.concatenate([zeros, rotary], axis=1)

    flat_rows = heads * tokens
    score_scale = HEAD_WIDTH ** (-0.5)
    row_token = lax.broadcasted_iota(jnp.int32, (flat_rows, 1), 0) % tokens
    query_place = prior_ref[0] + core * tokens + row_token
    group_slots = slots * Z_CHIPS * Y_CHIPS * X_CHIPS

    def attend(state, k, positions):
        blocks = []
        for p in positions:
            source = chip(z_of[k], 1 - y if p in (2, 3) else y, 1 - x if p in (1, 3) else x)
            blocks.append((mine, p, core * group_slots + source * slots))
            blocks.append((other, p, (1 - core) * group_slots + source * slots))
        count = len(blocks)
        width = count * half_slots

        def latent_of(part):
            return jnp.concatenate(
                [
                    jnp.concatenate(
                        [
                            ref[k, p, pl.ds(c * slots + part * half_slots, half_slots), :]
                            for c in range(tiles)
                        ],
                        axis=1,
                    )
                    for ref, p, _ in blocks
                ],
                axis=0,
            )

        rotary = jnp.concatenate(
            [ref[k, p, pl.ds(tiles * slots, half_slots), :] for ref, p, _ in blocks], axis=0
        )
        column = lax.broadcasted_iota(jnp.int32, (1, width), 1)
        key_place = column
        for b, (_, _, base) in enumerate(blocks):
            inside = (column >= b * half_slots) & (column < (b + 1) * half_slots)
            key_place = key_place + jnp.where(inside, base - b * half_slots, 0)
        latents, scores, visible = [], [], []
        for part, query in ((0, query_low), (1, query_high)):
            latent = latent_of(part)
            score = lax.dot_general(
                query[...], jnp.concatenate([latent, rotary], axis=1),
                (((1,), (1,)), ((), ())), preferred_element_type=jnp.float32,
            ) * score_scale
            seen = key_place + part * half_slots <= query_place
            latents.append(latent)
            visible.append(seen)
            scores.append(jnp.where(seen, score, -1e30))
        peak = jnp.max(jnp.maximum(scores[0], scores[1]), axis=1, keepdims=True)
        if state is not None:
            peak = jnp.maximum(peak, state[0])
        probs = [
            jnp.where(seen, jnp.exp(score - peak), 0.0)
            for seen, score in zip(visible, scores)
        ]
        total = jnp.sum(probs[0] + probs[1], axis=1, keepdims=True)
        weighted = jnp.dot(
            jnp.concatenate([prob.astype(jnp.bfloat16) for prob in probs], axis=1),
            jnp.concatenate(latents, axis=0),
            preferred_element_type=jnp.float32,
        )
        if state is None:
            numerator[...] = weighted
        else:
            shrink = jnp.exp(state[0] - peak)
            total = total + state[1] * shrink
            numerator[...] = numerator[...] * shrink + weighted
        return peak, total

    project_queries()
    plane_step(0)
    column_step(1)
    diagonal_step(0)
    plane_step(1)
    for p in range(4):
        other_arrived(0, p)
    state = attend(None, 0, (0, 1, 2, 3))
    column_step(2)
    diagonal_step(1)
    plane_step(2)
    column_step(3)
    for p in range(4):
        other_arrived(1, p)
    state = attend(state, 1, (0, 1, 2, 3))
    diagonal_step(2)
    plane_step(3)
    for p in range(4):
        other_arrived(2, p)
    state = attend(state, 2, (0, 1, 2, 3))
    other_arrived(3, 0)
    other_arrived(3, 1)
    state = attend(state, 3, (0, 1))
    diagonal_step(3)
    other_arrived(3, 2)
    other_arrived(3, 3)
    peak, total = attend(state, 3, (2, 3))

    local[1].wait()
    arrived(value_panel.at[1 - core], panel_sem.at[1])
    averaged = numerator[...] / total
    for h in range(heads):
        here = slice(h * tokens, (h + 1) * tokens)
        result = None
        for c in (0, 1):
            width = value_panel.shape[3]
            term = lax.dot_general(
                averaged[here, c * width:(c + 1) * width].astype(jnp.bfloat16),
                value_panel[c, h],
                (((1,), (1,)), ((), ())), preferred_element_type=jnp.float32,
            )
            result = term if result is None else result + term
        out_ref[:, h * VALUE_WIDTH:(h + 1) * VALUE_WIDTH] = result.astype(jnp.bfloat16)
    for copy in sends:
        copy.wait_send()


def per_device_fused(queries, cache, key_up_weight, value_up_weight, prior_len):
    heads = key_up_weight.shape[0]
    tokens = queries.shape[0]
    slots = cache.shape[0]
    block_rows = slots * cache.shape[1] // LANES
    flat_rows = heads * tokens
    vmem = pl.BlockSpec(memory_space=pltpu.VMEM)
    dma = pltpu.SemaphoreType.DMA
    return pl.pallas_call(
        fused_kernel,
        out_shape=jax.ShapeDtypeStruct((tokens, heads * VALUE_WIDTH), jnp.bfloat16),
        in_specs=[
            vmem, vmem, pl.BlockSpec(memory_space=pl.ANY), pl.BlockSpec(memory_space=pl.ANY),
            pl.BlockSpec(memory_space=pltpu.SMEM),
        ],
        out_specs=vmem,
        scratch_shapes=[
            pltpu.VMEM((4, 4, block_rows, LANES), jnp.bfloat16),
            pltpu.VMEM((4, 4, block_rows, LANES), jnp.bfloat16),
            pltpu.VMEM((2,) + key_up_weight.shape, jnp.bfloat16),
            pltpu.VMEM((2,) + value_up_weight.shape, jnp.bfloat16),
            pltpu.VMEM((flat_rows, LATENT_WIDTH + LANES), jnp.bfloat16),
            pltpu.VMEM((flat_rows, LATENT_WIDTH + LANES), jnp.bfloat16),
            pltpu.VMEM((flat_rows, LATENT_WIDTH), jnp.float32),
            dma((4, 3)), dma((4, 2)), dma((4, 3)), dma((4, 2)), dma((48,)), dma((2,)), dma((2,)),
        ],
        compiler_params=pltpu.CompilerParams(
            collective_id=0, has_side_effects=True, vmem_limit_bytes=40 * 1024 * 1024
        ),
        cost_estimate=pl.CostEstimate(
            flops=2 * flat_rows * slots * 32 * 1088, bytes_accessed=4 * 1024 * 1024,
            transcendentals=flat_rows * slots * 32,
        ),
    )(queries, cache, key_up_weight, value_up_weight, prior_len)


def solution(mesh):
    in_specs = (
        P("ctx", "head"),
        P(("ctx", "head"), None),
        P("head", None, "ctx"),
        P("head", None, "ctx"),
        P(),
    )
    out_specs = P("ctx", "head")
    chips = Z_CHIPS * Y_CHIPS * X_CHIPS
    body = per_device_fused if mesh.shape["ctx"] == 2 and mesh.shape["head"] == chips else per_device
    return jax.shard_map(
        body, mesh=mesh, in_specs=in_specs, out_specs=out_specs, check_vma=False
    )
```

```python
import jax
import jax.numpy as jnp
from jax import lax
from jax.experimental import pallas as pl
from jax.experimental.pallas import tpu as pltpu
from jax.sharding import PartitionSpec as P

PLAIN_WIDTH = 128
ROTARY_WIDTH = 64
LATENT_WIDTH = 512
VALUE_WIDTH = 128


def per_device(queries, cache, key_up_weight, value_up_weight, prior_len):
    heads_number = key_up_weight.shape[0]
    block_rows = queries.shape[0]
    combined_width = LATENT_WIDTH + ROTARY_WIDTH
    key_panel, value_panel = (
        lax.all_gather(key_up_weight, "ctx", axis=2, tiled=True),
        lax.all_gather(value_up_weight, "ctx", axis=2, tiled=True),
    )
    gathered = lax.all_gather(queries, "ctx", axis=0, tiled=True)
    split_rows = gathered.reshape(gathered.shape[0], heads_number, PLAIN_WIDTH + ROTARY_WIDTH)
    latent = jnp.einsum(
        "thn,hnc->thc",
        split_rows[:, :, :PLAIN_WIDTH],
        key_panel,
        preferred_element_type=jnp.float32,
    ).astype(jnp.bfloat16)
    flat_queries = jnp.concatenate([latent, split_rows[:, :, PLAIN_WIDTH:]], axis=2).reshape(
        -1, combined_width
    )
    flat_rows = flat_queries.shape[0]
    query_number = flat_rows // heads_number
    query_place = prior_len[0] + jnp.arange(flat_rows, dtype=jnp.int32) // heads_number
    group_slots = cache.shape[0] * lax.axis_size("head")
    block_base = lax.axis_index("ctx") * group_slots
    score_scale = (PLAIN_WIDTH + ROTARY_WIDTH) ** (-0.5)
    key_section = lax.all_gather(cache, "head", axis=0, tiled=True)
    row_peak = jnp.full((flat_rows,), -1e30, jnp.float32)
    key_count = key_section.shape[0]
    scores = (
        jnp.einsum("rc,nc->rn", flat_queries, key_section, preferred_element_type=jnp.float32)
        * score_scale
    )
    key_place = block_base + jnp.arange(key_count, dtype=jnp.int32)
    visible = key_place[None, :] <= query_place[:, None]
    scores = jnp.where(visible, scores, jnp.float32(-1e30))
    new_peak = jnp.maximum(row_peak, jnp.max(scores, axis=1))
    probabilities = jnp.where(visible, jnp.exp(scores - new_peak[:, None]), jnp.float32(0.0))
    row_total = jnp.sum(probabilities, axis=1)
    weighted_values = jnp.dot(
        probabilities.astype(jnp.bfloat16),
        key_section[:, :LATENT_WIDTH],
        preferred_element_type=jnp.float32,
    )
    row_peak, row_total, weighted_values = (new_peak, row_total, weighted_values)
    global_peak = lax.pmax(row_peak, "ctx")
    softmax_scale = jnp.exp(row_peak - global_peak)
    scaled_sums = (row_total * softmax_scale).reshape(query_number, heads_number)
    latent_scaled = (weighted_values * softmax_scale[:, None]).reshape(
        query_number, heads_number * LATENT_WIDTH
    )
    block_latent, own_totals = (
        lax.psum_scatter(
            latent_scaled.astype(jnp.bfloat16), "ctx", scatter_dimension=0, tiled=True
        ).astype(jnp.float32),
        lax.psum_scatter(
            scaled_sums.astype(jnp.bfloat16), "ctx", scatter_dimension=0, tiled=True
        ).astype(jnp.float32),
    )
    reshaped_queries = block_latent.reshape(block_rows, heads_number, LATENT_WIDTH)
    projected = jnp.einsum(
        "thc,hvc->thv",
        reshaped_queries,
        value_panel.astype(jnp.float32),
        precision=lax.Precision.HIGHEST,
    )
    result = projected / own_totals[:, :, None]
    return result.reshape(block_rows, heads_number * VALUE_WIDTH).astype(jnp.bfloat16)


MESH = pl.DeviceIdType.MESH
HEAD_WIDTH = PLAIN_WIDTH + ROTARY_WIDTH
Z_CHIPS, Y_CHIPS, X_CHIPS = 4, 2, 2
LANES = 128


def fused_kernel(
    queries_hbm, cache_hbm, key_hbm, value_hbm, prior_ref, out_ref,
    queries_ref, cache_ref, mine, other, key_panel, value_panel, query_low, query_high, numerator,
    mine_recv, half_recv, other_recv, other_half_recv, send_sem, panel_sem, local_sem,
):
    core = lax.axis_index("ctx")
    place = lax.axis_index("head")
    z = place // (Y_CHIPS * X_CHIPS)
    y = (place // X_CHIPS) % Y_CHIPS
    x = place % X_CHIPS
    heads = key_hbm.shape[0]
    tokens = queries_ref.shape[0]
    slots = cache_ref.shape[0]
    half_slots = slots // 2
    tiles = LATENT_WIDTH // LANES
    half_rows = mine.shape[2] // 2

    def chip(zz, yy, xx):
        return (zz * Y_CHIPS + yy) * X_CHIPS + xx

    z_of = [z, z + 1 - 2 * (z % 2), (z + 2) % 4, 3 - z]
    x_peer = (core, chip(z, y, 1 - x))
    y_peer = (core, chip(z, 1 - y, x))
    core_peer = (1 - core, place)
    z_peer = [None] + [(core, chip(z_of[k], y, x)) for k in (1, 2, 3)]
    partners = [x_peer, y_peer, core_peer] + z_peer[1:]

    barrier = pltpu.get_barrier_semaphore()
    for partner in partners:
        pl.semaphore_signal(barrier, inc=1, device_id=partner, device_id_type=MESH)

    local = [
        pltpu.make_async_copy(key_hbm, key_panel.at[core], local_sem.at[0]),
        pltpu.make_async_copy(value_hbm, value_panel.at[core], local_sem.at[1]),
        pltpu.make_async_copy(queries_hbm, queries_ref, local_sem.at[2]),
    ]
    fetch = pltpu.make_async_copy(cache_hbm, cache_ref, local_sem.at[3])
    fetch.start()
    for copy in local:
        copy.start()
    fetch.wait()
    for c in range(tiles):
        mine[0, 0, c * slots:(c + 1) * slots, :] = cache_ref[:, c * LANES:(c + 1) * LANES]
    rotary = cache_ref[:, LATENT_WIDTH:]
    mine[0, 0, tiles * slots:, :] = jnp.concatenate(
        [rotary[:half_slots], rotary[half_slots:]], axis=1
    )
    pl.semaphore_wait(barrier, len(partners))

    sends = []

    def send(src, dst, recv, to):
        copy = pltpu.make_async_remote_copy(
            src_ref=src, dst_ref=dst, send_sem=send_sem.at[len(sends)], recv_sem=recv,
            device_id=to, device_id_type=MESH,
        )
        copy.start()
        sends.append(copy)

    def arrived(ref, sem):
        pltpu.make_async_copy(ref, ref, sem).wait()

    def rows(ref, k, p, half):
        return ref.at[k, p, pl.ds(half * half_rows, half_rows)]

    def share_column(k):
        block = mine.at[k, 0]
        send(block, mine.at[k, 1], mine_recv.at[k, 1], x_peer)
        send(block, mine.at[k, 2], mine_recv.at[k, 2], y_peer)
        if k == 0:
            for j in (1, 2, 3):
                send(block, mine.at[j, 0], mine_recv.at[j, 0], z_peer[j])
        send(block, other.at[k, 0], other_recv.at[k, 0], core_peer)

    def column_step(k):
        arrived(mine.at[k, 0], mine_recv.at[k, 0])
        share_column(k)

    def plane_step(k):
        arrived(mine.at[k, 1], mine_recv.at[k, 1])
        send(rows(mine, k, 1, 1), rows(mine, k, 3, 1), half_recv.at[k, 1], y_peer)
        send(mine.at[k, 1], other.at[k, 1], other_recv.at[k, 1], core_peer)
        arrived(mine.at[k, 2], mine_recv.at[k, 2])
        send(rows(mine, k, 2, 0), rows(mine, k, 3, 0), half_recv.at[k, 0], x_peer)
        send(mine.at[k, 2], other.at[k, 2], other_recv.at[k, 2], core_peer)

    def diagonal_step(k):
        for half in (0, 1):
            arrived(rows(mine, k, 3, half), half_recv.at[k, half])
            send(rows(mine, k, 3, half), rows(other, k, 3, half), other_half_recv.at[k, half], core_peer)

    def other_arrived(k, p):
        if p < 3:
            arrived(other.at[k, p], other_recv.at[k, p])
        else:
            for half in (0, 1):
                arrived(rows(other, k, 3, half), other_half_recv.at[k, half])

    share_column(0)
    send(key_hbm, key_panel.at[core], panel_sem.at[0], core_peer)

    def project_queries():
        local[0].wait()
        local[2].wait()
        arrived(key_panel.at[1 - core], panel_sem.at[0])
        zeros = jnp.zeros((tokens, ROTARY_WIDTH), jnp.bfloat16)
        for h in range(heads):
            here = slice(h * tokens, (h + 1) * tokens)
            plain = queries_ref[:, h * HEAD_WIDTH:h * HEAD_WIDTH + PLAIN_WIDTH]
            rotary = queries_ref[:, h * HEAD_WIDTH + PLAIN_WIDTH:(h + 1) * HEAD_WIDTH]
            for c in (0, 1):
                latent = jnp.dot(
                    plain, key_panel[c, h], preferred_element_type=jnp.float32
                ).astype(jnp.bfloat16)
                width = latent.shape[1]
                query_low[here, c * width:(c + 1) * width] = latent
                query_high[here, c * width:(c + 1) * width] = latent
            query_low[here, LATENT_WIDTH:] = jnp.concatenate([rotary, zeros], axis=1)
            query_high[here, LATENT_WIDTH:] = jnp.concatenate([zeros, rotary], axis=1)

    flat_rows = heads * tokens
    score_scale = HEAD_WIDTH ** (-0.5)
    row_token = lax.broadcasted_iota(jnp.int32, (flat_rows, 1), 0) % tokens
    query_place = prior_ref[0] + core * tokens + row_token
    group_slots = slots * Z_CHIPS * Y_CHIPS * X_CHIPS

    def attend(state, k, positions):
        blocks = []
        for p in positions:
            source = chip(z_of[k], 1 - y if p in (2, 3) else y, 1 - x if p in (1, 3) else x)
            blocks.append((mine, p, core * group_slots + source * slots))
            blocks.append((other, p, (1 - core) * group_slots + source * slots))
        count = len(blocks)
        width = count * half_slots

        def latent_of(part):
            return jnp.concatenate(
                [
                    jnp.concatenate(
                        [
                            ref[k, p, pl.ds(c * slots + part * half_slots, half_slots), :]
                            for c in range(tiles)
                        ],
                        axis=1,
                    )
                    for ref, p, _ in blocks
                ],
                axis=0,
            )

        rotary = jnp.concatenate(
            [ref[k, p, pl.ds(tiles * slots, half_slots), :] for ref, p, _ in blocks], axis=0
        )
        column = lax.broadcasted_iota(jnp.int32, (1, width), 1)
        key_place = column
        for b, (_, _, base) in enumerate(blocks):
            inside = (column >= b * half_slots) & (column < (b + 1) * half_slots)
            key_place = key_place + jnp.where(inside, base - b * half_slots, 0)
        latents, scores, visible = [], [], []
        for part, query in ((0, query_low), (1, query_high)):
            latent = latent_of(part)
            score = lax.dot_general(
                query[...], jnp.concatenate([latent, rotary], axis=1),
                (((1,), (1,)), ((), ())), preferred_element_type=jnp.float32,
            ) * score_scale
            seen = key_place + part * half_slots <= query_place
            latents.append(latent)
            visible.append(seen)
            scores.append(jnp.where(seen, score, -1e30))
        peak = jnp.max(jnp.maximum(scores[0], scores[1]), axis=1, keepdims=True)
        if state is not None:
            peak = jnp.maximum(peak, state[0])
        probs = [
            jnp.where(seen, jnp.exp(score - peak), 0.0)
            for seen, score in zip(visible, scores)
        ]
        total = jnp.sum(probs[0] + probs[1], axis=1, keepdims=True)
        weighted = jnp.dot(
            jnp.concatenate([prob.astype(jnp.bfloat16) for prob in probs], axis=1),
            jnp.concatenate(latents, axis=0),
            preferred_element_type=jnp.float32,
        )
        if state is None:
            numerator[...] = weighted
        else:
            shrink = jnp.exp(state[0] - peak)
            total = total + state[1] * shrink
            numerator[...] = numerator[...] * shrink + weighted
        return peak, total

    def piece(state, k, positions):
        for p in positions:
            other_arrived(k, p)
        return attend(state, k, positions)

    project_queries()
    plane_step(0)
    send(value_hbm, value_panel.at[core], panel_sem.at[1], core_peer)
    column_step(1)
    state = piece(None, 0, (0, 1))
    column_step(2)
    diagonal_step(0)
    plane_step(1)
    state = piece(state, 0, (2, 3))
    column_step(3)
    diagonal_step(1)
    state = piece(state, 1, (0, 1))
    plane_step(2)
    state = piece(state, 1, (2, 3))
    diagonal_step(2)
    plane_step(3)
    state = piece(state, 2, (0, 1, 2, 3))
    state = piece(state, 3, (0, 1))
    diagonal_step(3)
    peak, total = piece(state, 3, (2, 3))

    local[1].wait()
    arrived(value_panel.at[1 - core], panel_sem.at[1])
    averaged = numerator[...] / total
    for h in range(heads):
        here = slice(h * tokens, (h + 1) * tokens)
        result = None
        for c in (0, 1):
            width = value_panel.shape[3]
            term = lax.dot_general(
                averaged[here, c * width:(c + 1) * width].astype(jnp.bfloat16),
                value_panel[c, h],
                (((1,), (1,)), ((), ())), preferred_element_type=jnp.float32,
            )
            result = term if result is None else result + term
        out_ref[:, h * VALUE_WIDTH:(h + 1) * VALUE_WIDTH] = result.astype(jnp.bfloat16)
    for copy in sends:
        copy.wait_send()


def per_device_fused(queries, cache, key_up_weight, value_up_weight, prior_len):
    heads = key_up_weight.shape[0]
    tokens = queries.shape[0]
    slots = cache.shape[0]
    block_rows = slots * cache.shape[1] // LANES
    flat_rows = heads * tokens
    vmem = pl.BlockSpec(memory_space=pltpu.VMEM)
    hbm = pl.BlockSpec(memory_space=pltpu.HBM)
    dma = pltpu.SemaphoreType.DMA
    return pl.pallas_call(
        fused_kernel,
        out_shape=jax.ShapeDtypeStruct((tokens, heads * VALUE_WIDTH), jnp.bfloat16),
        in_specs=[
            hbm, hbm, hbm, hbm, pl.BlockSpec(memory_space=pltpu.SMEM),
        ],
        out_specs=vmem,
        scratch_shapes=[
            pltpu.VMEM(queries.shape, jnp.bfloat16),
            pltpu.VMEM(cache.shape, jnp.bfloat16),
            pltpu.VMEM((4, 4, block_rows, LANES), jnp.bfloat16),
            pltpu.VMEM((4, 4, block_rows, LANES), jnp.bfloat16),
            pltpu.VMEM((2,) + key_up_weight.shape, jnp.bfloat16),
            pltpu.VMEM((2,) + value_up_weight.shape, jnp.bfloat16),
            pltpu.VMEM((flat_rows, LATENT_WIDTH + LANES), jnp.bfloat16),
            pltpu.VMEM((flat_rows, LATENT_WIDTH + LANES), jnp.bfloat16),
            pltpu.VMEM((flat_rows, LATENT_WIDTH), jnp.float32),
            dma((4, 3)), dma((4, 2)), dma((4, 3)), dma((4, 2)), dma((48,)), dma((2,)), dma((4,)),
        ],
        compiler_params=pltpu.CompilerParams(
            collective_id=0, has_side_effects=True, vmem_limit_bytes=40 * 1024 * 1024
        ),
        cost_estimate=pl.CostEstimate(
            flops=2 * flat_rows * slots * 32 * 1088, bytes_accessed=4 * 1024 * 1024,
            transcendentals=flat_rows * slots * 32,
        ),
    )(queries, cache, key_up_weight, value_up_weight, prior_len)


def solution(mesh):
    in_specs = (
        P("ctx", "head"),
        P(("ctx", "head"), None),
        P("head", None, "ctx"),
        P("head", None, "ctx"),
        P(),
    )
    out_specs = P("ctx", "head")
    chips = Z_CHIPS * Y_CHIPS * X_CHIPS
    body = per_device_fused if mesh.shape["ctx"] == 2 and mesh.shape["head"] == chips else per_device
    return jax.shard_map(
        body, mesh=mesh, in_specs=in_specs, out_specs=out_specs, check_vma=False
    )
```

```python
import jax
import jax.numpy as jnp
from jax import lax
from jax.experimental import pallas as pl
from jax.experimental.pallas import tpu as pltpu
from jax.sharding import PartitionSpec as P

PLAIN_WIDTH = 128
ROTARY_WIDTH = 64
LATENT_WIDTH = 512
VALUE_WIDTH = 128


def per_device(queries, cache, key_up_weight, value_up_weight, prior_len):
    heads_number = key_up_weight.shape[0]
    block_rows = queries.shape[0]
    combined_width = LATENT_WIDTH + ROTARY_WIDTH
    key_panel, value_panel = (
        lax.all_gather(key_up_weight, "ctx", axis=2, tiled=True),
        lax.all_gather(value_up_weight, "ctx", axis=2, tiled=True),
    )
    gathered = lax.all_gather(queries, "ctx", axis=0, tiled=True)
    split_rows = gathered.reshape(gathered.shape[0], heads_number, PLAIN_WIDTH + ROTARY_WIDTH)
    latent = jnp.einsum(
        "thn,hnc->thc",
        split_rows[:, :, :PLAIN_WIDTH],
        key_panel,
        preferred_element_type=jnp.float32,
    ).astype(jnp.bfloat16)
    flat_queries = jnp.concatenate([latent, split_rows[:, :, PLAIN_WIDTH:]], axis=2).reshape(
        -1, combined_width
    )
    flat_rows = flat_queries.shape[0]
    query_number = flat_rows // heads_number
    query_place = prior_len[0] + jnp.arange(flat_rows, dtype=jnp.int32) // heads_number
    group_slots = cache.shape[0] * lax.axis_size("head")
    block_base = lax.axis_index("ctx") * group_slots
    score_scale = (PLAIN_WIDTH + ROTARY_WIDTH) ** (-0.5)
    key_section = lax.all_gather(cache, "head", axis=0, tiled=True)
    row_peak = jnp.full((flat_rows,), -1e30, jnp.float32)
    key_count = key_section.shape[0]
    scores = (
        jnp.einsum("rc,nc->rn", flat_queries, key_section, preferred_element_type=jnp.float32)
        * score_scale
    )
    key_place = block_base + jnp.arange(key_count, dtype=jnp.int32)
    visible = key_place[None, :] <= query_place[:, None]
    scores = jnp.where(visible, scores, jnp.float32(-1e30))
    new_peak = jnp.maximum(row_peak, jnp.max(scores, axis=1))
    probabilities = jnp.where(visible, jnp.exp(scores - new_peak[:, None]), jnp.float32(0.0))
    row_total = jnp.sum(probabilities, axis=1)
    weighted_values = jnp.dot(
        probabilities.astype(jnp.bfloat16),
        key_section[:, :LATENT_WIDTH],
        preferred_element_type=jnp.float32,
    )
    row_peak, row_total, weighted_values = (new_peak, row_total, weighted_values)
    global_peak = lax.pmax(row_peak, "ctx")
    softmax_scale = jnp.exp(row_peak - global_peak)
    scaled_sums = (row_total * softmax_scale).reshape(query_number, heads_number)
    latent_scaled = (weighted_values * softmax_scale[:, None]).reshape(
        query_number, heads_number * LATENT_WIDTH
    )
    block_latent, own_totals = (
        lax.psum_scatter(
            latent_scaled.astype(jnp.bfloat16), "ctx", scatter_dimension=0, tiled=True
        ).astype(jnp.float32),
        lax.psum_scatter(
            scaled_sums.astype(jnp.bfloat16), "ctx", scatter_dimension=0, tiled=True
        ).astype(jnp.float32),
    )
    reshaped_queries = block_latent.reshape(block_rows, heads_number, LATENT_WIDTH)
    projected = jnp.einsum(
        "thc,hvc->thv",
        reshaped_queries,
        value_panel.astype(jnp.float32),
        precision=lax.Precision.HIGHEST,
    )
    result = projected / own_totals[:, :, None]
    return result.reshape(block_rows, heads_number * VALUE_WIDTH).astype(jnp.bfloat16)


MESH = pl.DeviceIdType.MESH
HEAD_WIDTH = PLAIN_WIDTH + ROTARY_WIDTH
Z_CHIPS, Y_CHIPS, X_CHIPS = 4, 2, 2
LANES = 128


def fused_kernel(
    queries_hbm, cache_hbm, key_hbm, value_hbm, prior_ref, out_ref,
    queries_ref, cache_ref, mine, key_half, value_panel, query_latent, query_rotary,
    numerator, own_part, peer_part, own_stats, peer_stats,
    mine_recv, half_recv, send_sem, core_recv, local_sem,
):
    core = lax.axis_index("ctx")
    place = lax.axis_index("head")
    z = place // (Y_CHIPS * X_CHIPS)
    y = (place // X_CHIPS) % Y_CHIPS
    x = place % X_CHIPS
    heads = key_hbm.shape[0]
    tokens = queries_hbm.shape[0]
    slots = cache_hbm.shape[0]
    half_slots = slots // 2
    tiles = LATENT_WIDTH // LANES
    half_rows = mine.shape[2] // 2
    core_rows = heads * tokens
    flat_rows = 2 * core_rows

    def chip(zz, yy, xx):
        return (zz * Y_CHIPS + yy) * X_CHIPS + xx

    z_of = [z, z + 1 - 2 * (z % 2), (z + 2) % 4, 3 - z]
    x_peer = (core, chip(z, y, 1 - x))
    y_peer = (core, chip(z, 1 - y, x))
    core_peer = (1 - core, place)
    z_peer = [None] + [(core, chip(z_of[k], y, x)) for k in (1, 2, 3)]
    partners = [x_peer, y_peer, core_peer] + z_peer[1:]

    barrier = pltpu.get_barrier_semaphore()
    for partner in partners:
        pl.semaphore_signal(barrier, inc=1, device_id=partner, device_id_type=MESH)

    local = [
        pltpu.make_async_copy(cache_hbm, cache_ref, local_sem.at[0]),
        pltpu.make_async_copy(queries_hbm, queries_ref.at[core], local_sem.at[1]),
        pltpu.make_async_copy(key_hbm, key_half, local_sem.at[2]),
        pltpu.make_async_copy(value_hbm, value_panel.at[core], local_sem.at[3]),
    ]
    for copy in local:
        copy.start()
    local[0].wait()
    for c in range(tiles):
        mine[0, 0, c * slots:(c + 1) * slots, :] = cache_ref[:, c * LANES:(c + 1) * LANES]
    rotary_keys = cache_ref[:, LATENT_WIDTH:]
    mine[0, 0, tiles * slots:, :] = jnp.concatenate(
        [rotary_keys[:half_slots], rotary_keys[half_slots:]], axis=1
    )
    pl.semaphore_wait(barrier, len(partners))

    sends = []

    def send(src, dst, recv, to):
        copy = pltpu.make_async_remote_copy(
            src_ref=src, dst_ref=dst, send_sem=send_sem.at[len(sends)], recv_sem=recv,
            device_id=to, device_id_type=MESH,
        )
        copy.start()
        sends.append(copy)

    def arrived(ref, sem):
        pltpu.make_async_copy(ref, ref, sem).wait()

    def rows(k, p, half):
        return mine.at[k, p, pl.ds(half * half_rows, half_rows)]

    def share_column(k):
        block = mine.at[k, 0]
        send(block, mine.at[k, 1], mine_recv.at[k, 1], x_peer)
        send(block, mine.at[k, 2], mine_recv.at[k, 2], y_peer)

    def column_step(k):
        arrived(mine.at[k, 0], mine_recv.at[k, 0])
        share_column(k)

    def plane_step(k):
        arrived(mine.at[k, 1], mine_recv.at[k, 1])
        send(rows(k, 1, 1), rows(k, 3, 1), half_recv.at[k, 1], y_peer)
        arrived(mine.at[k, 2], mine_recv.at[k, 2])
        send(rows(k, 2, 0), rows(k, 3, 0), half_recv.at[k, 0], x_peer)

    def diagonal_step(k):
        for half in (0, 1):
            arrived(rows(k, 3, half), half_recv.at[k, half])

    def project_queries():
        local[2].wait()
        arrived(queries_ref.at[1 - core], core_recv.at[0])
        zeros = jnp.zeros((2 * tokens, ROTARY_WIDTH), jnp.bfloat16)
        both = jnp.concatenate([queries_ref[0], queries_ref[1]], axis=0)
        for h in range(heads):
            plain = both[:, h * HEAD_WIDTH:h * HEAD_WIDTH + PLAIN_WIDTH]
            rotary = both[:, h * HEAD_WIDTH + PLAIN_WIDTH:(h + 1) * HEAD_WIDTH]
            latent = jnp.dot(
                plain, key_half[h], preferred_element_type=jnp.float32
            ).astype(jnp.bfloat16)
            low = jnp.concatenate([rotary, zeros], axis=1)
            high = jnp.concatenate([zeros, rotary], axis=1)
            for c in (0, 1):
                there = slice(c * core_rows + h * tokens, c * core_rows + (h + 1) * tokens)
                of = slice(c * tokens, (c + 1) * tokens)
                query_latent[core, there, :] = latent[of]
                query_rotary[0, there, :] = low[of]
                query_rotary[1, there, :] = high[of]

    score_scale = HEAD_WIDTH ** (-0.5)
    flat_row = lax.broadcasted_iota(jnp.int32, (flat_rows, 1), 0)
    query_place = prior_ref[0] + flat_row // core_rows * tokens + flat_row % tokens
    group_slots = slots * Z_CHIPS * Y_CHIPS * X_CHIPS

    def attend(state, k):
        bases = []
        for p in range(4):
            source = chip(z_of[k], 1 - y if p in (2, 3) else y, 1 - x if p in (1, 3) else x)
            bases.append(core * group_slots + source * slots)
        width = 4 * half_slots

        def latent_of(part):
            return jnp.concatenate(
                [
                    jnp.concatenate(
                        [
                            mine[k, p, pl.ds(c * slots + part * half_slots, half_slots), :]
                            for c in range(tiles)
                        ],
                        axis=1,
                    )
                    for p in range(4)
                ],
                axis=0,
            )

        latents = jnp.concatenate([latent_of(0), latent_of(1)], axis=0)
        rotary = jnp.concatenate(
            [mine[k, p, pl.ds(tiles * slots, half_slots), :] for p in range(4)], axis=0
        )
        column = lax.broadcasted_iota(jnp.int32, (1, 2 * width), 1)
        key_place = column
        for b in range(8):
            inside = (column >= b * half_slots) & (column < (b + 1) * half_slots)
            shift = bases[b % 4] + (b // 4) * half_slots - b * half_slots
            key_place = key_place + jnp.where(inside, shift, 0)
        contract = (((1,), (1,)), ((), ()))
        rotary_scores = [
            lax.dot_general(
                query_rotary[part], rotary, contract, preferred_element_type=jnp.float32
            )
            for part in (0, 1)
        ]
        scores = lax.dot_general(
            jnp.concatenate([query_latent[0], query_latent[1]], axis=1), latents, contract,
            preferred_element_type=jnp.float32,
        )
        scores = (scores + jnp.concatenate(rotary_scores, axis=1)) * score_scale
        visible = key_place <= query_place
        scores = jnp.where(visible, scores, -1e30)
        peak = jnp.max(scores, axis=1, keepdims=True)
        if state is not None:
            peak = jnp.maximum(peak, state[0])
        probs = jnp.where(visible, jnp.exp(scores - peak), 0.0)
        total = jnp.sum(probs, axis=1, keepdims=True)
        weighted = jnp.dot(
            probs.astype(jnp.bfloat16), latents, preferred_element_type=jnp.float32
        )
        if state is None:
            numerator[...] = weighted
        else:
            shrink = jnp.exp(state[0] - peak)
            total = total + state[1] * shrink
            numerator[...] = numerator[...] * shrink + weighted
        return peak, total

    share_column(0)
    for k in (1, 2, 3):
        send(mine.at[0, 0], mine.at[k, 0], mine_recv.at[k, 0], z_peer[k])
    send(queries_hbm, queries_ref.at[core], core_recv.at[0], core_peer)
    local[1].wait()
    project_queries()
    send(query_latent.at[core], query_latent.at[core], core_recv.at[1], core_peer)
    plane_step(0)
    column_step(1)
    send(value_hbm, value_panel.at[core], core_recv.at[2], core_peer)
    diagonal_step(0)
    arrived(query_latent.at[1 - core], core_recv.at[1])
    state = attend(None, 0)
    column_step(2)
    plane_step(1)
    column_step(3)
    diagonal_step(1)
    state = attend(state, 1)
    plane_step(2)
    diagonal_step(2)
    state = attend(state, 2)
    plane_step(3)
    diagonal_step(3)
    peak, total = attend(state, 3)

    lane = lax.broadcasted_iota(jnp.int32, (core_rows, LANES), 1)
    theirs = pl.ds(pl.multiple_of((1 - core) * core_rows, core_rows), core_rows)
    ours = pl.ds(pl.multiple_of(core * core_rows, core_rows), core_rows)
    pick = core == 0
    peak_of = [peak[:core_rows], peak[core_rows:]]
    total_of = [total[:core_rows], total[core_rows:]]
    own_stats[...] = jnp.where(
        lane < LANES // 2,
        jnp.where(pick, peak_of[1], peak_of[0]), jnp.where(pick, total_of[1], total_of[0]),
    )
    send(own_stats, peer_stats, core_recv.at[3], core_peer)
    own_part[...] = numerator[theirs, :].astype(jnp.bfloat16)
    send(own_part, peer_part, core_recv.at[4], core_peer)
    our_peak = jnp.where(pick, peak_of[0], peak_of[1])
    our_total = jnp.where(pick, total_of[0], total_of[1])

    local[3].wait()
    arrived(value_panel.at[1 - core], core_recv.at[2])
    arrived(peer_stats, core_recv.at[3])
    their_peak = peer_stats[:, 0:1]
    their_total = peer_stats[:, LANES // 2:LANES // 2 + 1]
    joint_peak = jnp.maximum(our_peak, their_peak)
    our_weight = jnp.exp(our_peak - joint_peak)
    their_weight = jnp.exp(their_peak - joint_peak)
    joint_total = our_total * our_weight + their_total * their_weight
    our_weight = our_weight / joint_total
    their_weight = their_weight / joint_total
    arrived(peer_part, core_recv.at[4])
    averaged = (
        numerator[ours, :] * our_weight + peer_part[...].astype(jnp.float32) * their_weight
    ).astype(jnp.bfloat16)
    for h in range(heads):
        here = slice(h * tokens, (h + 1) * tokens)
        result = lax.dot_general(
            averaged[here], jnp.concatenate([value_panel[0, h], value_panel[1, h]], axis=1),
            (((1,), (1,)), ((), ())), preferred_element_type=jnp.float32,
        )
        out_ref[:, h * VALUE_WIDTH:(h + 1) * VALUE_WIDTH] = result.astype(jnp.bfloat16)
    for copy in sends:
        copy.wait_send()


def per_device_fused(queries, cache, key_up_weight, value_up_weight, prior_len):
    heads = key_up_weight.shape[0]
    tokens = queries.shape[0]
    slots = cache.shape[0]
    block_rows = slots * cache.shape[1] // LANES
    core_rows = heads * tokens
    hbm = pl.BlockSpec(memory_space=pltpu.HBM)
    dma = pltpu.SemaphoreType.DMA
    vmem = pltpu.VMEM
    return pl.pallas_call(
        fused_kernel,
        out_shape=jax.ShapeDtypeStruct((tokens, heads * VALUE_WIDTH), jnp.bfloat16),
        in_specs=[hbm, hbm, hbm, hbm, pl.BlockSpec(memory_space=pltpu.SMEM)],
        out_specs=pl.BlockSpec(memory_space=pltpu.VMEM),
        scratch_shapes=[
            vmem((2,) + queries.shape, jnp.bfloat16),
            vmem(cache.shape, jnp.bfloat16),
            vmem((4, 4, block_rows, LANES), jnp.bfloat16),
            vmem(key_up_weight.shape, jnp.bfloat16),
            vmem((2,) + value_up_weight.shape, jnp.bfloat16),
            vmem((2, 2 * core_rows, LATENT_WIDTH // 2), jnp.bfloat16),
            vmem((2, 2 * core_rows, LANES), jnp.bfloat16),
            vmem((2 * core_rows, LATENT_WIDTH), jnp.float32),
            vmem((core_rows, LATENT_WIDTH), jnp.bfloat16),
            vmem((core_rows, LATENT_WIDTH), jnp.bfloat16),
            vmem((core_rows, LANES), jnp.float32),
            vmem((core_rows, LANES), jnp.float32),
            dma((4, 3)), dma((4, 2)), dma((32,)), dma((5,)), dma((4,)),
        ],
        compiler_params=pltpu.CompilerParams(
            collective_id=0, has_side_effects=True, vmem_limit_bytes=64 * 1024 * 1024
        ),
    )(queries, cache, key_up_weight, value_up_weight, prior_len)


def solution(mesh):
    in_specs = (
        P("ctx", "head"),
        P(("ctx", "head"), None),
        P("head", None, "ctx"),
        P("head", None, "ctx"),
        P(),
    )
    out_specs = P("ctx", "head")
    chips = Z_CHIPS * Y_CHIPS * X_CHIPS
    body = per_device_fused if mesh.shape["ctx"] == 2 and mesh.shape["head"] == chips else per_device
    return jax.shard_map(
        body, mesh=mesh, in_specs=in_specs, out_specs=out_specs, check_vma=False
    )
```

```python
import jax
import jax.numpy as jnp
from jax import lax
from jax.experimental import pallas as pl
from jax.experimental.pallas import tpu as pltpu
from jax.sharding import PartitionSpec as P

PLAIN_WIDTH = 128
ROTARY_WIDTH = 64
LATENT_WIDTH = 512
VALUE_WIDTH = 128


def per_device(queries, cache, key_up_weight, value_up_weight, prior_len):
    heads_number = key_up_weight.shape[0]
    block_rows = queries.shape[0]
    combined_width = LATENT_WIDTH + ROTARY_WIDTH
    key_panel, value_panel = (
        lax.all_gather(key_up_weight, "ctx", axis=2, tiled=True),
        lax.all_gather(value_up_weight, "ctx", axis=2, tiled=True),
    )
    gathered = lax.all_gather(queries, "ctx", axis=0, tiled=True)
    split_rows = gathered.reshape(gathered.shape[0], heads_number, PLAIN_WIDTH + ROTARY_WIDTH)
    latent = jnp.einsum(
        "thn,hnc->thc",
        split_rows[:, :, :PLAIN_WIDTH],
        key_panel,
        preferred_element_type=jnp.float32,
    ).astype(jnp.bfloat16)
    flat_queries = jnp.concatenate([latent, split_rows[:, :, PLAIN_WIDTH:]], axis=2).reshape(
        -1, combined_width
    )
    flat_rows = flat_queries.shape[0]
    query_number = flat_rows // heads_number
    query_place = prior_len[0] + jnp.arange(flat_rows, dtype=jnp.int32) // heads_number
    group_slots = cache.shape[0] * lax.axis_size("head")
    block_base = lax.axis_index("ctx") * group_slots
    score_scale = (PLAIN_WIDTH + ROTARY_WIDTH) ** (-0.5)
    key_section = lax.all_gather(cache, "head", axis=0, tiled=True)
    row_peak = jnp.full((flat_rows,), -1e30, jnp.float32)
    key_count = key_section.shape[0]
    scores = (
        jnp.einsum("rc,nc->rn", flat_queries, key_section, preferred_element_type=jnp.float32)
        * score_scale
    )
    key_place = block_base + jnp.arange(key_count, dtype=jnp.int32)
    visible = key_place[None, :] <= query_place[:, None]
    scores = jnp.where(visible, scores, jnp.float32(-1e30))
    new_peak = jnp.maximum(row_peak, jnp.max(scores, axis=1))
    probabilities = jnp.where(visible, jnp.exp(scores - new_peak[:, None]), jnp.float32(0.0))
    row_total = jnp.sum(probabilities, axis=1)
    weighted_values = jnp.dot(
        probabilities.astype(jnp.bfloat16),
        key_section[:, :LATENT_WIDTH],
        preferred_element_type=jnp.float32,
    )
    row_peak, row_total, weighted_values = (new_peak, row_total, weighted_values)
    global_peak = lax.pmax(row_peak, "ctx")
    softmax_scale = jnp.exp(row_peak - global_peak)
    scaled_sums = (row_total * softmax_scale).reshape(query_number, heads_number)
    latent_scaled = (weighted_values * softmax_scale[:, None]).reshape(
        query_number, heads_number * LATENT_WIDTH
    )
    block_latent, own_totals = (
        lax.psum_scatter(
            latent_scaled.astype(jnp.bfloat16), "ctx", scatter_dimension=0, tiled=True
        ).astype(jnp.float32),
        lax.psum_scatter(
            scaled_sums.astype(jnp.bfloat16), "ctx", scatter_dimension=0, tiled=True
        ).astype(jnp.float32),
    )
    reshaped_queries = block_latent.reshape(block_rows, heads_number, LATENT_WIDTH)
    projected = jnp.einsum(
        "thc,hvc->thv",
        reshaped_queries,
        value_panel.astype(jnp.float32),
        precision=lax.Precision.HIGHEST,
    )
    result = projected / own_totals[:, :, None]
    return result.reshape(block_rows, heads_number * VALUE_WIDTH).astype(jnp.bfloat16)


MESH = pl.DeviceIdType.MESH
HEAD_WIDTH = PLAIN_WIDTH + ROTARY_WIDTH
Z_CHIPS, Y_CHIPS, X_CHIPS = 4, 2, 2
LANES = 128


def fused_kernel(
    queries_hbm, cache_hbm, key_hbm, value_hbm, prior_ref, out_ref,
    queries_ref, cache_ref, mine, key_half, value_panel, query_latent, query_rotary,
    numerator, own_part, peer_part, own_stats, peer_stats,
    mine_recv, half_recv, send_sem, core_recv, local_sem,
):
    core = lax.axis_index("ctx")
    place = lax.axis_index("head")
    z = place // (Y_CHIPS * X_CHIPS)
    y = (place // X_CHIPS) % Y_CHIPS
    x = place % X_CHIPS
    heads = key_hbm.shape[0]
    tokens = queries_hbm.shape[0]
    slots = cache_hbm.shape[0]
    half_slots = slots // 2
    tiles = LATENT_WIDTH // LANES
    half_rows = mine.shape[2] // 2
    core_rows = heads * tokens
    flat_rows = 2 * core_rows

    def chip(zz, yy, xx):
        return (zz * Y_CHIPS + yy) * X_CHIPS + xx

    middle = z % 3 != 0
    levels = [z, 1 + z % 2, 2 - 2 * (z % 2) + z // 2, 3 - 3 * (z // 2)]
    x_peer = (core, chip(z, y, 1 - x))
    y_peer = (core, chip(z, 1 - y, x))
    core_peer = (1 - core, place)
    pair_peer = (core, chip(z + 1 - 2 * (z % 2), y, x))
    cross_peer = (core, chip(3 - z, y, x))
    partners = [x_peer, y_peer, core_peer, pair_peer]

    barrier = pltpu.get_barrier_semaphore()
    for partner in partners:
        pl.semaphore_signal(barrier, inc=1, device_id=partner, device_id_type=MESH)

    @pl.when(middle)
    def _():
        pl.semaphore_signal(barrier, inc=1, device_id=cross_peer, device_id_type=MESH)

    local = [
        pltpu.make_async_copy(cache_hbm, cache_ref, local_sem.at[0]),
        pltpu.make_async_copy(queries_hbm, queries_ref.at[core], local_sem.at[1]),
        pltpu.make_async_copy(key_hbm, key_half, local_sem.at[2]),
        pltpu.make_async_copy(value_hbm, value_panel.at[core], local_sem.at[3]),
    ]
    for copy in local:
        copy.start()
    local[0].wait()
    for c in range(tiles):
        mine[z, 0, c * slots:(c + 1) * slots, :] = cache_ref[:, c * LANES:(c + 1) * LANES]
    rotary_keys = cache_ref[:, LATENT_WIDTH:]
    mine[z, 0, tiles * slots:, :] = jnp.concatenate(
        [rotary_keys[:half_slots], rotary_keys[half_slots:]], axis=1
    )
    @pl.when(middle)
    def _():
        pl.semaphore_wait(barrier, len(partners) + 1)

    @pl.when(jnp.logical_not(middle))
    def _():
        pl.semaphore_wait(barrier, len(partners))

    sends, middle_sends = [], []

    def send(src, dst, recv, to, only_middle=False):
        copy = pltpu.make_async_remote_copy(
            src_ref=src, dst_ref=dst, recv_sem=recv,
            send_sem=send_sem.at[len(sends) + len(middle_sends)],
            device_id=to, device_id_type=MESH,
        )
        if only_middle:
            pl.when(middle)(copy.start)
            middle_sends.append(copy)
        else:
            copy.start()
            sends.append(copy)

    def arrived(ref, sem):
        pltpu.make_async_copy(ref, ref, sem).wait()

    def rows(k, p, half):
        return mine.at[k, p, pl.ds(half * half_rows, half_rows)]

    def share_column(k):
        block = mine.at[k, 0]
        send(block, mine.at[k, 1], mine_recv.at[k, 1], x_peer)
        send(block, mine.at[k, 2], mine_recv.at[k, 2], y_peer)

    def along_z(k, to, only_middle):
        send(mine.at[k, 0], mine.at[k, 0], mine_recv.at[k, 0], to, only_middle)

    def column_step(i):
        k = levels[i]
        arrived(mine.at[k, 0], mine_recv.at[k, 0])
        along_z(k, cross_peer if i == 2 else pair_peer, True)
        share_column(k)

    def plane_step(i):
        k = levels[i]
        arrived(mine.at[k, 1], mine_recv.at[k, 1])
        send(rows(k, 1, 1), rows(k, 3, 1), half_recv.at[k, 1], y_peer)
        arrived(mine.at[k, 2], mine_recv.at[k, 2])
        send(rows(k, 2, 0), rows(k, 3, 0), half_recv.at[k, 0], x_peer)

    def diagonal_step(i):
        k = levels[i]
        for half in (0, 1):
            arrived(rows(k, 3, half), half_recv.at[k, half])

    def project_queries():
        local[2].wait()
        arrived(queries_ref.at[1 - core], core_recv.at[0])
        zeros = jnp.zeros((2 * tokens, ROTARY_WIDTH), jnp.bfloat16)
        both = jnp.concatenate([queries_ref[0], queries_ref[1]], axis=0)
        for h in range(heads):
            plain = both[:, h * HEAD_WIDTH:h * HEAD_WIDTH + PLAIN_WIDTH]
            rotary = both[:, h * HEAD_WIDTH + PLAIN_WIDTH:(h + 1) * HEAD_WIDTH]
            latent = jnp.dot(
                plain, key_half[h], preferred_element_type=jnp.float32
            ).astype(jnp.bfloat16)
            low = jnp.concatenate([rotary, zeros], axis=1)
            high = jnp.concatenate([zeros, rotary], axis=1)
            for c in (0, 1):
                there = slice(c * core_rows + h * tokens, c * core_rows + (h + 1) * tokens)
                of = slice(c * tokens, (c + 1) * tokens)
                query_latent[core, there, :] = latent[of]
                query_rotary[0, there, :] = low[of]
                query_rotary[1, there, :] = high[of]

    score_scale = HEAD_WIDTH ** (-0.5)
    flat_row = lax.broadcasted_iota(jnp.int32, (flat_rows, 1), 0)
    query_place = prior_ref[0] + flat_row // core_rows * tokens + flat_row % tokens
    group_slots = slots * Z_CHIPS * Y_CHIPS * X_CHIPS

    def attend(state, i):
        k = levels[i]
        bases = []
        for p in range(4):
            source = chip(k, 1 - y if p in (2, 3) else y, 1 - x if p in (1, 3) else x)
            bases.append(core * group_slots + source * slots)
        width = 4 * half_slots

        def latent_of(part):
            return jnp.concatenate(
                [
                    jnp.concatenate(
                        [
                            mine[k, p, pl.ds(c * slots + part * half_slots, half_slots), :]
                            for c in range(tiles)
                        ],
                        axis=1,
                    )
                    for p in range(4)
                ],
                axis=0,
            )

        latents = jnp.concatenate([latent_of(0), latent_of(1)], axis=0)
        rotary = jnp.concatenate(
            [mine[k, p, pl.ds(tiles * slots, half_slots), :] for p in range(4)], axis=0
        )
        column = lax.broadcasted_iota(jnp.int32, (1, 2 * width), 1)
        key_place = column
        for b in range(8):
            inside = (column >= b * half_slots) & (column < (b + 1) * half_slots)
            shift = bases[b % 4] + (b // 4) * half_slots - b * half_slots
            key_place = key_place + jnp.where(inside, shift, 0)
        contract = (((1,), (1,)), ((), ()))
        rotary_scores = [
            lax.dot_general(
                query_rotary[part], rotary, contract, preferred_element_type=jnp.float32
            )
            for part in (0, 1)
        ]
        scores = lax.dot_general(
            jnp.concatenate([query_latent[0], query_latent[1]], axis=1), latents, contract,
            preferred_element_type=jnp.float32,
        )
        scores = (scores + jnp.concatenate(rotary_scores, axis=1)) * score_scale
        visible = key_place <= query_place
        scores = jnp.where(visible, scores, -1e30)
        peak = jnp.max(scores, axis=1, keepdims=True)
        if state is not None:
            peak = jnp.maximum(peak, state[0])
        probs = jnp.where(visible, jnp.exp(scores - peak), 0.0)
        total = jnp.sum(probs, axis=1, keepdims=True)
        weighted = jnp.dot(
            probs.astype(jnp.bfloat16), latents, preferred_element_type=jnp.float32
        )
        if state is None:
            numerator[...] = weighted
        else:
            shrink = jnp.exp(state[0] - peak)
            total = total + state[1] * shrink
            numerator[...] = numerator[...] * shrink + weighted
        return peak, total

    along_z(z, pair_peer, False)
    along_z(z, cross_peer, True)
    share_column(z)
    send(queries_hbm, queries_ref.at[core], core_recv.at[0], core_peer)
    local[1].wait()
    project_queries()
    send(query_latent.at[core], query_latent.at[core], core_recv.at[1], core_peer)
    column_step(1)
    plane_step(0)
    column_step(2)
    send(value_hbm, value_panel.at[core], core_recv.at[2], core_peer)
    diagonal_step(0)
    plane_step(1)
    arrived(query_latent.at[1 - core], core_recv.at[1])
    state = attend(None, 0)
    column_step(3)
    diagonal_step(1)
    state = attend(state, 1)
    plane_step(2)
    diagonal_step(2)
    plane_step(3)
    state = attend(state, 2)
    diagonal_step(3)
    peak, total = attend(state, 3)

    lane = lax.broadcasted_iota(jnp.int32, (core_rows, LANES), 1)
    theirs = pl.ds(pl.multiple_of((1 - core) * core_rows, core_rows), core_rows)
    ours = pl.ds(pl.multiple_of(core * core_rows, core_rows), core_rows)
    pick = core == 0
    peak_of = [peak[:core_rows], peak[core_rows:]]
    total_of = [total[:core_rows], total[core_rows:]]
    own_stats[...] = jnp.where(
        lane < LANES // 2,
        jnp.where(pick, peak_of[1], peak_of[0]), jnp.where(pick, total_of[1], total_of[0]),
    )
    send(own_stats, peer_stats, core_recv.at[3], core_peer)
    own_part[...] = numerator[theirs, :].astype(jnp.bfloat16)
    send(own_part, peer_part, core_recv.at[4], core_peer)
    our_peak = jnp.where(pick, peak_of[0], peak_of[1])
    our_total = jnp.where(pick, total_of[0], total_of[1])

    local[3].wait()
    arrived(value_panel.at[1 - core], core_recv.at[2])
    arrived(peer_stats, core_recv.at[3])
    their_peak = peer_stats[:, 0:1]
    their_total = peer_stats[:, LANES // 2:LANES // 2 + 1]
    joint_peak = jnp.maximum(our_peak, their_peak)
    our_weight = jnp.exp(our_peak - joint_peak)
    their_weight = jnp.exp(their_peak - joint_peak)
    joint_total = our_total * our_weight + their_total * their_weight
    our_weight = our_weight / joint_total
    their_weight = their_weight / joint_total
    arrived(peer_part, core_recv.at[4])
    averaged = (
        numerator[ours, :] * our_weight + peer_part[...].astype(jnp.float32) * their_weight
    ).astype(jnp.bfloat16)
    for h in range(heads):
        here = slice(h * tokens, (h + 1) * tokens)
        result = lax.dot_general(
            averaged[here], jnp.concatenate([value_panel[0, h], value_panel[1, h]], axis=1),
            (((1,), (1,)), ((), ())), preferred_element_type=jnp.float32,
        )
        out_ref[:, h * VALUE_WIDTH:(h + 1) * VALUE_WIDTH] = result.astype(jnp.bfloat16)
    for copy in sends:
        copy.wait_send()

    @pl.when(middle)
    def _():
        for copy in middle_sends:
            copy.wait_send()


def per_device_fused(queries, cache, key_up_weight, value_up_weight, prior_len):
    heads = key_up_weight.shape[0]
    tokens = queries.shape[0]
    slots = cache.shape[0]
    block_rows = slots * cache.shape[1] // LANES
    core_rows = heads * tokens
    hbm = pl.BlockSpec(memory_space=pltpu.HBM)
    dma = pltpu.SemaphoreType.DMA
    vmem = pltpu.VMEM
    return pl.pallas_call(
        fused_kernel,
        out_shape=jax.ShapeDtypeStruct((tokens, heads * VALUE_WIDTH), jnp.bfloat16),
        in_specs=[hbm, hbm, hbm, hbm, pl.BlockSpec(memory_space=pltpu.SMEM)],
        out_specs=pl.BlockSpec(memory_space=pltpu.VMEM),
        scratch_shapes=[
            vmem((2,) + queries.shape, jnp.bfloat16),
            vmem(cache.shape, jnp.bfloat16),
            vmem((4, 4, block_rows, LANES), jnp.bfloat16),
            vmem(key_up_weight.shape, jnp.bfloat16),
            vmem((2,) + value_up_weight.shape, jnp.bfloat16),
            vmem((2, 2 * core_rows, LATENT_WIDTH // 2), jnp.bfloat16),
            vmem((2, 2 * core_rows, LANES), jnp.bfloat16),
            vmem((2 * core_rows, LATENT_WIDTH), jnp.float32),
            vmem((core_rows, LATENT_WIDTH), jnp.bfloat16),
            vmem((core_rows, LATENT_WIDTH), jnp.bfloat16),
            vmem((core_rows, LANES), jnp.float32),
            vmem((core_rows, LANES), jnp.float32),
            dma((4, 3)), dma((4, 2)), dma((32,)), dma((5,)), dma((4,)),
        ],
        compiler_params=pltpu.CompilerParams(
            collective_id=0, has_side_effects=True, vmem_limit_bytes=64 * 1024 * 1024 - 40 * 1024
        ),
    )(queries, cache, key_up_weight, value_up_weight, prior_len)


def solution(mesh):
    in_specs = (
        P("ctx", "head"),
        P(("ctx", "head"), None),
        P("head", None, "ctx"),
        P("head", None, "ctx"),
        P(),
    )
    out_specs = P("ctx", "head")
    chips = Z_CHIPS * Y_CHIPS * X_CHIPS
    body = per_device_fused if mesh.shape["ctx"] == 2 and mesh.shape["head"] == chips else per_device
    return jax.shard_map(
        body, mesh=mesh, in_specs=in_specs, out_specs=out_specs, check_vma=False
    )
```

```python
import jax
import jax.numpy as jnp
from jax import lax
from jax.experimental import pallas as pl
from jax.experimental.pallas import tpu as pltpu
from jax.sharding import PartitionSpec as P

PLAIN_WIDTH = 128
ROTARY_WIDTH = 64
LATENT_WIDTH = 512
VALUE_WIDTH = 128


def per_device(queries, cache, key_up_weight, value_up_weight, prior_len):
    heads_number = key_up_weight.shape[0]
    block_rows = queries.shape[0]
    combined_width = LATENT_WIDTH + ROTARY_WIDTH
    key_panel, value_panel = (
        lax.all_gather(key_up_weight, "ctx", axis=2, tiled=True),
        lax.all_gather(value_up_weight, "ctx", axis=2, tiled=True),
    )
    gathered = lax.all_gather(queries, "ctx", axis=0, tiled=True)
    split_rows = gathered.reshape(gathered.shape[0], heads_number, PLAIN_WIDTH + ROTARY_WIDTH)
    latent = jnp.einsum(
        "thn,hnc->thc",
        split_rows[:, :, :PLAIN_WIDTH],
        key_panel,
        preferred_element_type=jnp.float32,
    ).astype(jnp.bfloat16)
    flat_queries = jnp.concatenate([latent, split_rows[:, :, PLAIN_WIDTH:]], axis=2).reshape(
        -1, combined_width
    )
    flat_rows = flat_queries.shape[0]
    query_number = flat_rows // heads_number
    query_place = prior_len[0] + jnp.arange(flat_rows, dtype=jnp.int32) // heads_number
    group_slots = cache.shape[0] * lax.axis_size("head")
    block_base = lax.axis_index("ctx") * group_slots
    score_scale = (PLAIN_WIDTH + ROTARY_WIDTH) ** (-0.5)
    key_section = lax.all_gather(cache, "head", axis=0, tiled=True)
    row_peak = jnp.full((flat_rows,), -1e30, jnp.float32)
    key_count = key_section.shape[0]
    scores = (
        jnp.einsum("rc,nc->rn", flat_queries, key_section, preferred_element_type=jnp.float32)
        * score_scale
    )
    key_place = block_base + jnp.arange(key_count, dtype=jnp.int32)
    visible = key_place[None, :] <= query_place[:, None]
    scores = jnp.where(visible, scores, jnp.float32(-1e30))
    new_peak = jnp.maximum(row_peak, jnp.max(scores, axis=1))
    probabilities = jnp.where(visible, jnp.exp(scores - new_peak[:, None]), jnp.float32(0.0))
    row_total = jnp.sum(probabilities, axis=1)
    weighted_values = jnp.dot(
        probabilities.astype(jnp.bfloat16),
        key_section[:, :LATENT_WIDTH],
        preferred_element_type=jnp.float32,
    )
    row_peak, row_total, weighted_values = (new_peak, row_total, weighted_values)
    global_peak = lax.pmax(row_peak, "ctx")
    softmax_scale = jnp.exp(row_peak - global_peak)
    scaled_sums = (row_total * softmax_scale).reshape(query_number, heads_number)
    latent_scaled = (weighted_values * softmax_scale[:, None]).reshape(
        query_number, heads_number * LATENT_WIDTH
    )
    block_latent, own_totals = (
        lax.psum_scatter(
            latent_scaled.astype(jnp.bfloat16), "ctx", scatter_dimension=0, tiled=True
        ).astype(jnp.float32),
        lax.psum_scatter(
            scaled_sums.astype(jnp.bfloat16), "ctx", scatter_dimension=0, tiled=True
        ).astype(jnp.float32),
    )
    reshaped_queries = block_latent.reshape(block_rows, heads_number, LATENT_WIDTH)
    projected = jnp.einsum(
        "thc,hvc->thv",
        reshaped_queries,
        value_panel.astype(jnp.float32),
        precision=lax.Precision.HIGHEST,
    )
    result = projected / own_totals[:, :, None]
    return result.reshape(block_rows, heads_number * VALUE_WIDTH).astype(jnp.bfloat16)


MESH = pl.DeviceIdType.MESH
HEAD_WIDTH = PLAIN_WIDTH + ROTARY_WIDTH
Z_CHIPS, Y_CHIPS, X_CHIPS = 4, 2, 2
LANES = 128


def fused_kernel(
    queries_hbm, cache_hbm, key_hbm, value_hbm, prior_ref, out_ref,
    queries_ref, cache_ref, mine, key_half, value_panel, query_latent, query_rotary,
    numerator, own_part, peer_part, own_stats, peer_stats,
    mine_recv, half_recv, whole_recv, send_sem, core_recv, local_sem,
):
    core = lax.axis_index("ctx")
    place = lax.axis_index("head")
    z = place // (Y_CHIPS * X_CHIPS)
    y = (place // X_CHIPS) % Y_CHIPS
    x = place % X_CHIPS
    heads = key_hbm.shape[0]
    tokens = queries_hbm.shape[0]
    slots = cache_hbm.shape[0]
    half_slots = slots // 2
    tiles = LATENT_WIDTH // LANES
    half_rows = mine.shape[2] // 2
    core_rows = heads * tokens
    flat_rows = 2 * core_rows

    def chip(zz, yy, xx):
        return (zz * Y_CHIPS + yy) * X_CHIPS + xx

    middle = z % 3 != 0
    levels = [z, 1 + z % 2, 2 - 2 * (z % 2) + z // 2, 3 - 3 * (z // 2)]
    x_peer = (core, chip(z, y, 1 - x))
    y_peer = (core, chip(z, 1 - y, x))
    core_peer = (1 - core, place)
    pair_peer = (core, chip(z + 1 - 2 * (z % 2), y, x))
    cross_peer = (core, chip(3 - z, y, x))
    partners = [x_peer, y_peer, core_peer, pair_peer]

    barrier = pltpu.get_barrier_semaphore()
    for partner in partners:
        pl.semaphore_signal(barrier, inc=1, device_id=partner, device_id_type=MESH)

    @pl.when(middle)
    def _():
        pl.semaphore_signal(barrier, inc=1, device_id=cross_peer, device_id_type=MESH)

    local = [
        pltpu.make_async_copy(cache_hbm, cache_ref, local_sem.at[0]),
        pltpu.make_async_copy(queries_hbm, queries_ref.at[core], local_sem.at[1]),
        pltpu.make_async_copy(key_hbm, key_half, local_sem.at[2]),
        pltpu.make_async_copy(value_hbm, value_panel.at[core], local_sem.at[3]),
    ]
    for copy in local:
        copy.start()
    local[0].wait()
    for c in range(tiles):
        mine[z, 0, c * slots:(c + 1) * slots, :] = cache_ref[:, c * LANES:(c + 1) * LANES]
    rotary_keys = cache_ref[:, LATENT_WIDTH:]
    mine[z, 0, tiles * slots:, :] = jnp.concatenate(
        [rotary_keys[:half_slots], rotary_keys[half_slots:]], axis=1
    )
    @pl.when(middle)
    def _():
        pl.semaphore_wait(barrier, len(partners) + 1)

    @pl.when(jnp.logical_not(middle))
    def _():
        pl.semaphore_wait(barrier, len(partners))

    sends, middle_sends = [], []

    def send(src, dst, recv, to, only_middle=False):
        copy = pltpu.make_async_remote_copy(
            src_ref=src, dst_ref=dst, recv_sem=recv,
            send_sem=send_sem.at[len(sends) + len(middle_sends)],
            device_id=to, device_id_type=MESH,
        )
        if only_middle:
            pl.when(middle)(copy.start)
            middle_sends.append(copy)
        else:
            copy.start()
            sends.append(copy)

    def arrived(ref, sem):
        pltpu.make_async_copy(ref, ref, sem).wait()

    def rows(k, p, half):
        return mine.at[k, p, pl.ds(half * half_rows, half_rows)]

    def share_column(k):
        block = mine.at[k, 0]
        send(block, mine.at[k, 1], mine_recv.at[k, 1], x_peer)
        send(block, mine.at[k, 2], mine_recv.at[k, 2], y_peer)

    def along_z(k, to, only_middle):
        send(mine.at[k, 0], mine.at[k, 0], mine_recv.at[k, 0], to, only_middle)

    def column_step(i):
        k = levels[i]
        arrived(mine.at[k, 0], mine_recv.at[k, 0])
        along_z(k, cross_peer if i == 2 else pair_peer, True)
        share_column(k)

    def plane_step(i):
        k = levels[i]
        arrived(mine.at[k, 1], mine_recv.at[k, 1])
        if i in (0, 3):
            send(rows(k, 1, 1), rows(k, 3, 1), half_recv.at[k, 1], y_peer)
        arrived(mine.at[k, 2], mine_recv.at[k, 2])
        if i in (0, 3):
            send(rows(k, 2, 0), rows(k, 3, 0), half_recv.at[k, 0], x_peer)

    def diagonal_along_z(k, to, only_middle):
        send(mine.at[k, 3], mine.at[k, 3], whole_recv.at[k], to, only_middle)

    def diagonal_step(i):
        k = levels[i]
        if i in (0, 3):
            for half in (0, 1):
                arrived(rows(k, 3, half), half_recv.at[k, half])
        else:
            arrived(mine.at[k, 3], whole_recv.at[k])
        if i == 0:
            diagonal_along_z(k, pair_peer, False)
            diagonal_along_z(k, cross_peer, True)
        if i == 1:
            diagonal_along_z(k, pair_peer, True)

    def project_queries():
        local[2].wait()
        arrived(queries_ref.at[1 - core], core_recv.at[0])
        zeros = jnp.zeros((2 * tokens, ROTARY_WIDTH), jnp.bfloat16)
        both = jnp.concatenate([queries_ref[0], queries_ref[1]], axis=0)
        for h in range(heads):
            plain = both[:, h * HEAD_WIDTH:h * HEAD_WIDTH + PLAIN_WIDTH]
            rotary = both[:, h * HEAD_WIDTH + PLAIN_WIDTH:(h + 1) * HEAD_WIDTH]
            latent = jnp.dot(
                plain, key_half[h], preferred_element_type=jnp.float32
            ).astype(jnp.bfloat16)
            low = jnp.concatenate([rotary, zeros], axis=1)
            high = jnp.concatenate([zeros, rotary], axis=1)
            for c in (0, 1):
                there = slice(c * core_rows + h * tokens, c * core_rows + (h + 1) * tokens)
                of = slice(c * tokens, (c + 1) * tokens)
                query_latent[core, there, :] = latent[of]
                query_rotary[0, there, :] = low[of]
                query_rotary[1, there, :] = high[of]

    score_scale = HEAD_WIDTH ** (-0.5)
    flat_row = lax.broadcasted_iota(jnp.int32, (flat_rows, 1), 0)
    query_place = prior_ref[0] + flat_row // core_rows * tokens + flat_row % tokens
    group_slots = slots * Z_CHIPS * Y_CHIPS * X_CHIPS

    def attend(state, i):
        k = levels[i]
        bases = []
        for p in range(4):
            source = chip(k, 1 - y if p in (2, 3) else y, 1 - x if p in (1, 3) else x)
            bases.append(core * group_slots + source * slots)
        width = 4 * half_slots

        def latent_of(part):
            return jnp.concatenate(
                [
                    jnp.concatenate(
                        [
                            mine[k, p, pl.ds(c * slots + part * half_slots, half_slots), :]
                            for c in range(tiles)
                        ],
                        axis=1,
                    )
                    for p in range(4)
                ],
                axis=0,
            )

        latents = jnp.concatenate([latent_of(0), latent_of(1)], axis=0)
        rotary = jnp.concatenate(
            [mine[k, p, pl.ds(tiles * slots, half_slots), :] for p in range(4)], axis=0
        )
        column = lax.broadcasted_iota(jnp.int32, (1, 2 * width), 1)
        key_place = column
        for b in range(8):
            inside = (column >= b * half_slots) & (column < (b + 1) * half_slots)
            shift = bases[b % 4] + (b // 4) * half_slots - b * half_slots
            key_place = key_place + jnp.where(inside, shift, 0)
        contract = (((1,), (1,)), ((), ()))
        rotary_scores = [
            lax.dot_general(
                query_rotary[part], rotary, contract, preferred_element_type=jnp.float32
            )
            for part in (0, 1)
        ]
        scores = lax.dot_general(
            jnp.concatenate([query_latent[0], query_latent[1]], axis=1), latents, contract,
            preferred_element_type=jnp.float32,
        )
        scores = (scores + jnp.concatenate(rotary_scores, axis=1)) * score_scale
        visible = key_place <= query_place
        scores = jnp.where(visible, scores, -1e30)
        peak = jnp.max(scores, axis=1, keepdims=True)
        if state is not None:
            peak = jnp.maximum(peak, state[0])
        probs = jnp.where(visible, jnp.exp(scores - peak), 0.0)
        total = jnp.sum(probs, axis=1, keepdims=True)
        weighted = jnp.dot(
            probs.astype(jnp.bfloat16), latents, preferred_element_type=jnp.float32
        )
        if state is None:
            numerator[...] = weighted
        else:
            shrink = jnp.exp(state[0] - peak)
            total = total + state[1] * shrink
            numerator[...] = numerator[...] * shrink + weighted
        return peak, total

    along_z(z, pair_peer, False)
    along_z(z, cross_peer, True)
    share_column(z)
    send(queries_hbm, queries_ref.at[core], core_recv.at[0], core_peer)
    local[1].wait()
    project_queries()
    send(query_latent.at[core], query_latent.at[core], core_recv.at[1], core_peer)
    column_step(1)
    plane_step(0)
    column_step(2)
    send(value_hbm, value_panel.at[core], core_recv.at[2], core_peer)
    diagonal_step(0)
    arrived(query_latent.at[1 - core], core_recv.at[1])
    state = attend(None, 0)
    column_step(3)
    diagonal_step(1)
    plane_step(1)
    state = attend(state, 1)
    plane_step(2)
    plane_step(3)
    diagonal_step(2)
    state = attend(state, 2)
    diagonal_step(3)
    peak, total = attend(state, 3)

    lane = lax.broadcasted_iota(jnp.int32, (core_rows, LANES), 1)
    theirs = pl.ds(pl.multiple_of((1 - core) * core_rows, core_rows), core_rows)
    ours = pl.ds(pl.multiple_of(core * core_rows, core_rows), core_rows)
    pick = core == 0
    peak_of = [peak[:core_rows], peak[core_rows:]]
    total_of = [total[:core_rows], total[core_rows:]]
    own_stats[...] = jnp.where(
        lane < LANES // 2,
        jnp.where(pick, peak_of[1], peak_of[0]), jnp.where(pick, total_of[1], total_of[0]),
    )
    send(own_stats, peer_stats, core_recv.at[3], core_peer)
    own_part[...] = numerator[theirs, :].astype(jnp.bfloat16)
    send(own_part, peer_part, core_recv.at[4], core_peer)
    our_peak = jnp.where(pick, peak_of[0], peak_of[1])
    our_total = jnp.where(pick, total_of[0], total_of[1])

    local[3].wait()
    arrived(value_panel.at[1 - core], core_recv.at[2])
    arrived(peer_stats, core_recv.at[3])
    their_peak = peer_stats[:, 0:1]
    their_total = peer_stats[:, LANES // 2:LANES // 2 + 1]
    joint_peak = jnp.maximum(our_peak, their_peak)
    our_weight = jnp.exp(our_peak - joint_peak)
    their_weight = jnp.exp(their_peak - joint_peak)
    joint_total = our_total * our_weight + their_total * their_weight
    our_weight = our_weight / joint_total
    their_weight = their_weight / joint_total
    arrived(peer_part, core_recv.at[4])
    averaged = (
        numerator[ours, :] * our_weight + peer_part[...].astype(jnp.float32) * their_weight
    ).astype(jnp.bfloat16)
    for h in range(heads):
        here = slice(h * tokens, (h + 1) * tokens)
        result = lax.dot_general(
            averaged[here], jnp.concatenate([value_panel[0, h], value_panel[1, h]], axis=1),
            (((1,), (1,)), ((), ())), preferred_element_type=jnp.float32,
        )
        out_ref[:, h * VALUE_WIDTH:(h + 1) * VALUE_WIDTH] = result
    for copy in sends:
        copy.wait_send()

    @pl.when(middle)
    def _():
        for copy in middle_sends:
            copy.wait_send()


def per_device_fused(queries, cache, key_up_weight, value_up_weight, prior_len):
    heads = key_up_weight.shape[0]
    tokens = queries.shape[0]
    slots = cache.shape[0]
    block_rows = slots * cache.shape[1] // LANES
    core_rows = heads * tokens
    hbm = pl.BlockSpec(memory_space=pltpu.HBM)
    dma = pltpu.SemaphoreType.DMA
    vmem = pltpu.VMEM
    return pl.pallas_call(
        fused_kernel,
        out_shape=jax.ShapeDtypeStruct((tokens, heads * VALUE_WIDTH), jnp.float32),
        in_specs=[hbm, hbm, hbm, hbm, pl.BlockSpec(memory_space=pltpu.SMEM)],
        out_specs=pl.BlockSpec(memory_space=pltpu.VMEM),
        scratch_shapes=[
            vmem((2,) + queries.shape, jnp.bfloat16),
            vmem(cache.shape, jnp.bfloat16),
            vmem((4, 4, block_rows, LANES), jnp.bfloat16),
            vmem(key_up_weight.shape, jnp.bfloat16),
            vmem((2,) + value_up_weight.shape, jnp.bfloat16),
            vmem((2, 2 * core_rows, LATENT_WIDTH // 2), jnp.bfloat16),
            vmem((2, 2 * core_rows, LANES), jnp.bfloat16),
            vmem((2 * core_rows, LATENT_WIDTH), jnp.float32),
            vmem((core_rows, LATENT_WIDTH), jnp.bfloat16),
            vmem((core_rows, LATENT_WIDTH), jnp.bfloat16),
            vmem((core_rows, LANES), jnp.float32),
            vmem((core_rows, LANES), jnp.float32),
            dma((4, 3)), dma((4, 2)), dma((4,)), dma((32,)), dma((5,)), dma((4,)),
        ],
        compiler_params=pltpu.CompilerParams(
            collective_id=0, has_side_effects=True, vmem_limit_bytes=64 * 1024 * 1024 - 40 * 1024
        ),
    )(queries, cache, key_up_weight, value_up_weight, prior_len).astype(jnp.bfloat16)


def solution(mesh):
    in_specs = (
        P("ctx", "head"),
        P(("ctx", "head"), None),
        P("head", None, "ctx"),
        P("head", None, "ctx"),
        P(),
    )
    out_specs = P("ctx", "head")
    chips = Z_CHIPS * Y_CHIPS * X_CHIPS
    body = per_device_fused if mesh.shape["ctx"] == 2 and mesh.shape["head"] == chips else per_device
    return jax.shard_map(
        body, mesh=mesh, in_specs=in_specs, out_specs=out_specs, check_vma=False
    )
```

```python
import jax
import jax.numpy as jnp
from jax import lax
from jax.experimental import pallas as pl
from jax.experimental.pallas import tpu as pltpu
from jax.sharding import PartitionSpec as P

PLAIN_WIDTH = 128
ROTARY_WIDTH = 64
LATENT_WIDTH = 512
VALUE_WIDTH = 128


def per_device(queries, cache, key_up_weight, value_up_weight, prior_len):
    heads_number = key_up_weight.shape[0]
    block_rows = queries.shape[0]
    combined_width = LATENT_WIDTH + ROTARY_WIDTH
    key_panel, value_panel = (
        lax.all_gather(key_up_weight, "ctx", axis=2, tiled=True),
        lax.all_gather(value_up_weight, "ctx", axis=2, tiled=True),
    )
    gathered = lax.all_gather(queries, "ctx", axis=0, tiled=True)
    split_rows = gathered.reshape(gathered.shape[0], heads_number, PLAIN_WIDTH + ROTARY_WIDTH)
    latent = jnp.einsum(
        "thn,hnc->thc",
        split_rows[:, :, :PLAIN_WIDTH],
        key_panel,
        preferred_element_type=jnp.float32,
    ).astype(jnp.bfloat16)
    flat_queries = jnp.concatenate([latent, split_rows[:, :, PLAIN_WIDTH:]], axis=2).reshape(
        -1, combined_width
    )
    flat_rows = flat_queries.shape[0]
    query_number = flat_rows // heads_number
    query_place = prior_len[0] + jnp.arange(flat_rows, dtype=jnp.int32) // heads_number
    group_slots = cache.shape[0] * lax.axis_size("head")
    block_base = lax.axis_index("ctx") * group_slots
    score_scale = (PLAIN_WIDTH + ROTARY_WIDTH) ** (-0.5)
    key_section = lax.all_gather(cache, "head", axis=0, tiled=True)
    row_peak = jnp.full((flat_rows,), -1e30, jnp.float32)
    key_count = key_section.shape[0]
    scores = (
        jnp.einsum("rc,nc->rn", flat_queries, key_section, preferred_element_type=jnp.float32)
        * score_scale
    )
    key_place = block_base + jnp.arange(key_count, dtype=jnp.int32)
    visible = key_place[None, :] <= query_place[:, None]
    scores = jnp.where(visible, scores, jnp.float32(-1e30))
    new_peak = jnp.maximum(row_peak, jnp.max(scores, axis=1))
    probabilities = jnp.where(visible, jnp.exp(scores - new_peak[:, None]), jnp.float32(0.0))
    row_total = jnp.sum(probabilities, axis=1)
    weighted_values = jnp.dot(
        probabilities.astype(jnp.bfloat16),
        key_section[:, :LATENT_WIDTH],
        preferred_element_type=jnp.float32,
    )
    row_peak, row_total, weighted_values = (new_peak, row_total, weighted_values)
    global_peak = lax.pmax(row_peak, "ctx")
    softmax_scale = jnp.exp(row_peak - global_peak)
    scaled_sums = (row_total * softmax_scale).reshape(query_number, heads_number)
    latent_scaled = (weighted_values * softmax_scale[:, None]).reshape(
        query_number, heads_number * LATENT_WIDTH
    )
    block_latent, own_totals = (
        lax.psum_scatter(
            latent_scaled.astype(jnp.bfloat16), "ctx", scatter_dimension=0, tiled=True
        ).astype(jnp.float32),
        lax.psum_scatter(
            scaled_sums.astype(jnp.bfloat16), "ctx", scatter_dimension=0, tiled=True
        ).astype(jnp.float32),
    )
    reshaped_queries = block_latent.reshape(block_rows, heads_number, LATENT_WIDTH)
    projected = jnp.einsum(
        "thc,hvc->thv",
        reshaped_queries,
        value_panel.astype(jnp.float32),
        precision=lax.Precision.HIGHEST,
    )
    result = projected / own_totals[:, :, None]
    return result.reshape(block_rows, heads_number * VALUE_WIDTH).astype(jnp.bfloat16)


MESH = pl.DeviceIdType.MESH
HEAD_WIDTH = PLAIN_WIDTH + ROTARY_WIDTH
Z_CHIPS, Y_CHIPS, X_CHIPS = 4, 2, 2
LANES = 128


def fused_kernel(
    queries_hbm, cache_hbm, key_hbm, value_hbm, prior_ref, out_ref,
    queries_ref, cache_ref, mine, key_half, value_panel, query_latent, query_rotary,
    numerator, own_part, peer_part, own_stats, peer_stats,
    mine_recv, half_recv, whole_recv, send_sem, core_recv, local_sem,
):
    core = lax.axis_index("ctx")
    place = lax.axis_index("head")
    z = place // (Y_CHIPS * X_CHIPS)
    y = (place // X_CHIPS) % Y_CHIPS
    x = place % X_CHIPS
    heads = key_hbm.shape[0]
    tokens = queries_hbm.shape[0]
    slots = cache_hbm.shape[0]
    half_slots = slots // 2
    tiles = LATENT_WIDTH // LANES
    half_rows = mine.shape[2] // 2
    core_rows = heads * tokens
    flat_rows = 2 * core_rows

    def chip(zz, yy, xx):
        return (zz * Y_CHIPS + yy) * X_CHIPS + xx

    middle = z % 3 != 0
    levels = [z, 1 + z % 2, 2 - 2 * (z % 2) + z // 2, 3 - 3 * (z // 2)]
    x_peer = (core, chip(z, y, 1 - x))
    y_peer = (core, chip(z, 1 - y, x))
    core_peer = (1 - core, place)
    pair_peer = (core, chip(z + 1 - 2 * (z % 2), y, x))
    mirror_peer = (core, chip(3 - z, y, x))
    partners = [x_peer, y_peer, core_peer, pair_peer, mirror_peer]

    barrier = pltpu.get_barrier_semaphore()
    for partner in partners:
        pl.semaphore_signal(barrier, inc=1, device_id=partner, device_id_type=MESH)

    local = [
        pltpu.make_async_copy(cache_hbm, cache_ref, local_sem.at[0]),
        pltpu.make_async_copy(queries_hbm, queries_ref.at[core], local_sem.at[1]),
        pltpu.make_async_copy(key_hbm, key_half, local_sem.at[2]),
        pltpu.make_async_copy(value_hbm, value_panel.at[core], local_sem.at[3]),
    ]
    for copy in local:
        copy.start()
    local[0].wait()
    for c in range(tiles):
        mine[z, 0, c * slots:(c + 1) * slots, :] = cache_ref[:, c * LANES:(c + 1) * LANES]
    rotary_keys = cache_ref[:, LATENT_WIDTH:]
    mine[z, 0, tiles * slots:, :] = jnp.concatenate(
        [rotary_keys[:half_slots], rotary_keys[half_slots:]], axis=1
    )
    pl.semaphore_wait(barrier, len(partners))

    sends, middle_sends = [], []

    def send(src, dst, recv, to, only_middle=False):
        copy = pltpu.make_async_remote_copy(
            src_ref=src, dst_ref=dst, recv_sem=recv,
            send_sem=send_sem.at[len(sends) + len(middle_sends)],
            device_id=to, device_id_type=MESH,
        )
        if only_middle:
            pl.when(middle)(copy.start)
            middle_sends.append(copy)
        else:
            copy.start()
            sends.append(copy)
        return copy

    def arrived(ref, sem):
        pltpu.make_async_copy(ref, ref, sem).wait()

    def rows(k, p, half):
        return mine.at[k, p, pl.ds(half * half_rows, half_rows)]

    def share_column(k):
        block = mine.at[k, 0]
        send(block, mine.at[k, 1], mine_recv.at[k, 1], x_peer)
        send(block, mine.at[k, 2], mine_recv.at[k, 2], y_peer)

    def along_z(k, to, only_middle):
        return send(mine.at[k, 0], mine.at[k, 0], mine_recv.at[k, 0], to, only_middle)

    def column_step(i):
        k = levels[i]
        arrived(mine.at[k, 0], mine_recv.at[k, 0])
        if i < 3:
            along_z(k, mirror_peer if i == 2 else pair_peer, True)
        share_column(k)

    def plane_step(i):
        k = levels[i]
        arrived(mine.at[k, 1], mine_recv.at[k, 1])
        if i in (0, 3):
            send(rows(k, 1, 1), rows(k, 3, 1), half_recv.at[k, 1], y_peer)
        arrived(mine.at[k, 2], mine_recv.at[k, 2])
        if i in (0, 3):
            send(rows(k, 2, 0), rows(k, 3, 0), half_recv.at[k, 0], x_peer)

    def diagonal_along_z(k, to, only_middle):
        send(mine.at[k, 3], mine.at[k, 3], whole_recv.at[k], to, only_middle)

    def diagonal_step(i):
        k = levels[i]
        if i in (0, 3):
            for half in (0, 1):
                arrived(rows(k, 3, half), half_recv.at[k, half])
        else:
            arrived(mine.at[k, 3], whole_recv.at[k])
        if i == 0:
            diagonal_along_z(k, pair_peer, False)
            diagonal_along_z(k, mirror_peer, True)
        if i == 1:
            diagonal_along_z(k, pair_peer, True)

    def project_queries():
        local[2].wait()
        arrived(queries_ref.at[1 - core], core_recv.at[0])
        zeros = jnp.zeros((2 * tokens, ROTARY_WIDTH), jnp.bfloat16)
        both = jnp.concatenate([queries_ref[0], queries_ref[1]], axis=0)
        for h in range(heads):
            plain = both[:, h * HEAD_WIDTH:h * HEAD_WIDTH + PLAIN_WIDTH]
            rotary = both[:, h * HEAD_WIDTH + PLAIN_WIDTH:(h + 1) * HEAD_WIDTH]
            latent = jnp.dot(
                plain, key_half[h], preferred_element_type=jnp.float32
            ).astype(jnp.bfloat16)
            low = jnp.concatenate([rotary, zeros], axis=1)
            high = jnp.concatenate([zeros, rotary], axis=1)
            for c in (0, 1):
                there = slice(c * core_rows + h * tokens, c * core_rows + (h + 1) * tokens)
                of = slice(c * tokens, (c + 1) * tokens)
                query_latent[core, there, :] = latent[of]
                query_rotary[0, there, :] = low[of]
                query_rotary[1, there, :] = high[of]

    score_scale = HEAD_WIDTH ** (-0.5)
    flat_row = lax.broadcasted_iota(jnp.int32, (flat_rows, 1), 0)
    query_place = prior_ref[0] + flat_row // core_rows * tokens + flat_row % tokens
    group_slots = slots * Z_CHIPS * Y_CHIPS * X_CHIPS

    def attend(state, blocks):
        blocks = [(levels[i], p) for i, p in blocks]
        bases = []
        for k, p in blocks:
            source = chip(k, 1 - y if p in (2, 3) else y, 1 - x if p in (1, 3) else x)
            bases.append(core * group_slots + source * slots)
        width = 4 * half_slots

        def latent_of(part):
            return jnp.concatenate(
                [
                    jnp.concatenate(
                        [
                            mine[k, p, pl.ds(c * slots + part * half_slots, half_slots), :]
                            for c in range(tiles)
                        ],
                        axis=1,
                    )
                    for k, p in blocks
                ],
                axis=0,
            )

        latents = jnp.concatenate([latent_of(0), latent_of(1)], axis=0)
        rotary = jnp.concatenate(
            [mine[k, p, pl.ds(tiles * slots, half_slots), :] for k, p in blocks], axis=0
        )
        column = lax.broadcasted_iota(jnp.int32, (1, 2 * width), 1)
        key_place = column
        for b in range(8):
            inside = (column >= b * half_slots) & (column < (b + 1) * half_slots)
            shift = bases[b % 4] + (b // 4) * half_slots - b * half_slots
            key_place = key_place + jnp.where(inside, shift, 0)
        contract = (((1,), (1,)), ((), ()))
        rotary_scores = [
            lax.dot_general(
                query_rotary[part], rotary, contract, preferred_element_type=jnp.float32
            )
            for part in (0, 1)
        ]
        scores = lax.dot_general(
            jnp.concatenate([query_latent[0], query_latent[1]], axis=1), latents, contract,
            preferred_element_type=jnp.float32,
        )
        scores = (scores + jnp.concatenate(rotary_scores, axis=1)) * score_scale
        visible = key_place <= query_place
        scores = jnp.where(visible, scores, -1e30)
        peak = jnp.max(scores, axis=1, keepdims=True)
        if state is not None:
            peak = jnp.maximum(peak, state[0])
        probs = jnp.where(visible, jnp.exp(scores - peak), 0.0)
        total = jnp.sum(probs, axis=1, keepdims=True)
        weighted = jnp.dot(
            probs.astype(jnp.bfloat16), latents, preferred_element_type=jnp.float32
        )
        if state is None:
            numerator[...] = weighted
        else:
            shrink = jnp.exp(state[0] - peak)
            total = total + state[1] * shrink
            numerator[...] = numerator[...] * shrink + weighted
        return peak, total

    along_z(z, pair_peer, False)
    own_mirrored = along_z(z, mirror_peer, True)
    share_column(z)
    send(queries_hbm, queries_ref.at[core], core_recv.at[0], core_peer)
    local[1].wait()
    project_queries()
    send(query_latent.at[core], query_latent.at[core], core_recv.at[1], core_peer)
    sends.append(middle_sends.pop(0))
    pl.when(jnp.logical_not(middle))(own_mirrored.start)
    column_step(1)
    plane_step(0)
    column_step(2)
    send(value_hbm, value_panel.at[core], core_recv.at[2], core_peer)
    diagonal_step(0)
    arrived(query_latent.at[1 - core], core_recv.at[1])
    state = attend(None, [(0, p) for p in range(4)])
    column_step(3)
    diagonal_step(1)
    plane_step(1)
    state = attend(state, [(1, p) for p in range(4)])
    plane_step(2)
    plane_step(3)
    state = attend(state, [(2, 0), (2, 1), (2, 2), (3, 0)])
    diagonal_step(2)
    diagonal_step(3)
    peak, total = attend(state, [(2, 3), (3, 1), (3, 2), (3, 3)])

    lane = lax.broadcasted_iota(jnp.int32, (core_rows, LANES), 1)
    theirs = pl.ds(pl.multiple_of((1 - core) * core_rows, core_rows), core_rows)
    ours = pl.ds(pl.multiple_of(core * core_rows, core_rows), core_rows)
    pick = core == 0
    peak_of = [peak[:core_rows], peak[core_rows:]]
    total_of = [total[:core_rows], total[core_rows:]]
    own_stats[...] = jnp.where(
        lane < LANES // 2,
        jnp.where(pick, peak_of[1], peak_of[0]), jnp.where(pick, total_of[1], total_of[0]),
    )
    send(own_stats, peer_stats, core_recv.at[3], core_peer)
    own_part[...] = numerator[theirs, :].astype(jnp.bfloat16)
    send(own_part, peer_part, core_recv.at[4], core_peer)
    our_peak = jnp.where(pick, peak_of[0], peak_of[1])
    our_total = jnp.where(pick, total_of[0], total_of[1])

    local[3].wait()
    arrived(value_panel.at[1 - core], core_recv.at[2])
    arrived(peer_stats, core_recv.at[3])
    their_peak = peer_stats[:, 0:1]
    their_total = peer_stats[:, LANES // 2:LANES // 2 + 1]
    joint_peak = jnp.maximum(our_peak, their_peak)
    our_weight = jnp.exp(our_peak - joint_peak)
    their_weight = jnp.exp(their_peak - joint_peak)
    joint_total = our_total * our_weight + their_total * their_weight
    our_weight = our_weight / joint_total
    their_weight = their_weight / joint_total
    arrived(peer_part, core_recv.at[4])
    averaged = (
        numerator[ours, :] * our_weight + peer_part[...].astype(jnp.float32) * their_weight
    ).astype(jnp.bfloat16)
    for h in range(heads):
        here = slice(h * tokens, (h + 1) * tokens)
        result = lax.dot_general(
            averaged[here], jnp.concatenate([value_panel[0, h], value_panel[1, h]], axis=1),
            (((1,), (1,)), ((), ())), preferred_element_type=jnp.float32,
        )
        out_ref[:, h * VALUE_WIDTH:(h + 1) * VALUE_WIDTH] = result.astype(jnp.bfloat16)
    for copy in sends:
        copy.wait_send()

    @pl.when(middle)
    def _():
        for copy in middle_sends:
            copy.wait_send()


def per_device_fused(queries, cache, key_up_weight, value_up_weight, prior_len):
    heads = key_up_weight.shape[0]
    tokens = queries.shape[0]
    slots = cache.shape[0]
    block_rows = slots * cache.shape[1] // LANES
    core_rows = heads * tokens
    hbm = pl.BlockSpec(memory_space=pltpu.HBM)
    dma = pltpu.SemaphoreType.DMA
    vmem = pltpu.VMEM
    return pl.pallas_call(
        fused_kernel,
        out_shape=jax.ShapeDtypeStruct((tokens, heads * VALUE_WIDTH), jnp.bfloat16),
        in_specs=[hbm, hbm, hbm, hbm, pl.BlockSpec(memory_space=pltpu.SMEM)],
        out_specs=pl.BlockSpec(memory_space=pltpu.VMEM),
        scratch_shapes=[
            vmem((2,) + queries.shape, jnp.bfloat16),
            vmem(cache.shape, jnp.bfloat16),
            vmem((4, 4, block_rows, LANES), jnp.bfloat16),
            vmem(key_up_weight.shape, jnp.bfloat16),
            vmem((2,) + value_up_weight.shape, jnp.bfloat16),
            vmem((2, 2 * core_rows, LATENT_WIDTH // 2), jnp.bfloat16),
            vmem((2, 2 * core_rows, LANES), jnp.bfloat16),
            vmem((2 * core_rows, LATENT_WIDTH), jnp.float32),
            vmem((core_rows, LATENT_WIDTH), jnp.bfloat16),
            vmem((core_rows, LATENT_WIDTH), jnp.bfloat16),
            vmem((core_rows, LANES), jnp.float32),
            vmem((core_rows, LANES), jnp.float32),
            dma((4, 3)), dma((4, 2)), dma((4,)), dma((32,)), dma((5,)), dma((4,)),
        ],
        compiler_params=pltpu.CompilerParams(
            collective_id=0, has_side_effects=True, vmem_limit_bytes=64 * 1024 * 1024 - 40 * 1024
        ),
    )(queries, cache, key_up_weight, value_up_weight, prior_len)


def solution(mesh):
    in_specs = (
        P("ctx", "head"),
        P(("ctx", "head"), None),
        P("head", None, "ctx"),
        P("head", None, "ctx"),
        P(),
    )
    out_specs = P("ctx", "head")
    chips = Z_CHIPS * Y_CHIPS * X_CHIPS
    body = per_device_fused if mesh.shape["ctx"] == 2 and mesh.shape["head"] == chips else per_device
    return jax.shard_map(
        body, mesh=mesh, in_specs=in_specs, out_specs=out_specs, check_vma=False
    )
```

```python
import jax
import jax.numpy as jnp
from jax import lax
from jax.experimental import pallas as pl
from jax.experimental.pallas import tpu as pltpu
from jax.sharding import PartitionSpec as P

PLAIN_WIDTH = 128
ROTARY_WIDTH = 64
LATENT_WIDTH = 512
VALUE_WIDTH = 128


def per_device(queries, cache, key_up_weight, value_up_weight, prior_len):
    heads_number = key_up_weight.shape[0]
    block_rows = queries.shape[0]
    combined_width = LATENT_WIDTH + ROTARY_WIDTH
    key_panel, value_panel = (
        lax.all_gather(key_up_weight, "ctx", axis=2, tiled=True),
        lax.all_gather(value_up_weight, "ctx", axis=2, tiled=True),
    )
    gathered = lax.all_gather(queries, "ctx", axis=0, tiled=True)
    split_rows = gathered.reshape(gathered.shape[0], heads_number, PLAIN_WIDTH + ROTARY_WIDTH)
    latent = jnp.einsum(
        "thn,hnc->thc",
        split_rows[:, :, :PLAIN_WIDTH],
        key_panel,
        preferred_element_type=jnp.float32,
    ).astype(jnp.bfloat16)
    flat_queries = jnp.concatenate([latent, split_rows[:, :, PLAIN_WIDTH:]], axis=2).reshape(
        -1, combined_width
    )
    flat_rows = flat_queries.shape[0]
    query_number = flat_rows // heads_number
    query_place = prior_len[0] + jnp.arange(flat_rows, dtype=jnp.int32) // heads_number
    group_slots = cache.shape[0] * lax.axis_size("head")
    block_base = lax.axis_index("ctx") * group_slots
    score_scale = (PLAIN_WIDTH + ROTARY_WIDTH) ** (-0.5)
    key_section = lax.all_gather(cache, "head", axis=0, tiled=True)
    row_peak = jnp.full((flat_rows,), -1e30, jnp.float32)
    key_count = key_section.shape[0]
    scores = (
        jnp.einsum("rc,nc->rn", flat_queries, key_section, preferred_element_type=jnp.float32)
        * score_scale
    )
    key_place = block_base + jnp.arange(key_count, dtype=jnp.int32)
    visible = key_place[None, :] <= query_place[:, None]
    scores = jnp.where(visible, scores, jnp.float32(-1e30))
    new_peak = jnp.maximum(row_peak, jnp.max(scores, axis=1))
    probabilities = jnp.where(visible, jnp.exp(scores - new_peak[:, None]), jnp.float32(0.0))
    row_total = jnp.sum(probabilities, axis=1)
    weighted_values = jnp.dot(
        probabilities.astype(jnp.bfloat16),
        key_section[:, :LATENT_WIDTH],
        preferred_element_type=jnp.float32,
    )
    row_peak, row_total, weighted_values = (new_peak, row_total, weighted_values)
    global_peak = lax.pmax(row_peak, "ctx")
    softmax_scale = jnp.exp(row_peak - global_peak)
    scaled_sums = (row_total * softmax_scale).reshape(query_number, heads_number)
    latent_scaled = (weighted_values * softmax_scale[:, None]).reshape(
        query_number, heads_number * LATENT_WIDTH
    )
    block_latent, own_totals = (
        lax.psum_scatter(
            latent_scaled.astype(jnp.bfloat16), "ctx", scatter_dimension=0, tiled=True
        ).astype(jnp.float32),
        lax.psum_scatter(
            scaled_sums.astype(jnp.bfloat16), "ctx", scatter_dimension=0, tiled=True
        ).astype(jnp.float32),
    )
    reshaped_queries = block_latent.reshape(block_rows, heads_number, LATENT_WIDTH)
    projected = jnp.einsum(
        "thc,hvc->thv",
        reshaped_queries,
        value_panel.astype(jnp.float32),
        precision=lax.Precision.HIGHEST,
    )
    result = projected / own_totals[:, :, None]
    return result.reshape(block_rows, heads_number * VALUE_WIDTH).astype(jnp.bfloat16)


MESH = pl.DeviceIdType.MESH
HEAD_WIDTH = PLAIN_WIDTH + ROTARY_WIDTH
Z_CHIPS, Y_CHIPS, X_CHIPS = 4, 2, 2
LANES = 128


def fused_kernel(
    queries_hbm, cache_hbm, key_hbm, value_hbm, prior_ref, out_ref,
    queries_ref, cache_ref, mine, key_half, value_panel, query_latent, query_rotary,
    numerator, own_part, peer_part, own_stats, peer_stats,
    mine_recv, half_recv, whole_recv, send_sem, core_recv, local_sem,
):
    core = lax.axis_index("ctx")
    place = lax.axis_index("head")
    z = place // (Y_CHIPS * X_CHIPS)
    y = (place // X_CHIPS) % Y_CHIPS
    x = place % X_CHIPS
    heads = key_hbm.shape[0]
    tokens = queries_hbm.shape[0]
    slots = cache_hbm.shape[0]
    half_slots = slots // 2
    tiles = LATENT_WIDTH // LANES
    half_rows = mine.shape[2] // 2
    core_rows = heads * tokens
    flat_rows = 2 * core_rows

    def chip(zz, yy, xx):
        return (zz * Y_CHIPS + yy) * X_CHIPS + xx

    middle = z % 3 != 0
    levels = [z, 1 + z % 2, 2 - 2 * (z % 2) + z // 2, 3 - 3 * (z // 2)]
    x_peer = (core, chip(z, y, 1 - x))
    y_peer = (core, chip(z, 1 - y, x))
    core_peer = (1 - core, place)
    pair_peer = (core, chip(z + 1 - 2 * (z % 2), y, x))
    mirror_peer = (core, chip(3 - z, y, x))
    partners = [x_peer, y_peer, core_peer, pair_peer, mirror_peer]

    barrier = pltpu.get_barrier_semaphore()
    for partner in partners:
        pl.semaphore_signal(barrier, inc=1, device_id=partner, device_id_type=MESH)

    local = [
        pltpu.make_async_copy(cache_hbm, cache_ref, local_sem.at[0]),
        pltpu.make_async_copy(queries_hbm, queries_ref.at[core], local_sem.at[1]),
        pltpu.make_async_copy(key_hbm, key_half, local_sem.at[2]),
        pltpu.make_async_copy(value_hbm, value_panel.at[core], local_sem.at[3]),
    ]
    for copy in local:
        copy.start()
    local[0].wait()
    for c in range(tiles):
        mine[z, 0, c * slots:(c + 1) * slots, :] = cache_ref[:, c * LANES:(c + 1) * LANES]
    rotary_keys = cache_ref[:, LATENT_WIDTH:]
    mine[z, 0, tiles * slots:, :] = jnp.concatenate(
        [rotary_keys[:half_slots], rotary_keys[half_slots:]], axis=1
    )
    pl.semaphore_wait(barrier, len(partners))

    sends, middle_sends = [], []

    def send(src, dst, recv, to, only_middle=False):
        copy = pltpu.make_async_remote_copy(
            src_ref=src, dst_ref=dst, recv_sem=recv,
            send_sem=send_sem.at[len(sends) + len(middle_sends)],
            device_id=to, device_id_type=MESH,
        )
        if only_middle:
            pl.when(middle)(copy.start)
            middle_sends.append(copy)
        else:
            copy.start()
            sends.append(copy)
        return copy

    def arrived(ref, sem):
        pltpu.make_async_copy(ref, ref, sem).wait()

    def rows(k, p, half):
        return mine.at[k, p, pl.ds(half * half_rows, half_rows)]

    def share_column(k):
        block = mine.at[k, 0]
        send(block, mine.at[k, 1], mine_recv.at[k, 1], x_peer)
        send(block, mine.at[k, 2], mine_recv.at[k, 2], y_peer)

    def along_z(k, to, only_middle):
        return send(mine.at[k, 0], mine.at[k, 0], mine_recv.at[k, 0], to, only_middle)

    def column_step(i):
        k = levels[i]
        arrived(mine.at[k, 0], mine_recv.at[k, 0])
        if i < 3:
            along_z(k, mirror_peer if i == 2 else pair_peer, True)
        share_column(k)

    def plane_step(i):
        k = levels[i]
        arrived(mine.at[k, 1], mine_recv.at[k, 1])
        if i in (0, 3):
            send(rows(k, 1, 1), rows(k, 3, 1), half_recv.at[k, 1], y_peer)
        arrived(mine.at[k, 2], mine_recv.at[k, 2])
        if i in (0, 3):
            send(rows(k, 2, 0), rows(k, 3, 0), half_recv.at[k, 0], x_peer)

    def diagonal_along_z(k, to, only_middle):
        send(mine.at[k, 3], mine.at[k, 3], whole_recv.at[k], to, only_middle)

    def diagonal_step(i):
        k = levels[i]
        if i in (0, 3):
            for half in (0, 1):
                arrived(rows(k, 3, half), half_recv.at[k, half])
        else:
            arrived(mine.at[k, 3], whole_recv.at[k])
        if i == 0:
            diagonal_along_z(k, pair_peer, False)
            diagonal_along_z(k, mirror_peer, True)
        if i == 1:
            diagonal_along_z(k, pair_peer, True)

    def project_queries(first, last):
        zeros = jnp.zeros((2 * tokens, ROTARY_WIDTH), jnp.bfloat16)
        both = jnp.concatenate([queries_ref[0], queries_ref[1]], axis=0)
        for h in range(first, last):
            plain = both[:, h * HEAD_WIDTH:h * HEAD_WIDTH + PLAIN_WIDTH]
            rotary = both[:, h * HEAD_WIDTH + PLAIN_WIDTH:(h + 1) * HEAD_WIDTH]
            latent = jnp.dot(
                plain, key_half[h], preferred_element_type=jnp.float32
            ).astype(jnp.bfloat16)
            low = jnp.concatenate([rotary, zeros], axis=1)
            high = jnp.concatenate([zeros, rotary], axis=1)
            for c in (0, 1):
                there = slice(c * core_rows + h * tokens, c * core_rows + (h + 1) * tokens)
                of = slice(c * tokens, (c + 1) * tokens)
                query_latent[core, there, :] = latent[of]
                query_rotary[0, there, :] = low[of]
                query_rotary[1, there, :] = high[of]

    score_scale = HEAD_WIDTH ** (-0.5)
    group_slots = slots * Z_CHIPS * Y_CHIPS * X_CHIPS

    def attend(state, blocks, part_of=None):
        if part_of is None:
            here = pl.ds(0, flat_rows)
            flat_row = lax.broadcasted_iota(jnp.int32, (flat_rows, 1), 0)
            query_place = prior_ref[0] + flat_row // core_rows * tokens + flat_row % tokens
        else:
            here = pl.ds(pl.multiple_of(part_of * core_rows, core_rows), core_rows)
            flat_row = lax.broadcasted_iota(jnp.int32, (core_rows, 1), 0)
            query_place = prior_ref[0] + part_of * tokens + flat_row % tokens
        blocks = [(levels[i], p) for i, p in blocks]
        bases = []
        for k, p in blocks:
            source = chip(k, 1 - y if p in (2, 3) else y, 1 - x if p in (1, 3) else x)
            bases.append(core * group_slots + source * slots)
        width = 4 * half_slots

        def latent_of(part):
            return jnp.concatenate(
                [
                    jnp.concatenate(
                        [
                            mine[k, p, pl.ds(c * slots + part * half_slots, half_slots), :]
                            for c in range(tiles)
                        ],
                        axis=1,
                    )
                    for k, p in blocks
                ],
                axis=0,
            )

        latents = jnp.concatenate([latent_of(0), latent_of(1)], axis=0)
        rotary = jnp.concatenate(
            [mine[k, p, pl.ds(tiles * slots, half_slots), :] for k, p in blocks], axis=0
        )
        column = lax.broadcasted_iota(jnp.int32, (1, 2 * width), 1)
        key_place = column
        for b in range(8):
            inside = (column >= b * half_slots) & (column < (b + 1) * half_slots)
            shift = bases[b % 4] + (b // 4) * half_slots - b * half_slots
            key_place = key_place + jnp.where(inside, shift, 0)
        contract = (((1,), (1,)), ((), ()))
        rotary_scores = [
            lax.dot_general(
                query_rotary[part, here, :], rotary, contract, preferred_element_type=jnp.float32
            )
            for part in (0, 1)
        ]
        scores = lax.dot_general(
            jnp.concatenate([query_latent[0, here, :], query_latent[1, here, :]], axis=1), latents, contract,
            preferred_element_type=jnp.float32,
        )
        scores = (scores + jnp.concatenate(rotary_scores, axis=1)) * score_scale
        visible = key_place <= query_place
        scores = jnp.where(visible, scores, -1e30)
        peak = jnp.max(scores, axis=1, keepdims=True)
        if state is not None:
            peak = jnp.maximum(peak, state[0])
        probs = jnp.where(visible, jnp.exp(scores - peak), 0.0)
        total = jnp.sum(probs, axis=1, keepdims=True)
        weighted = jnp.dot(
            probs.astype(jnp.bfloat16), latents, preferred_element_type=jnp.float32
        )
        if state is None:
            numerator[here, :] = weighted
        else:
            shrink = jnp.exp(state[0] - peak)
            total = total + state[1] * shrink
            numerator[here, :] = numerator[here, :] * shrink + weighted
        return peak, total

    along_z(z, pair_peer, False)
    own_mirrored = along_z(z, mirror_peer, True)
    share_column(z)
    send(queries_hbm, queries_ref.at[core], core_recv.at[0], core_peer)
    local[1].wait()
    local[2].wait()
    arrived(queries_ref.at[1 - core], core_recv.at[0])
    project_queries(0, heads // 2)
    sends.append(middle_sends.pop(0))
    pl.when(jnp.logical_not(middle))(own_mirrored.start)
    column_step(1)
    plane_step(0)
    project_queries(heads // 2, heads)
    send(query_latent.at[core], query_latent.at[core], core_recv.at[1], core_peer)
    column_step(2)
    send(value_hbm, value_panel.at[core], core_recv.at[2], core_peer)
    diagonal_step(0)
    arrived(query_latent.at[1 - core], core_recv.at[1])
    state = attend(None, [(0, p) for p in range(4)])
    column_step(3)
    diagonal_step(1)
    plane_step(1)
    state = attend(state, [(1, p) for p in range(4)])
    plane_step(2)
    plane_step(3)
    state = attend(state, [(2, 0), (2, 1), (2, 2), (3, 0)])
    diagonal_step(2)
    diagonal_step(3)
    pick = core == 0
    low = [value[:core_rows] for value in state]
    high = [value[core_rows:] for value in state]
    last = [(2, 3), (3, 1), (3, 2), (3, 3)]
    their_state = [jnp.where(pick, b, a) for a, b in zip(low, high)]
    our_state = [jnp.where(pick, a, b) for a, b in zip(low, high)]
    peak, total = attend(their_state, last, 1 - core)
    lane = lax.broadcasted_iota(jnp.int32, (core_rows, LANES), 1)
    own_stats[...] = jnp.where(lane < LANES // 2, peak, total)
    theirs = pl.ds(pl.multiple_of((1 - core) * core_rows, core_rows), core_rows)
    ours = pl.ds(pl.multiple_of(core * core_rows, core_rows), core_rows)
    own_part[...] = numerator[theirs, :].astype(jnp.bfloat16)
    send(own_part, peer_part, core_recv.at[4], core_peer)
    send(own_stats, peer_stats, core_recv.at[3], core_peer)
    our_peak, our_total = attend(our_state, last, core)

    local[3].wait()
    arrived(value_panel.at[1 - core], core_recv.at[2])
    arrived(peer_stats, core_recv.at[3])
    their_peak = peer_stats[:, 0:1]
    their_total = peer_stats[:, LANES // 2:LANES // 2 + 1]
    joint_peak = jnp.maximum(our_peak, their_peak)
    our_weight = jnp.exp(our_peak - joint_peak)
    their_weight = jnp.exp(their_peak - joint_peak)
    joint_total = our_total * our_weight + their_total * their_weight
    our_weight = our_weight / joint_total
    their_weight = their_weight / joint_total
    arrived(peer_part, core_recv.at[4])
    averaged = (
        numerator[ours, :] * our_weight + peer_part[...].astype(jnp.float32) * their_weight
    ).astype(jnp.bfloat16)
    for h in range(heads):
        here = slice(h * tokens, (h + 1) * tokens)
        result = lax.dot_general(
            averaged[here], jnp.concatenate([value_panel[0, h], value_panel[1, h]], axis=1),
            (((1,), (1,)), ((), ())), preferred_element_type=jnp.float32,
        )
        out_ref[:, h * VALUE_WIDTH:(h + 1) * VALUE_WIDTH] = result.astype(jnp.bfloat16)
    for copy in sends:
        copy.wait_send()

    @pl.when(middle)
    def _():
        for copy in middle_sends:
            copy.wait_send()


def per_device_fused(queries, cache, key_up_weight, value_up_weight, prior_len):
    heads = key_up_weight.shape[0]
    tokens = queries.shape[0]
    slots = cache.shape[0]
    block_rows = slots * cache.shape[1] // LANES
    core_rows = heads * tokens
    hbm = pl.BlockSpec(memory_space=pltpu.HBM)
    dma = pltpu.SemaphoreType.DMA
    vmem = pltpu.VMEM
    return pl.pallas_call(
        fused_kernel,
        out_shape=jax.ShapeDtypeStruct((tokens, heads * VALUE_WIDTH), jnp.bfloat16),
        in_specs=[hbm, hbm, hbm, hbm, pl.BlockSpec(memory_space=pltpu.SMEM)],
        out_specs=pl.BlockSpec(memory_space=pltpu.VMEM),
        scratch_shapes=[
            vmem((2,) + queries.shape, jnp.bfloat16),
            vmem(cache.shape, jnp.bfloat16),
            vmem((4, 4, block_rows, LANES), jnp.bfloat16),
            vmem(key_up_weight.shape, jnp.bfloat16),
            vmem((2,) + value_up_weight.shape, jnp.bfloat16),
            vmem((2, 2 * core_rows, LATENT_WIDTH // 2), jnp.bfloat16),
            vmem((2, 2 * core_rows, LANES), jnp.bfloat16),
            vmem((2 * core_rows, LATENT_WIDTH), jnp.float32),
            vmem((core_rows, LATENT_WIDTH), jnp.bfloat16),
            vmem((core_rows, LATENT_WIDTH), jnp.bfloat16),
            vmem((core_rows, LANES), jnp.float32),
            vmem((core_rows, LANES), jnp.float32),
            dma((4, 3)), dma((4, 2)), dma((4,)), dma((32,)), dma((5,)), dma((4,)),
        ],
        compiler_params=pltpu.CompilerParams(
            collective_id=0, has_side_effects=True, vmem_limit_bytes=(64 * 1024 - 10375) * 1024
        ),
    )(queries, cache, key_up_weight, value_up_weight, prior_len)


def solution(mesh):
    in_specs = (
        P("ctx", "head"),
        P(("ctx", "head"), None),
        P("head", None, "ctx"),
        P("head", None, "ctx"),
        P(),
    )
    out_specs = P("ctx", "head")
    chips = Z_CHIPS * Y_CHIPS * X_CHIPS
    body = per_device_fused if mesh.shape["ctx"] == 2 and mesh.shape["head"] == chips else per_device
    return jax.shard_map(
        body, mesh=mesh, in_specs=in_specs, out_specs=out_specs, check_vma=False
    )
```

```python
import jax
import jax.numpy as jnp
from jax import lax
from jax.experimental import pallas as pl
from jax.experimental.pallas import tpu as pltpu
from jax.sharding import PartitionSpec as P

PLAIN_WIDTH = 128
ROTARY_WIDTH = 64
LATENT_WIDTH = 512
VALUE_WIDTH = 128


def per_device(queries, cache, key_up_weight, value_up_weight, prior_len):
    heads_number = key_up_weight.shape[0]
    block_rows = queries.shape[0]
    combined_width = LATENT_WIDTH + ROTARY_WIDTH
    key_panel, value_panel = (
        lax.all_gather(key_up_weight, "ctx", axis=2, tiled=True),
        lax.all_gather(value_up_weight, "ctx", axis=2, tiled=True),
    )
    gathered = lax.all_gather(queries, "ctx", axis=0, tiled=True)
    split_rows = gathered.reshape(gathered.shape[0], heads_number, PLAIN_WIDTH + ROTARY_WIDTH)
    latent = jnp.einsum(
        "thn,hnc->thc",
        split_rows[:, :, :PLAIN_WIDTH],
        key_panel,
        preferred_element_type=jnp.float32,
    ).astype(jnp.bfloat16)
    flat_queries = jnp.concatenate([latent, split_rows[:, :, PLAIN_WIDTH:]], axis=2).reshape(
        -1, combined_width
    )
    flat_rows = flat_queries.shape[0]
    query_number = flat_rows // heads_number
    query_place = prior_len[0] + jnp.arange(flat_rows, dtype=jnp.int32) // heads_number
    group_slots = cache.shape[0] * lax.axis_size("head")
    block_base = lax.axis_index("ctx") * group_slots
    score_scale = (PLAIN_WIDTH + ROTARY_WIDTH) ** (-0.5)
    key_section = lax.all_gather(cache, "head", axis=0, tiled=True)
    row_peak = jnp.full((flat_rows,), -1e30, jnp.float32)
    key_count = key_section.shape[0]
    scores = (
        jnp.einsum("rc,nc->rn", flat_queries, key_section, preferred_element_type=jnp.float32)
        * score_scale
    )
    key_place = block_base + jnp.arange(key_count, dtype=jnp.int32)
    visible = key_place[None, :] <= query_place[:, None]
    scores = jnp.where(visible, scores, jnp.float32(-1e30))
    new_peak = jnp.maximum(row_peak, jnp.max(scores, axis=1))
    probabilities = jnp.where(visible, jnp.exp(scores - new_peak[:, None]), jnp.float32(0.0))
    row_total = jnp.sum(probabilities, axis=1)
    weighted_values = jnp.dot(
        probabilities.astype(jnp.bfloat16),
        key_section[:, :LATENT_WIDTH],
        preferred_element_type=jnp.float32,
    )
    row_peak, row_total, weighted_values = (new_peak, row_total, weighted_values)
    global_peak = lax.pmax(row_peak, "ctx")
    softmax_scale = jnp.exp(row_peak - global_peak)
    scaled_sums = (row_total * softmax_scale).reshape(query_number, heads_number)
    latent_scaled = (weighted_values * softmax_scale[:, None]).reshape(
        query_number, heads_number * LATENT_WIDTH
    )
    block_latent, own_totals = (
        lax.psum_scatter(
            latent_scaled.astype(jnp.bfloat16), "ctx", scatter_dimension=0, tiled=True
        ).astype(jnp.float32),
        lax.psum_scatter(
            scaled_sums.astype(jnp.bfloat16), "ctx", scatter_dimension=0, tiled=True
        ).astype(jnp.float32),
    )
    reshaped_queries = block_latent.reshape(block_rows, heads_number, LATENT_WIDTH)
    projected = jnp.einsum(
        "thc,hvc->thv",
        reshaped_queries,
        value_panel.astype(jnp.float32),
        precision=lax.Precision.HIGHEST,
    )
    result = projected / own_totals[:, :, None]
    return result.reshape(block_rows, heads_number * VALUE_WIDTH).astype(jnp.bfloat16)


MESH = pl.DeviceIdType.MESH
HEAD_WIDTH = PLAIN_WIDTH + ROTARY_WIDTH
Z_CHIPS, Y_CHIPS, X_CHIPS = 4, 2, 2
LANES = 128


def fused_kernel(
    queries_hbm, cache_hbm, key_hbm, value_hbm, prior_ref, out_ref,
    queries_ref, cache_ref, mine, key_half, value_panel, query_latent, query_rotary,
    numerator, own_part, peer_part, own_stats, peer_stats,
    mine_recv, rest_recv, half_recv, whole_recv, send_sem, core_recv, local_sem,
):
    core = lax.axis_index("ctx")
    place = lax.axis_index("head")
    z = place // (Y_CHIPS * X_CHIPS)
    y = (place // X_CHIPS) % Y_CHIPS
    x = place % X_CHIPS
    heads = key_hbm.shape[0]
    tokens = queries_hbm.shape[0]
    slots = cache_hbm.shape[0]
    half_slots = slots // 2
    tiles = LATENT_WIDTH // LANES
    half_rows = mine.shape[2] // 2
    core_rows = heads * tokens
    flat_rows = 2 * core_rows

    def chip(zz, yy, xx):
        return (zz * Y_CHIPS + yy) * X_CHIPS + xx

    middle = z % 3 != 0
    levels = [z, 1 + z % 2, 2 - 2 * (z % 2) + z // 2, 3 - 3 * (z // 2)]
    x_peer = (core, chip(z, y, 1 - x))
    y_peer = (core, chip(z, 1 - y, x))
    core_peer = (1 - core, place)
    pair_peer = (core, chip(z + 1 - 2 * (z % 2), y, x))
    mirror_peer = (core, chip(3 - z, y, x))
    partners = [x_peer, y_peer, core_peer, pair_peer, mirror_peer]

    barrier = pltpu.get_barrier_semaphore()
    for partner in partners:
        pl.semaphore_signal(barrier, inc=1, device_id=partner, device_id_type=MESH)

    local = [
        pltpu.make_async_copy(cache_hbm, cache_ref, local_sem.at[0]),
        pltpu.make_async_copy(queries_hbm, queries_ref.at[core], local_sem.at[1]),
        pltpu.make_async_copy(key_hbm, key_half, local_sem.at[2]),
        pltpu.make_async_copy(value_hbm, value_panel.at[core], local_sem.at[3]),
    ]
    for copy in local:
        copy.start()
    local[0].wait()
    for c in range(tiles):
        mine[z, 0, c * slots:(c + 1) * slots, :] = cache_ref[:, c * LANES:(c + 1) * LANES]
    rotary_keys = cache_ref[:, LATENT_WIDTH:]
    mine[z, 0, tiles * slots:, :] = jnp.concatenate(
        [rotary_keys[:half_slots], rotary_keys[half_slots:]], axis=1
    )
    pl.semaphore_wait(barrier, len(partners))

    sends, middle_sends = [], []

    def send(src, dst, recv, to, only_middle=False):
        copy = pltpu.make_async_remote_copy(
            src_ref=src, dst_ref=dst, recv_sem=recv,
            send_sem=send_sem.at[len(sends) + len(middle_sends)],
            device_id=to, device_id_type=MESH,
        )
        if only_middle:
            pl.when(middle)(copy.start)
            middle_sends.append(copy)
        else:
            copy.start()
            sends.append(copy)
        return copy

    def arrived(ref, sem):
        pltpu.make_async_copy(ref, ref, sem).wait()

    def rows(k, p, half):
        return mine.at[k, p, pl.ds(half * half_rows, half_rows)]

    def share_column(i):
        k = levels[i]
        if i in (0, 3):
            send(rows(k, 0, 1), rows(k, 1, 1), mine_recv.at[k, 1], x_peer)
            send(rows(k, 0, 0), rows(k, 2, 0), mine_recv.at[k, 2], y_peer)
            send(rows(k, 0, 0), rows(k, 1, 0), rest_recv.at[k, 0], x_peer)
            send(rows(k, 0, 1), rows(k, 2, 1), rest_recv.at[k, 1], y_peer)
        else:
            send(mine.at[k, 0], mine.at[k, 1], mine_recv.at[k, 1], x_peer)
            send(mine.at[k, 0], mine.at[k, 2], mine_recv.at[k, 2], y_peer)

    def along_z(k, to, only_middle):
        return send(mine.at[k, 0], mine.at[k, 0], mine_recv.at[k, 0], to, only_middle)

    def column_step(i):
        k = levels[i]
        arrived(mine.at[k, 0], mine_recv.at[k, 0])
        if i == 1:
            along_z(k, pair_peer, True)
        share_column(i)

    def plane_step(i):
        k = levels[i]
        if i in (0, 3):
            arrived(rows(k, 1, 1), mine_recv.at[k, 1])
            send(rows(k, 1, 1), rows(k, 3, 1), half_recv.at[k, 1], y_peer)
            arrived(rows(k, 2, 0), mine_recv.at[k, 2])
            send(rows(k, 2, 0), rows(k, 3, 0), half_recv.at[k, 0], x_peer)
        else:
            arrived(mine.at[k, 1], mine_recv.at[k, 1])
            arrived(mine.at[k, 2], mine_recv.at[k, 2])

    def plane_rest(i):
        k = levels[i]
        arrived(rows(k, 1, 0), rest_recv.at[k, 0])
        arrived(rows(k, 2, 1), rest_recv.at[k, 1])

    def diagonal_along_z(k, to, only_middle):
        send(mine.at[k, 3], mine.at[k, 3], whole_recv.at[k], to, only_middle)

    def diagonal_step(i):
        k = levels[i]
        if i in (0, 3):
            for half in (0, 1):
                arrived(rows(k, 3, half), half_recv.at[k, half])
        else:
            arrived(mine.at[k, 3], whole_recv.at[k])
        if i == 0:
            diagonal_along_z(k, pair_peer, False)
            diagonal_along_z(k, mirror_peer, True)
        if i == 1:
            diagonal_along_z(k, pair_peer, True)

    def project_queries(first, last):
        zeros = jnp.zeros((2 * tokens, ROTARY_WIDTH), jnp.bfloat16)
        both = jnp.concatenate([queries_ref[0], queries_ref[1]], axis=0)
        for h in range(first, last):
            plain = both[:, h * HEAD_WIDTH:h * HEAD_WIDTH + PLAIN_WIDTH]
            rotary = both[:, h * HEAD_WIDTH + PLAIN_WIDTH:(h + 1) * HEAD_WIDTH]
            latent = jnp.dot(
                plain, key_half[h], preferred_element_type=jnp.float32
            ).astype(jnp.bfloat16)
            low = jnp.concatenate([rotary, zeros], axis=1)
            high = jnp.concatenate([zeros, rotary], axis=1)
            for c in (0, 1):
                there = slice(c * core_rows + h * tokens, c * core_rows + (h + 1) * tokens)
                of = slice(c * tokens, (c + 1) * tokens)
                query_latent[core, there, :] = latent[of]
                query_rotary[0, there, :] = low[of]
                query_rotary[1, there, :] = high[of]

    score_scale = HEAD_WIDTH ** (-0.5)
    group_slots = slots * Z_CHIPS * Y_CHIPS * X_CHIPS

    def attend(state, blocks, part_of=None):
        if part_of is None:
            here = pl.ds(0, flat_rows)
            flat_row = lax.broadcasted_iota(jnp.int32, (flat_rows, 1), 0)
            query_place = prior_ref[0] + flat_row // core_rows * tokens + flat_row % tokens
        else:
            here = pl.ds(pl.multiple_of(part_of * core_rows, core_rows), core_rows)
            flat_row = lax.broadcasted_iota(jnp.int32, (core_rows, 1), 0)
            query_place = prior_ref[0] + part_of * tokens + flat_row % tokens
        blocks = [(levels[i], p) for i, p in blocks]
        bases = []
        for k, p in blocks:
            source = chip(k, 1 - y if p in (2, 3) else y, 1 - x if p in (1, 3) else x)
            bases.append(core * group_slots + source * slots)
        width = 4 * half_slots

        def latent_of(part):
            return jnp.concatenate(
                [
                    jnp.concatenate(
                        [
                            mine[k, p, pl.ds(c * slots + part * half_slots, half_slots), :]
                            for c in range(tiles)
                        ],
                        axis=1,
                    )
                    for k, p in blocks
                ],
                axis=0,
            )

        latents = jnp.concatenate([latent_of(0), latent_of(1)], axis=0)
        rotary = jnp.concatenate(
            [mine[k, p, pl.ds(tiles * slots, half_slots), :] for k, p in blocks], axis=0
        )
        column = lax.broadcasted_iota(jnp.int32, (1, 2 * width), 1)
        key_place = column
        for b in range(8):
            inside = (column >= b * half_slots) & (column < (b + 1) * half_slots)
            shift = bases[b % 4] + (b // 4) * half_slots - b * half_slots
            key_place = key_place + jnp.where(inside, shift, 0)
        contract = (((1,), (1,)), ((), ()))
        rotary_scores = [
            lax.dot_general(
                query_rotary[part, here, :], rotary, contract, preferred_element_type=jnp.float32
            )
            for part in (0, 1)
        ]
        scores = lax.dot_general(
            jnp.concatenate([query_latent[0, here, :], query_latent[1, here, :]], axis=1), latents, contract,
            preferred_element_type=jnp.float32,
        )
        scores = (scores + jnp.concatenate(rotary_scores, axis=1)) * score_scale
        visible = key_place <= query_place
        scores = jnp.where(visible, scores, -1e30)
        peak = jnp.max(scores, axis=1, keepdims=True)
        if state is not None:
            peak = jnp.maximum(peak, state[0])
        probs = jnp.where(visible, jnp.exp(scores - peak), 0.0)
        total = jnp.sum(probs, axis=1, keepdims=True)
        weighted = jnp.dot(
            probs.astype(jnp.bfloat16), latents, preferred_element_type=jnp.float32
        )
        if state is None:
            numerator[here, :] = weighted
        else:
            shrink = jnp.exp(state[0] - peak)
            total = total + state[1] * shrink
            numerator[here, :] = numerator[here, :] * shrink + weighted
        return peak, total

    along_z(z, pair_peer, False)
    own_mirrored = along_z(z, mirror_peer, True)
    share_column(0)
    send(queries_hbm, queries_ref.at[core], core_recv.at[0], core_peer)
    local[1].wait()
    local[2].wait()
    arrived(queries_ref.at[1 - core], core_recv.at[0])
    project_queries(0, heads // 2)
    sends.append(middle_sends.pop(0))
    pl.when(jnp.logical_not(middle))(own_mirrored.start)
    column_step(1)
    plane_step(0)

    @pl.when(middle)
    def _():
        arrived(mine.at[levels[2], 0], mine_recv.at[levels[2], 0])

    along_z(levels[2], mirror_peer, True)
    project_queries(heads // 2, heads)
    send(query_latent.at[core], query_latent.at[core], core_recv.at[1], core_peer)

    @pl.when(jnp.logical_not(middle))
    def _():
        arrived(mine.at[levels[2], 0], mine_recv.at[levels[2], 0])

    share_column(2)
    send(value_hbm, value_panel.at[core], core_recv.at[2], core_peer)
    diagonal_step(0)
    plane_rest(0)
    arrived(query_latent.at[1 - core], core_recv.at[1])
    state = attend(None, [(0, p) for p in range(4)])
    column_step(3)
    diagonal_step(1)
    plane_step(1)
    state = attend(state, [(1, p) for p in range(4)])
    plane_step(2)
    plane_step(3)
    state = attend(state, [(2, 0), (2, 1), (2, 2), (3, 0)])
    plane_rest(3)
    diagonal_step(2)
    diagonal_step(3)
    pick = core == 0
    low = [value[:core_rows] for value in state]
    high = [value[core_rows:] for value in state]
    last = [(2, 3), (3, 1), (3, 2), (3, 3)]
    their_state = [jnp.where(pick, b, a) for a, b in zip(low, high)]
    our_state = [jnp.where(pick, a, b) for a, b in zip(low, high)]
    peak, total = attend(their_state, last, 1 - core)
    lane = lax.broadcasted_iota(jnp.int32, (core_rows, LANES), 1)
    own_stats[...] = jnp.where(lane < LANES // 2, peak, total)
    theirs = pl.ds(pl.multiple_of((1 - core) * core_rows, core_rows), core_rows)
    ours = pl.ds(pl.multiple_of(core * core_rows, core_rows), core_rows)
    own_part[...] = numerator[theirs, :].astype(jnp.bfloat16)
    send(own_part, peer_part, core_recv.at[4], core_peer)
    send(own_stats, peer_stats, core_recv.at[3], core_peer)
    our_peak, our_total = attend(our_state, last, core)

    local[3].wait()
    arrived(value_panel.at[1 - core], core_recv.at[2])
    arrived(peer_stats, core_recv.at[3])
    their_peak = peer_stats[:, 0:1]
    their_total = peer_stats[:, LANES // 2:LANES // 2 + 1]
    joint_peak = jnp.maximum(our_peak, their_peak)
    our_weight = jnp.exp(our_peak - joint_peak)
    their_weight = jnp.exp(their_peak - joint_peak)
    joint_total = our_total * our_weight + their_total * their_weight
    our_weight = our_weight / joint_total
    their_weight = their_weight / joint_total
    arrived(peer_part, core_recv.at[4])
    averaged = (
        numerator[ours, :] * our_weight + peer_part[...].astype(jnp.float32) * their_weight
    ).astype(jnp.bfloat16)
    for h in range(heads):
        here = slice(h * tokens, (h + 1) * tokens)
        result = lax.dot_general(
            averaged[here], jnp.concatenate([value_panel[0, h], value_panel[1, h]], axis=1),
            (((1,), (1,)), ((), ())), preferred_element_type=jnp.float32,
        )
        out_ref[:, h * VALUE_WIDTH:(h + 1) * VALUE_WIDTH] = result.astype(jnp.bfloat16)
    for copy in sends:
        copy.wait_send()

    @pl.when(middle)
    def _():
        for copy in middle_sends:
            copy.wait_send()


def per_device_fused(queries, cache, key_up_weight, value_up_weight, prior_len):
    heads = key_up_weight.shape[0]
    tokens = queries.shape[0]
    slots = cache.shape[0]
    block_rows = slots * cache.shape[1] // LANES
    core_rows = heads * tokens
    hbm = pl.BlockSpec(memory_space=pltpu.HBM)
    dma = pltpu.SemaphoreType.DMA
    vmem = pltpu.VMEM
    return pl.pallas_call(
        fused_kernel,
        out_shape=jax.ShapeDtypeStruct((tokens, heads * VALUE_WIDTH), jnp.bfloat16),
        in_specs=[hbm, hbm, hbm, hbm, pl.BlockSpec(memory_space=pltpu.SMEM)],
        out_specs=pl.BlockSpec(memory_space=pltpu.VMEM),
        scratch_shapes=[
            vmem((2,) + queries.shape, jnp.bfloat16),
            vmem(cache.shape, jnp.bfloat16),
            vmem((4, 4, block_rows, LANES), jnp.bfloat16),
            vmem(key_up_weight.shape, jnp.bfloat16),
            vmem((2,) + value_up_weight.shape, jnp.bfloat16),
            vmem((2, 2 * core_rows, LATENT_WIDTH // 2), jnp.bfloat16),
            vmem((2, 2 * core_rows, LANES), jnp.bfloat16),
            vmem((2 * core_rows, LATENT_WIDTH), jnp.float32),
            vmem((core_rows, LATENT_WIDTH), jnp.bfloat16),
            vmem((core_rows, LATENT_WIDTH), jnp.bfloat16),
            vmem((core_rows, LANES), jnp.float32),
            vmem((core_rows, LANES), jnp.float32),
            dma((4, 3)), dma((4, 2)), dma((4, 2)), dma((4,)), dma((40,)), dma((5,)), dma((4,)),
        ],
        compiler_params=pltpu.CompilerParams(
            collective_id=0, has_side_effects=True, vmem_limit_bytes=(64 * 1024 - 10375) * 1024
        ),
    )(queries, cache, key_up_weight, value_up_weight, prior_len)


def solution(mesh):
    in_specs = (
        P("ctx", "head"),
        P(("ctx", "head"), None),
        P("head", None, "ctx"),
        P("head", None, "ctx"),
        P(),
    )
    out_specs = P("ctx", "head")
    chips = Z_CHIPS * Y_CHIPS * X_CHIPS
    body = per_device_fused if mesh.shape["ctx"] == 2 and mesh.shape["head"] == chips else per_device
    return jax.shard_map(
        body, mesh=mesh, in_specs=in_specs, out_specs=out_specs, check_vma=False
    )
```

```python
import jax
import jax.numpy as jnp
from jax import lax
from jax.experimental import pallas as pl
from jax.experimental.pallas import tpu as pltpu
from jax.sharding import PartitionSpec as P

PLAIN_WIDTH = 128
ROTARY_WIDTH = 64
LATENT_WIDTH = 512
VALUE_WIDTH = 128


def per_device(queries, cache, key_up_weight, value_up_weight, prior_len):
    heads_number = key_up_weight.shape[0]
    block_rows = queries.shape[0]
    combined_width = LATENT_WIDTH + ROTARY_WIDTH
    key_panel, value_panel = (
        lax.all_gather(key_up_weight, "ctx", axis=2, tiled=True),
        lax.all_gather(value_up_weight, "ctx", axis=2, tiled=True),
    )
    gathered = lax.all_gather(queries, "ctx", axis=0, tiled=True)
    split_rows = gathered.reshape(gathered.shape[0], heads_number, PLAIN_WIDTH + ROTARY_WIDTH)
    latent = jnp.einsum(
        "thn,hnc->thc",
        split_rows[:, :, :PLAIN_WIDTH],
        key_panel,
        preferred_element_type=jnp.float32,
    ).astype(jnp.bfloat16)
    flat_queries = jnp.concatenate([latent, split_rows[:, :, PLAIN_WIDTH:]], axis=2).reshape(
        -1, combined_width
    )
    flat_rows = flat_queries.shape[0]
    query_number = flat_rows // heads_number
    query_place = prior_len[0] + jnp.arange(flat_rows, dtype=jnp.int32) // heads_number
    group_slots = cache.shape[0] * lax.axis_size("head")
    block_base = lax.axis_index("ctx") * group_slots
    score_scale = (PLAIN_WIDTH + ROTARY_WIDTH) ** (-0.5)
    key_section = lax.all_gather(cache, "head", axis=0, tiled=True)
    row_peak = jnp.full((flat_rows,), -1e30, jnp.float32)
    key_count = key_section.shape[0]
    scores = (
        jnp.einsum("rc,nc->rn", flat_queries, key_section, preferred_element_type=jnp.float32)
        * score_scale
    )
    key_place = block_base + jnp.arange(key_count, dtype=jnp.int32)
    visible = key_place[None, :] <= query_place[:, None]
    scores = jnp.where(visible, scores, jnp.float32(-1e30))
    new_peak = jnp.maximum(row_peak, jnp.max(scores, axis=1))
    probabilities = jnp.where(visible, jnp.exp(scores - new_peak[:, None]), jnp.float32(0.0))
    row_total = jnp.sum(probabilities, axis=1)
    weighted_values = jnp.dot(
        probabilities.astype(jnp.bfloat16),
        key_section[:, :LATENT_WIDTH],
        preferred_element_type=jnp.float32,
    )
    row_peak, row_total, weighted_values = (new_peak, row_total, weighted_values)
    global_peak = lax.pmax(row_peak, "ctx")
    softmax_scale = jnp.exp(row_peak - global_peak)
    scaled_sums = (row_total * softmax_scale).reshape(query_number, heads_number)
    latent_scaled = (weighted_values * softmax_scale[:, None]).reshape(
        query_number, heads_number * LATENT_WIDTH
    )
    block_latent, own_totals = (
        lax.psum_scatter(
            latent_scaled.astype(jnp.bfloat16), "ctx", scatter_dimension=0, tiled=True
        ).astype(jnp.float32),
        lax.psum_scatter(
            scaled_sums.astype(jnp.bfloat16), "ctx", scatter_dimension=0, tiled=True
        ).astype(jnp.float32),
    )
    reshaped_queries = block_latent.reshape(block_rows, heads_number, LATENT_WIDTH)
    projected = jnp.einsum(
        "thc,hvc->thv",
        reshaped_queries,
        value_panel.astype(jnp.float32),
        precision=lax.Precision.HIGHEST,
    )
    result = projected / own_totals[:, :, None]
    return result.reshape(block_rows, heads_number * VALUE_WIDTH).astype(jnp.bfloat16)


MESH = pl.DeviceIdType.MESH
HEAD_WIDTH = PLAIN_WIDTH + ROTARY_WIDTH
Z_CHIPS, Y_CHIPS, X_CHIPS = 4, 2, 2
LANES = 128
LOG2_E = 1.4426950408889634


def fused_kernel(
    queries_hbm, cache_hbm, key_hbm, value_hbm, prior_ref, out_ref,
    queries_ref, cache_ref, mine, key_half, value_panel, query_latent, query_rotary,
    numerator, own_part, peer_part, own_stats, peer_stats,
    mine_recv, rest_recv, half_recv, whole_recv, send_sem, core_recv, local_sem,
):
    core = lax.axis_index("ctx")
    place = lax.axis_index("head")
    z = place // (Y_CHIPS * X_CHIPS)
    y = (place // X_CHIPS) % Y_CHIPS
    x = place % X_CHIPS
    heads = key_hbm.shape[0]
    tokens = queries_hbm.shape[0]
    slots = cache_hbm.shape[0]
    half_slots = slots // 2
    tiles = LATENT_WIDTH // LANES
    half_rows = mine.shape[2] // 2
    core_rows = heads * tokens
    flat_rows = 2 * core_rows

    def chip(zz, yy, xx):
        return (zz * Y_CHIPS + yy) * X_CHIPS + xx

    middle = z % 3 != 0
    levels = [z, 1 + z % 2, 2 - 2 * (z % 2) + z // 2, 3 - 3 * (z // 2)]
    x_peer = (core, chip(z, y, 1 - x))
    y_peer = (core, chip(z, 1 - y, x))
    core_peer = (1 - core, place)
    pair_peer = (core, chip(z + 1 - 2 * (z % 2), y, x))
    mirror_peer = (core, chip(3 - z, y, x))
    partners = [x_peer, y_peer, core_peer, pair_peer, mirror_peer]

    barrier = pltpu.get_barrier_semaphore()
    for partner in partners:
        pl.semaphore_signal(barrier, inc=1, device_id=partner, device_id_type=MESH)

    local = [
        pltpu.make_async_copy(cache_hbm, cache_ref, local_sem.at[0]),
        pltpu.make_async_copy(queries_hbm, queries_ref.at[core], local_sem.at[1]),
        pltpu.make_async_copy(key_hbm, key_half, local_sem.at[2]),
        pltpu.make_async_copy(value_hbm, value_panel.at[core], local_sem.at[3]),
    ]
    for copy in local:
        copy.start()
    local[0].wait()
    for c in range(tiles):
        mine[z, 0, c * slots:(c + 1) * slots, :] = cache_ref[:, c * LANES:(c + 1) * LANES]
    rotary_keys = cache_ref[:, LATENT_WIDTH:]
    mine[z, 0, tiles * slots:, :] = jnp.concatenate(
        [rotary_keys[:half_slots], rotary_keys[half_slots:]], axis=1
    )
    pl.semaphore_wait(barrier, len(partners))

    sends, middle_sends = [], []

    def send(src, dst, recv, to, only_middle=False):
        copy = pltpu.make_async_remote_copy(
            src_ref=src, dst_ref=dst, recv_sem=recv,
            send_sem=send_sem.at[len(sends) + len(middle_sends)],
            device_id=to, device_id_type=MESH,
        )
        if only_middle:
            pl.when(middle)(copy.start)
            middle_sends.append(copy)
        else:
            copy.start()
            sends.append(copy)
        return copy

    def arrived(ref, sem):
        pltpu.make_async_copy(ref, ref, sem).wait()

    def rows(k, p, half):
        return mine.at[k, p, pl.ds(half * half_rows, half_rows)]

    def share_column(i):
        k = levels[i]
        if i in (0, 3):
            send(rows(k, 0, 1), rows(k, 1, 1), mine_recv.at[k, 1], x_peer)
            send(rows(k, 0, 0), rows(k, 2, 0), mine_recv.at[k, 2], y_peer)
            send(rows(k, 0, 0), rows(k, 1, 0), rest_recv.at[k, 0], x_peer)
            send(rows(k, 0, 1), rows(k, 2, 1), rest_recv.at[k, 1], y_peer)
        else:
            send(mine.at[k, 0], mine.at[k, 1], mine_recv.at[k, 1], x_peer)
            send(mine.at[k, 0], mine.at[k, 2], mine_recv.at[k, 2], y_peer)

    def along_z(k, to, only_middle):
        return send(mine.at[k, 0], mine.at[k, 0], mine_recv.at[k, 0], to, only_middle)

    def column_step(i):
        k = levels[i]
        arrived(mine.at[k, 0], mine_recv.at[k, 0])
        if i == 1:
            along_z(k, pair_peer, True)
        share_column(i)

    def plane_step(i):
        k = levels[i]
        if i in (0, 3):
            arrived(rows(k, 1, 1), mine_recv.at[k, 1])
            send(rows(k, 1, 1), rows(k, 3, 1), half_recv.at[k, 1], y_peer)
            arrived(rows(k, 2, 0), mine_recv.at[k, 2])
            send(rows(k, 2, 0), rows(k, 3, 0), half_recv.at[k, 0], x_peer)
        else:
            arrived(mine.at[k, 1], mine_recv.at[k, 1])
            arrived(mine.at[k, 2], mine_recv.at[k, 2])

    def plane_rest(i):
        k = levels[i]
        arrived(rows(k, 1, 0), rest_recv.at[k, 0])
        arrived(rows(k, 2, 1), rest_recv.at[k, 1])

    def diagonal_along_z(k, to, only_middle):
        send(mine.at[k, 3], mine.at[k, 3], whole_recv.at[k], to, only_middle)

    def diagonal_step(i):
        k = levels[i]
        if i in (0, 3):
            for half in (0, 1):
                arrived(rows(k, 3, half), half_recv.at[k, half])
        else:
            arrived(mine.at[k, 3], whole_recv.at[k])
        if i == 0:
            diagonal_along_z(k, pair_peer, False)
            diagonal_along_z(k, mirror_peer, True)
        if i == 1:
            diagonal_along_z(k, pair_peer, True)

    def project_queries(first, last):
        both = jnp.concatenate([queries_ref[0], queries_ref[1]], axis=0)
        for h in range(first, last):
            plain = both[:, h * HEAD_WIDTH:h * HEAD_WIDTH + PLAIN_WIDTH]
            rotary = both[:, h * HEAD_WIDTH + PLAIN_WIDTH:(h + 1) * HEAD_WIDTH]
            latent = jnp.dot(
                plain, key_half[h], preferred_element_type=jnp.float32
            ).astype(jnp.bfloat16)
            twice = jnp.concatenate([rotary, rotary], axis=1)
            for c in (0, 1):
                there = slice(c * core_rows + h * tokens, c * core_rows + (h + 1) * tokens)
                of = slice(c * tokens, (c + 1) * tokens)
                query_latent[core, there, :] = latent[of]
                query_rotary[there, :] = twice[of]

    score_scale = HEAD_WIDTH ** (-0.5) * LOG2_E
    key_lane = lax.broadcasted_iota(jnp.int32, (1, LANES), 1)
    low_lanes = jnp.where(key_lane < ROTARY_WIDTH, 1.0, 0.0).astype(jnp.bfloat16)
    high_lanes = jnp.where(key_lane < ROTARY_WIDTH, 0.0, 1.0).astype(jnp.bfloat16)
    group_slots = slots * Z_CHIPS * Y_CHIPS * X_CHIPS

    def attend(state, blocks, part_of=None):
        if part_of is None:
            here = pl.ds(0, flat_rows)
            flat_row = lax.broadcasted_iota(jnp.int32, (flat_rows, 1), 0)
            query_place = prior_ref[0] + flat_row // core_rows * tokens + flat_row % tokens
        else:
            here = pl.ds(pl.multiple_of(part_of * core_rows, core_rows), core_rows)
            flat_row = lax.broadcasted_iota(jnp.int32, (core_rows, 1), 0)
            query_place = prior_ref[0] + part_of * tokens + flat_row % tokens
        blocks = [(levels[i], p) for i, p in blocks]
        bases = []
        for k, p in blocks:
            source = chip(k, 1 - y if p in (2, 3) else y, 1 - x if p in (1, 3) else x)
            bases.append(core * group_slots + source * slots)
        width = 4 * half_slots

        def latent_of(part):
            return jnp.concatenate(
                [
                    jnp.concatenate(
                        [
                            mine[k, p, pl.ds(c * slots + part * half_slots, half_slots), :]
                            for c in range(tiles)
                        ],
                        axis=1,
                    )
                    for k, p in blocks
                ],
                axis=0,
            )

        latents = jnp.concatenate([latent_of(0), latent_of(1)], axis=0)
        rotary = jnp.concatenate(
            [mine[k, p, pl.ds(tiles * slots, half_slots), :] for k, p in blocks], axis=0
        )
        column = lax.broadcasted_iota(jnp.int32, (1, 2 * width), 1)
        key_place = column
        for b in range(8):
            inside = (column >= b * half_slots) & (column < (b + 1) * half_slots)
            shift = bases[b % 4] + (b // 4) * half_slots - b * half_slots
            key_place = key_place + jnp.where(inside, shift, 0)
        keys = jnp.concatenate(
            [latents, jnp.concatenate([rotary * low_lanes, rotary * high_lanes], axis=0)], axis=1
        )
        query = jnp.concatenate(
            [query_latent[0, here, :], query_latent[1, here, :], query_rotary[here, :]], axis=1
        )
        scores = lax.dot_general(
            query, keys, (((1,), (1,)), ((), ())), preferred_element_type=jnp.float32
        )
        scores = jnp.where(key_place <= query_place, scores * score_scale, -1e30)
        peak = jnp.maximum(jnp.max(scores, axis=1, keepdims=True), -1e29)
        if state is not None:
            peak = jnp.maximum(peak, state[0])
        probs = jnp.exp2(scores - peak)
        total = jnp.sum(probs, axis=1, keepdims=True)
        weighted = jnp.dot(
            probs.astype(jnp.bfloat16), latents, preferred_element_type=jnp.float32
        )
        if state is None:
            numerator[here, :] = weighted
        else:
            shrink = jnp.exp2(state[0] - peak)
            total = total + state[1] * shrink
            numerator[here, :] = numerator[here, :] * shrink + weighted
        return peak, total

    along_z(z, pair_peer, False)
    own_mirrored = along_z(z, mirror_peer, True)
    share_column(0)
    send(queries_hbm, queries_ref.at[core], core_recv.at[0], core_peer)
    local[1].wait()
    local[2].wait()
    arrived(queries_ref.at[1 - core], core_recv.at[0])
    project_queries(0, heads // 2)
    sends.append(middle_sends.pop(0))
    pl.when(jnp.logical_not(middle))(own_mirrored.start)
    column_step(1)
    plane_step(0)

    @pl.when(middle)
    def _():
        arrived(mine.at[levels[2], 0], mine_recv.at[levels[2], 0])

    along_z(levels[2], mirror_peer, True)
    project_queries(heads // 2, heads)
    send(query_latent.at[core], query_latent.at[core], core_recv.at[1], core_peer)

    @pl.when(jnp.logical_not(middle))
    def _():
        arrived(mine.at[levels[2], 0], mine_recv.at[levels[2], 0])

    share_column(2)
    send(value_hbm, value_panel.at[core], core_recv.at[2], core_peer)
    diagonal_step(0)
    plane_rest(0)
    arrived(query_latent.at[1 - core], core_recv.at[1])
    state = attend(None, [(0, p) for p in range(4)])
    column_step(3)
    diagonal_step(1)
    plane_step(1)
    state = attend(state, [(1, p) for p in range(4)])
    plane_step(2)
    plane_step(3)
    state = attend(state, [(2, 0), (2, 1), (2, 2), (3, 0)])
    plane_rest(3)
    diagonal_step(2)
    diagonal_step(3)
    pick = core == 0
    low = [value[:core_rows] for value in state]
    high = [value[core_rows:] for value in state]
    last = [(2, 3), (3, 1), (3, 2), (3, 3)]
    their_state = [jnp.where(pick, b, a) for a, b in zip(low, high)]
    our_state = [jnp.where(pick, a, b) for a, b in zip(low, high)]
    peak, total = attend(their_state, last, 1 - core)
    lane = lax.broadcasted_iota(jnp.int32, (core_rows, LANES), 1)
    own_stats[...] = jnp.where(lane < LANES // 2, peak, total)
    theirs = pl.ds(pl.multiple_of((1 - core) * core_rows, core_rows), core_rows)
    ours = pl.ds(pl.multiple_of(core * core_rows, core_rows), core_rows)
    own_part[...] = numerator[theirs, :].astype(jnp.bfloat16)
    send(own_part, peer_part, core_recv.at[4], core_peer)
    send(own_stats, peer_stats, core_recv.at[3], core_peer)
    our_peak, our_total = attend(our_state, last, core)

    local[3].wait()
    arrived(value_panel.at[1 - core], core_recv.at[2])
    arrived(peer_stats, core_recv.at[3])
    their_peak = peer_stats[:, 0:1]
    their_total = peer_stats[:, LANES // 2:LANES // 2 + 1]
    joint_peak = jnp.maximum(our_peak, their_peak)
    our_weight = jnp.exp2(our_peak - joint_peak)
    their_weight = jnp.exp2(their_peak - joint_peak)
    joint_total = our_total * our_weight + their_total * their_weight
    our_weight = our_weight / joint_total
    their_weight = their_weight / joint_total
    arrived(peer_part, core_recv.at[4])
    averaged = (
        numerator[ours, :] * our_weight + peer_part[...].astype(jnp.float32) * their_weight
    ).astype(jnp.bfloat16)
    for h in range(heads):
        here = slice(h * tokens, (h + 1) * tokens)
        result = lax.dot_general(
            averaged[here], jnp.concatenate([value_panel[0, h], value_panel[1, h]], axis=1),
            (((1,), (1,)), ((), ())), preferred_element_type=jnp.float32,
        )
        out_ref[:, h * VALUE_WIDTH:(h + 1) * VALUE_WIDTH] = result.astype(jnp.bfloat16)
    for copy in sends:
        copy.wait_send()

    @pl.when(middle)
    def _():
        for copy in middle_sends:
            copy.wait_send()


def per_device_fused(queries, cache, key_up_weight, value_up_weight, prior_len):
    heads = key_up_weight.shape[0]
    tokens = queries.shape[0]
    slots = cache.shape[0]
    block_rows = slots * cache.shape[1] // LANES
    core_rows = heads * tokens
    hbm = pl.BlockSpec(memory_space=pltpu.HBM)
    dma = pltpu.SemaphoreType.DMA
    vmem = pltpu.VMEM
    return pl.pallas_call(
        fused_kernel,
        out_shape=jax.ShapeDtypeStruct((tokens, heads * VALUE_WIDTH), jnp.bfloat16),
        in_specs=[hbm, hbm, hbm, hbm, pl.BlockSpec(memory_space=pltpu.SMEM)],
        out_specs=pl.BlockSpec(memory_space=pltpu.VMEM),
        scratch_shapes=[
            vmem((2,) + queries.shape, jnp.bfloat16),
            vmem(cache.shape, jnp.bfloat16),
            vmem((4, 4, block_rows, LANES), jnp.bfloat16),
            vmem(key_up_weight.shape, jnp.bfloat16),
            vmem((2,) + value_up_weight.shape, jnp.bfloat16),
            vmem((2, 2 * core_rows, LATENT_WIDTH // 2), jnp.bfloat16),
            vmem((2 * core_rows, LANES), jnp.bfloat16),
            vmem((2 * core_rows, LATENT_WIDTH), jnp.float32),
            vmem((core_rows, LATENT_WIDTH), jnp.bfloat16),
            vmem((core_rows, LATENT_WIDTH), jnp.bfloat16),
            vmem((core_rows, LANES), jnp.float32),
            vmem((core_rows, LANES), jnp.float32),
            dma((4, 3)), dma((4, 2)), dma((4, 2)), dma((4,)), dma((40,)), dma((5,)), dma((4,)),
        ],
        compiler_params=pltpu.CompilerParams(
            collective_id=0, has_side_effects=True, vmem_limit_bytes=(64 * 1024 - 10375) * 1024
        ),
    )(queries, cache, key_up_weight, value_up_weight, prior_len)


def solution(mesh):
    in_specs = (
        P("ctx", "head"),
        P(("ctx", "head"), None),
        P("head", None, "ctx"),
        P("head", None, "ctx"),
        P(),
    )
    out_specs = P("ctx", "head")
    chips = Z_CHIPS * Y_CHIPS * X_CHIPS
    body = per_device_fused if mesh.shape["ctx"] == 2 and mesh.shape["head"] == chips else per_device
    return jax.shard_map(
        body, mesh=mesh, in_specs=in_specs, out_specs=out_specs, check_vma=False
    )
```

```python
import jax
import jax.numpy as jnp
from jax import lax
from jax.experimental import pallas as pl
from jax.experimental.pallas import tpu as pltpu
from jax.sharding import PartitionSpec as P

PLAIN_WIDTH = 128
ROTARY_WIDTH = 64
LATENT_WIDTH = 512
VALUE_WIDTH = 128


def per_device(queries, cache, key_up_weight, value_up_weight, prior_len):
    heads_number = key_up_weight.shape[0]
    block_rows = queries.shape[0]
    combined_width = LATENT_WIDTH + ROTARY_WIDTH
    key_panel, value_panel = (
        lax.all_gather(key_up_weight, "ctx", axis=2, tiled=True),
        lax.all_gather(value_up_weight, "ctx", axis=2, tiled=True),
    )
    gathered = lax.all_gather(queries, "ctx", axis=0, tiled=True)
    split_rows = gathered.reshape(gathered.shape[0], heads_number, PLAIN_WIDTH + ROTARY_WIDTH)
    latent = jnp.einsum(
        "thn,hnc->thc",
        split_rows[:, :, :PLAIN_WIDTH],
        key_panel,
        preferred_element_type=jnp.float32,
    ).astype(jnp.bfloat16)
    flat_queries = jnp.concatenate([latent, split_rows[:, :, PLAIN_WIDTH:]], axis=2).reshape(
        -1, combined_width
    )
    flat_rows = flat_queries.shape[0]
    query_number = flat_rows // heads_number
    query_place = prior_len[0] + jnp.arange(flat_rows, dtype=jnp.int32) // heads_number
    group_slots = cache.shape[0] * lax.axis_size("head")
    block_base = lax.axis_index("ctx") * group_slots
    score_scale = (PLAIN_WIDTH + ROTARY_WIDTH) ** (-0.5)
    key_section = lax.all_gather(cache, "head", axis=0, tiled=True)
    row_peak = jnp.full((flat_rows,), -1e30, jnp.float32)
    key_count = key_section.shape[0]
    scores = (
        jnp.einsum("rc,nc->rn", flat_queries, key_section, preferred_element_type=jnp.float32)
        * score_scale
    )
    key_place = block_base + jnp.arange(key_count, dtype=jnp.int32)
    visible = key_place[None, :] <= query_place[:, None]
    scores = jnp.where(visible, scores, jnp.float32(-1e30))
    new_peak = jnp.maximum(row_peak, jnp.max(scores, axis=1))
    probabilities = jnp.where(visible, jnp.exp(scores - new_peak[:, None]), jnp.float32(0.0))
    row_total = jnp.sum(probabilities, axis=1)
    weighted_values = jnp.dot(
        probabilities.astype(jnp.bfloat16),
        key_section[:, :LATENT_WIDTH],
        preferred_element_type=jnp.float32,
    )
    row_peak, row_total, weighted_values = (new_peak, row_total, weighted_values)
    global_peak = lax.pmax(row_peak, "ctx")
    softmax_scale = jnp.exp(row_peak - global_peak)
    scaled_sums = (row_total * softmax_scale).reshape(query_number, heads_number)
    latent_scaled = (weighted_values * softmax_scale[:, None]).reshape(
        query_number, heads_number * LATENT_WIDTH
    )
    block_latent, own_totals = (
        lax.psum_scatter(
            latent_scaled.astype(jnp.bfloat16), "ctx", scatter_dimension=0, tiled=True
        ).astype(jnp.float32),
        lax.psum_scatter(
            scaled_sums.astype(jnp.bfloat16), "ctx", scatter_dimension=0, tiled=True
        ).astype(jnp.float32),
    )
    reshaped_queries = block_latent.reshape(block_rows, heads_number, LATENT_WIDTH)
    projected = jnp.einsum(
        "thc,hvc->thv",
        reshaped_queries,
        value_panel.astype(jnp.float32),
        precision=lax.Precision.HIGHEST,
    )
    result = projected / own_totals[:, :, None]
    return result.reshape(block_rows, heads_number * VALUE_WIDTH).astype(jnp.bfloat16)


MESH = pl.DeviceIdType.MESH
HEAD_WIDTH = PLAIN_WIDTH + ROTARY_WIDTH
Z_CHIPS, Y_CHIPS, X_CHIPS = 4, 2, 2
LANES = 128


def fused_kernel(
    queries_hbm, cache_hbm, key_hbm, value_hbm, prior_hbm, out_ref,
    prior_ref, queries_ref, cache_ref, mine, key_half, value_panel, query_latent, query_rotary,
    numerator, own_part, peer_part, own_stats, peer_stats,
    mine_recv, rest_recv, half_recv, whole_recv, send_sem, core_recv, local_sem,
):
    core = lax.axis_index("ctx")
    place = lax.axis_index("head")
    z = place // (Y_CHIPS * X_CHIPS)
    y = (place // X_CHIPS) % Y_CHIPS
    x = place % X_CHIPS
    heads = key_hbm.shape[0]
    tokens = queries_hbm.shape[0]
    slots = cache_hbm.shape[0]
    half_slots = slots // 2
    tiles = LATENT_WIDTH // LANES
    half_rows = mine.shape[2] // 2
    core_rows = heads * tokens
    flat_rows = 2 * core_rows

    def chip(zz, yy, xx):
        return (zz * Y_CHIPS + yy) * X_CHIPS + xx

    middle = z % 3 != 0
    levels = [z, 1 + z % 2, 2 - 2 * (z % 2) + z // 2, 3 - 3 * (z // 2)]
    x_peer = (core, chip(z, y, 1 - x))
    y_peer = (core, chip(z, 1 - y, x))
    core_peer = (1 - core, place)
    pair_peer = (core, chip(z + 1 - 2 * (z % 2), y, x))
    mirror_peer = (core, chip(3 - z, y, x))
    partners = [x_peer, y_peer, core_peer, pair_peer, mirror_peer]

    barrier = pltpu.get_barrier_semaphore()
    for partner in partners:
        pl.semaphore_signal(barrier, inc=1, device_id=partner, device_id_type=MESH)

    local = [
        pltpu.make_async_copy(cache_hbm, cache_ref, local_sem.at[0]),
        pltpu.make_async_copy(queries_hbm, queries_ref.at[core], local_sem.at[1]),
        pltpu.make_async_copy(key_hbm, key_half, local_sem.at[2]),
        pltpu.make_async_copy(value_hbm, value_panel.at[core], local_sem.at[3]),
        pltpu.make_async_copy(prior_hbm, prior_ref, local_sem.at[4]),
    ]
    for copy in local:
        copy.start()
    local[0].wait()
    for c in range(tiles):
        mine[z, 0, c * slots:(c + 1) * slots, :] = cache_ref[:, c * LANES:(c + 1) * LANES]
    rotary_keys = cache_ref[:, LATENT_WIDTH:]
    mine[z, 0, tiles * slots:, :] = jnp.concatenate(
        [rotary_keys[:half_slots], rotary_keys[half_slots:]], axis=1
    )
    pl.semaphore_wait(barrier, len(partners))

    sends, middle_sends = [], []

    def send(src, dst, recv, to, only_middle=False):
        copy = pltpu.make_async_remote_copy(
            src_ref=src, dst_ref=dst, recv_sem=recv,
            send_sem=send_sem.at[len(sends) + len(middle_sends)],
            device_id=to, device_id_type=MESH,
        )
        if only_middle:
            pl.when(middle)(copy.start)
            middle_sends.append(copy)
        else:
            copy.start()
            sends.append(copy)
        return copy

    def arrived(ref, sem):
        pltpu.make_async_copy(ref, ref, sem).wait()

    def rows(k, p, half):
        return mine.at[k, p, pl.ds(half * half_rows, half_rows)]

    def share_column(i):
        k = levels[i]
        if i in (0, 3):
            send(rows(k, 0, 1), rows(k, 1, 1), mine_recv.at[k, 1], x_peer)
            send(rows(k, 0, 0), rows(k, 2, 0), mine_recv.at[k, 2], y_peer)
            send(rows(k, 0, 0), rows(k, 1, 0), rest_recv.at[k, 0], x_peer)
            send(rows(k, 0, 1), rows(k, 2, 1), rest_recv.at[k, 1], y_peer)
        else:
            send(mine.at[k, 0], mine.at[k, 1], mine_recv.at[k, 1], x_peer)
            send(mine.at[k, 0], mine.at[k, 2], mine_recv.at[k, 2], y_peer)

    def along_z(k, to, only_middle):
        return send(mine.at[k, 0], mine.at[k, 0], mine_recv.at[k, 0], to, only_middle)

    def column_step(i):
        k = levels[i]
        arrived(mine.at[k, 0], mine_recv.at[k, 0])
        if i == 1:
            along_z(k, pair_peer, True)
        share_column(i)

    def plane_step(i):
        k = levels[i]
        if i in (0, 3):
            arrived(rows(k, 1, 1), mine_recv.at[k, 1])
            send(rows(k, 1, 1), rows(k, 3, 1), half_recv.at[k, 1], y_peer)
            arrived(rows(k, 2, 0), mine_recv.at[k, 2])
            send(rows(k, 2, 0), rows(k, 3, 0), half_recv.at[k, 0], x_peer)
        else:
            arrived(mine.at[k, 1], mine_recv.at[k, 1])
            arrived(mine.at[k, 2], mine_recv.at[k, 2])

    def plane_rest(i):
        k = levels[i]
        arrived(rows(k, 1, 0), rest_recv.at[k, 0])
        arrived(rows(k, 2, 1), rest_recv.at[k, 1])

    def diagonal_along_z(k, to, only_middle):
        send(mine.at[k, 3], mine.at[k, 3], whole_recv.at[k], to, only_middle)

    def diagonal_step(i):
        k = levels[i]
        if i in (0, 3):
            for half in (0, 1):
                arrived(rows(k, 3, half), half_recv.at[k, half])
        else:
            arrived(mine.at[k, 3], whole_recv.at[k])
        if i == 0:
            diagonal_along_z(k, pair_peer, False)
            diagonal_along_z(k, mirror_peer, True)
        if i == 1:
            diagonal_along_z(k, pair_peer, True)

    def project_queries(first, last):
        zeros = jnp.zeros((2 * tokens, ROTARY_WIDTH), jnp.bfloat16)
        both = jnp.concatenate([queries_ref[0], queries_ref[1]], axis=0)
        for h in range(first, last):
            plain = both[:, h * HEAD_WIDTH:h * HEAD_WIDTH + PLAIN_WIDTH]
            rotary = both[:, h * HEAD_WIDTH + PLAIN_WIDTH:(h + 1) * HEAD_WIDTH]
            latent = jnp.dot(
                plain, key_half[h], preferred_element_type=jnp.float32
            ).astype(jnp.bfloat16)
            low = jnp.concatenate([rotary, zeros], axis=1)
            high = jnp.concatenate([zeros, rotary], axis=1)
            for c in (0, 1):
                there = slice(c * core_rows + h * tokens, c * core_rows + (h + 1) * tokens)
                of = slice(c * tokens, (c + 1) * tokens)
                query_latent[core, there, :] = latent[of]
                query_rotary[0, there, :] = low[of]
                query_rotary[1, there, :] = high[of]

    score_scale = HEAD_WIDTH ** (-0.5)
    group_slots = slots * Z_CHIPS * Y_CHIPS * X_CHIPS

    def attend(state, blocks, part_of=None):
        if part_of is None:
            here = pl.ds(0, flat_rows)
            flat_row = lax.broadcasted_iota(jnp.int32, (flat_rows, 1), 0)
            query_place = prior_ref[0] + flat_row // core_rows * tokens + flat_row % tokens
        else:
            here = pl.ds(pl.multiple_of(part_of * core_rows, core_rows), core_rows)
            flat_row = lax.broadcasted_iota(jnp.int32, (core_rows, 1), 0)
            query_place = prior_ref[0] + part_of * tokens + flat_row % tokens
        blocks = [(levels[i], p) for i, p in blocks]
        bases = []
        for k, p in blocks:
            source = chip(k, 1 - y if p in (2, 3) else y, 1 - x if p in (1, 3) else x)
            bases.append(core * group_slots + source * slots)
        width = 4 * half_slots

        def latent_of(part):
            return jnp.concatenate(
                [
                    jnp.concatenate(
                        [
                            mine[k, p, pl.ds(c * slots + part * half_slots, half_slots), :]
                            for c in range(tiles)
                        ],
                        axis=1,
                    )
                    for k, p in blocks
                ],
                axis=0,
            )

        latents = jnp.concatenate([latent_of(0), latent_of(1)], axis=0)
        rotary = jnp.concatenate(
            [mine[k, p, pl.ds(tiles * slots, half_slots), :] for k, p in blocks], axis=0
        )
        column = lax.broadcasted_iota(jnp.int32, (1, 2 * width), 1)
        key_place = column
        for b in range(8):
            inside = (column >= b * half_slots) & (column < (b + 1) * half_slots)
            shift = bases[b % 4] + (b // 4) * half_slots - b * half_slots
            key_place = key_place + jnp.where(inside, shift, 0)
        contract = (((1,), (1,)), ((), ()))
        rotary_scores = [
            lax.dot_general(
                query_rotary[part, here, :], rotary, contract, preferred_element_type=jnp.float32
            )
            for part in (0, 1)
        ]
        scores = lax.dot_general(
            jnp.concatenate([query_latent[0, here, :], query_latent[1, here, :]], axis=1), latents, contract,
            preferred_element_type=jnp.float32,
        )
        scores = (scores + jnp.concatenate(rotary_scores, axis=1)) * score_scale
        visible = key_place <= query_place
        scores = jnp.where(visible, scores, -1e30)
        peak = jnp.max(scores, axis=1, keepdims=True)
        if state is not None:
            peak = jnp.maximum(peak, state[0])
        probs = jnp.where(visible, jnp.exp(scores - peak), 0.0)
        total = jnp.sum(probs, axis=1, keepdims=True)
        weighted = jnp.dot(
            probs.astype(jnp.bfloat16), latents, preferred_element_type=jnp.float32
        )
        if state is None:
            numerator[here, :] = weighted
        else:
            shrink = jnp.exp(state[0] - peak)
            total = total + state[1] * shrink
            numerator[here, :] = numerator[here, :] * shrink + weighted
        return peak, total

    along_z(z, pair_peer, False)
    own_mirrored = along_z(z, mirror_peer, True)
    share_column(0)
    send(queries_hbm, queries_ref.at[core], core_recv.at[0], core_peer)
    local[4].wait()
    local[1].wait()
    local[2].wait()
    arrived(queries_ref.at[1 - core], core_recv.at[0])
    sends.append(middle_sends.pop(0))
    pl.when(jnp.logical_not(middle))(own_mirrored.start)
    project_queries(0, heads // 2)
    column_step(1)
    plane_step(0)

    @pl.when(middle)
    def _():
        arrived(mine.at[levels[2], 0], mine_recv.at[levels[2], 0])

    along_z(levels[2], mirror_peer, True)
    project_queries(heads // 2, heads)
    send(query_latent.at[core], query_latent.at[core], core_recv.at[1], core_peer)

    @pl.when(jnp.logical_not(middle))
    def _():
        arrived(mine.at[levels[2], 0], mine_recv.at[levels[2], 0])

    share_column(2)
    send(value_hbm, value_panel.at[core], core_recv.at[2], core_peer)
    diagonal_step(0)
    plane_rest(0)
    arrived(query_latent.at[1 - core], core_recv.at[1])
    state = attend(None, [(0, p) for p in range(4)])
    column_step(3)
    diagonal_step(1)
    plane_step(1)
    state = attend(state, [(1, p) for p in range(4)])
    plane_step(2)
    plane_step(3)
    state = attend(state, [(2, 0), (2, 1), (2, 2), (3, 0)])
    plane_rest(3)
    diagonal_step(2)
    diagonal_step(3)
    pick = core == 0
    low = [value[:core_rows] for value in state]
    high = [value[core_rows:] for value in state]
    last = [(2, 3), (3, 1), (3, 2), (3, 3)]
    their_state = [jnp.where(pick, b, a) for a, b in zip(low, high)]
    our_state = [jnp.where(pick, a, b) for a, b in zip(low, high)]
    peak, total = attend(their_state, last, 1 - core)
    lane = lax.broadcasted_iota(jnp.int32, (core_rows, LANES), 1)
    own_stats[...] = jnp.where(lane < LANES // 2, peak, total)
    theirs = pl.ds(pl.multiple_of((1 - core) * core_rows, core_rows), core_rows)
    ours = pl.ds(pl.multiple_of(core * core_rows, core_rows), core_rows)
    own_part[...] = numerator[theirs, :].astype(jnp.bfloat16)
    send(own_part, peer_part, core_recv.at[4], core_peer)
    send(own_stats, peer_stats, core_recv.at[3], core_peer)
    our_peak, our_total = attend(our_state, last, core)

    local[3].wait()
    arrived(value_panel.at[1 - core], core_recv.at[2])
    arrived(peer_stats, core_recv.at[3])
    their_peak = peer_stats[:, 0:1]
    their_total = peer_stats[:, LANES // 2:LANES // 2 + 1]
    joint_peak = jnp.maximum(our_peak, their_peak)
    our_weight = jnp.exp(our_peak - joint_peak)
    their_weight = jnp.exp(their_peak - joint_peak)
    joint_total = our_total * our_weight + their_total * their_weight
    our_weight = our_weight / joint_total
    their_weight = their_weight / joint_total
    arrived(peer_part, core_recv.at[4])
    averaged = (
        numerator[ours, :] * our_weight + peer_part[...].astype(jnp.float32) * their_weight
    ).astype(jnp.bfloat16)
    for h in range(heads):
        here = slice(h * tokens, (h + 1) * tokens)
        result = lax.dot_general(
            averaged[here], jnp.concatenate([value_panel[0, h], value_panel[1, h]], axis=1),
            (((1,), (1,)), ((), ())), preferred_element_type=jnp.float32,
        )
        out_ref[:, h * VALUE_WIDTH:(h + 1) * VALUE_WIDTH] = result.astype(jnp.bfloat16)
    for copy in sends:
        copy.wait_send()

    @pl.when(middle)
    def _():
        for copy in middle_sends:
            copy.wait_send()


def per_device_fused(queries, cache, key_up_weight, value_up_weight, prior_len):
    heads = key_up_weight.shape[0]
    tokens = queries.shape[0]
    slots = cache.shape[0]
    block_rows = slots * cache.shape[1] // LANES
    core_rows = heads * tokens
    hbm = pl.BlockSpec(memory_space=pltpu.HBM)
    dma = pltpu.SemaphoreType.DMA
    vmem = pltpu.VMEM
    return pl.pallas_call(
        fused_kernel,
        out_shape=jax.ShapeDtypeStruct((tokens, heads * VALUE_WIDTH), jnp.bfloat16),
        in_specs=[hbm, hbm, hbm, hbm, hbm],
        out_specs=pl.BlockSpec(memory_space=pltpu.VMEM),
        scratch_shapes=[
            pltpu.SMEM((1,), jnp.int32),
            vmem((2,) + queries.shape, jnp.bfloat16),
            vmem(cache.shape, jnp.bfloat16),
            vmem((4, 4, block_rows, LANES), jnp.bfloat16),
            vmem(key_up_weight.shape, jnp.bfloat16),
            vmem((2,) + value_up_weight.shape, jnp.bfloat16),
            vmem((2, 2 * core_rows, LATENT_WIDTH // 2), jnp.bfloat16),
            vmem((2, 2 * core_rows, LANES), jnp.bfloat16),
            vmem((2 * core_rows, LATENT_WIDTH), jnp.float32),
            vmem((core_rows, LATENT_WIDTH), jnp.bfloat16),
            vmem((core_rows, LATENT_WIDTH), jnp.bfloat16),
            vmem((core_rows, LANES), jnp.float32),
            vmem((core_rows, LANES), jnp.float32),
            dma((4, 3)), dma((4, 2)), dma((4, 2)), dma((4,)), dma((40,)), dma((5,)), dma((5,)),
        ],
        compiler_params=pltpu.CompilerParams(
            collective_id=0, has_side_effects=True, vmem_limit_bytes=(64 * 1024 - 10375) * 1024
        ),
    )(queries, cache, key_up_weight, value_up_weight, prior_len)


def solution(mesh):
    in_specs = (
        P("ctx", "head"),
        P(("ctx", "head"), None),
        P("head", None, "ctx"),
        P("head", None, "ctx"),
        P(),
    )
    out_specs = P("ctx", "head")
    chips = Z_CHIPS * Y_CHIPS * X_CHIPS
    body = per_device_fused if mesh.shape["ctx"] == 2 and mesh.shape["head"] == chips else per_device
    return jax.shard_map(
        body, mesh=mesh, in_specs=in_specs, out_specs=out_specs, check_vma=False
    )
```

```python
import jax
import jax.numpy as jnp
from jax import lax
from jax.experimental import pallas as pl
from jax.experimental.pallas import tpu as pltpu
from jax.sharding import PartitionSpec as P

PLAIN_WIDTH = 128
ROTARY_WIDTH = 64
LATENT_WIDTH = 512
VALUE_WIDTH = 128


def per_device(queries, cache, key_up_weight, value_up_weight, prior_len):
    heads_number = key_up_weight.shape[0]
    block_rows = queries.shape[0]
    combined_width = LATENT_WIDTH + ROTARY_WIDTH
    key_panel, value_panel = (
        lax.all_gather(key_up_weight, "ctx", axis=2, tiled=True),
        lax.all_gather(value_up_weight, "ctx", axis=2, tiled=True),
    )
    gathered = lax.all_gather(queries, "ctx", axis=0, tiled=True)
    split_rows = gathered.reshape(gathered.shape[0], heads_number, PLAIN_WIDTH + ROTARY_WIDTH)
    latent = jnp.einsum(
        "thn,hnc->thc",
        split_rows[:, :, :PLAIN_WIDTH],
        key_panel,
        preferred_element_type=jnp.float32,
    ).astype(jnp.bfloat16)
    flat_queries = jnp.concatenate([latent, split_rows[:, :, PLAIN_WIDTH:]], axis=2).reshape(
        -1, combined_width
    )
    flat_rows = flat_queries.shape[0]
    query_number = flat_rows // heads_number
    query_place = prior_len[0] + jnp.arange(flat_rows, dtype=jnp.int32) // heads_number
    group_slots = cache.shape[0] * lax.axis_size("head")
    block_base = lax.axis_index("ctx") * group_slots
    score_scale = (PLAIN_WIDTH + ROTARY_WIDTH) ** (-0.5)
    key_section = lax.all_gather(cache, "head", axis=0, tiled=True)
    row_peak = jnp.full((flat_rows,), -1e30, jnp.float32)
    key_count = key_section.shape[0]
    scores = (
        jnp.einsum("rc,nc->rn", flat_queries, key_section, preferred_element_type=jnp.float32)
        * score_scale
    )
    key_place = block_base + jnp.arange(key_count, dtype=jnp.int32)
    visible = key_place[None, :] <= query_place[:, None]
    scores = jnp.where(visible, scores, jnp.float32(-1e30))
    new_peak = jnp.maximum(row_peak, jnp.max(scores, axis=1))
    probabilities = jnp.where(visible, jnp.exp(scores - new_peak[:, None]), jnp.float32(0.0))
    row_total = jnp.sum(probabilities, axis=1)
    weighted_values = jnp.dot(
        probabilities.astype(jnp.bfloat16),
        key_section[:, :LATENT_WIDTH],
        preferred_element_type=jnp.float32,
    )
    row_peak, row_total, weighted_values = (new_peak, row_total, weighted_values)
    global_peak = lax.pmax(row_peak, "ctx")
    softmax_scale = jnp.exp(row_peak - global_peak)
    scaled_sums = (row_total * softmax_scale).reshape(query_number, heads_number)
    latent_scaled = (weighted_values * softmax_scale[:, None]).reshape(
        query_number, heads_number * LATENT_WIDTH
    )
    block_latent, own_totals = (
        lax.psum_scatter(
            latent_scaled.astype(jnp.bfloat16), "ctx", scatter_dimension=0, tiled=True
        ).astype(jnp.float32),
        lax.psum_scatter(
            scaled_sums.astype(jnp.bfloat16), "ctx", scatter_dimension=0, tiled=True
        ).astype(jnp.float32),
    )
    reshaped_queries = block_latent.reshape(block_rows, heads_number, LATENT_WIDTH)
    projected = jnp.einsum(
        "thc,hvc->thv",
        reshaped_queries,
        value_panel.astype(jnp.float32),
        precision=lax.Precision.HIGHEST,
    )
    result = projected / own_totals[:, :, None]
    return result.reshape(block_rows, heads_number * VALUE_WIDTH).astype(jnp.bfloat16)


MESH = pl.DeviceIdType.MESH
HEAD_WIDTH = PLAIN_WIDTH + ROTARY_WIDTH
Z_CHIPS, Y_CHIPS, X_CHIPS = 4, 2, 2
LANES = 128


def fused_kernel(
    queries_hbm, cache_hbm, key_hbm, value_hbm, prior_ref, out_ref,
    queries_ref, cache_ref, mine, key_half, value_panel, query_latent, query_rotary,
    numerator, own_part, peer_part, own_stats, peer_stats,
    mine_recv, rest_recv, half_recv, whole_recv, send_sem, core_recv, local_sem,
):
    core = lax.axis_index("ctx")
    place = lax.axis_index("head")
    z = place // (Y_CHIPS * X_CHIPS)
    y = (place // X_CHIPS) % Y_CHIPS
    x = place % X_CHIPS
    heads = key_hbm.shape[0]
    tokens = queries_hbm.shape[0]
    slots = cache_hbm.shape[0]
    half_slots = slots // 2
    tiles = LATENT_WIDTH // LANES
    half_rows = mine.shape[2] // 2
    core_rows = heads * tokens
    flat_rows = 2 * core_rows

    def chip(zz, yy, xx):
        return (zz * Y_CHIPS + yy) * X_CHIPS + xx

    middle = z % 3 != 0
    levels = [z, 1 + z % 2, 2 - 2 * (z % 2) + z // 2, 3 - 3 * (z // 2)]
    x_peer = (core, chip(z, y, 1 - x))
    y_peer = (core, chip(z, 1 - y, x))
    core_peer = (1 - core, place)
    pair_peer = (core, chip(z + 1 - 2 * (z % 2), y, x))
    mirror_peer = (core, chip(3 - z, y, x))
    partners = [x_peer, y_peer, core_peer, pair_peer, mirror_peer]

    barrier = pltpu.get_barrier_semaphore()
    for partner in partners:
        pl.semaphore_signal(barrier, inc=1, device_id=partner, device_id_type=MESH)

    local = [
        pltpu.make_async_copy(cache_hbm, cache_ref, local_sem.at[0]),
        pltpu.make_async_copy(queries_hbm, queries_ref.at[core], local_sem.at[1]),
        pltpu.make_async_copy(key_hbm, key_half, local_sem.at[2]),
        pltpu.make_async_copy(value_hbm, value_panel.at[core], local_sem.at[3]),
    ]
    for copy in local:
        copy.start()
    local[0].wait()
    for c in range(tiles):
        mine[z, 0, c * slots:(c + 1) * slots, :] = cache_ref[:, c * LANES:(c + 1) * LANES]
    rotary_keys = cache_ref[:, LATENT_WIDTH:]
    mine[z, 0, tiles * slots:, :] = jnp.concatenate(
        [rotary_keys[:half_slots], rotary_keys[half_slots:]], axis=1
    )
    pl.semaphore_wait(barrier, len(partners))

    sends, middle_sends = [], []

    def send(src, dst, recv, to, only_middle=False):
        copy = pltpu.make_async_remote_copy(
            src_ref=src, dst_ref=dst, recv_sem=recv,
            send_sem=send_sem.at[len(sends) + len(middle_sends)],
            device_id=to, device_id_type=MESH,
        )
        if only_middle:
            pl.when(middle)(copy.start)
            middle_sends.append(copy)
        else:
            copy.start()
            sends.append(copy)
        return copy

    def arrived(ref, sem):
        pltpu.make_async_copy(ref, ref, sem).wait()

    def rows(k, p, half):
        return mine.at[k, p, pl.ds(half * half_rows, half_rows)]

    def share_column(i):
        k = levels[i]
        if i in (0, 3):
            send(rows(k, 0, 1), rows(k, 1, 1), mine_recv.at[k, 1], x_peer)
            send(rows(k, 0, 0), rows(k, 2, 0), mine_recv.at[k, 2], y_peer)
            send(rows(k, 0, 0), rows(k, 1, 0), rest_recv.at[k, 0], x_peer)
            send(rows(k, 0, 1), rows(k, 2, 1), rest_recv.at[k, 1], y_peer)
        else:
            send(mine.at[k, 0], mine.at[k, 1], mine_recv.at[k, 1], x_peer)
            send(mine.at[k, 0], mine.at[k, 2], mine_recv.at[k, 2], y_peer)

    def along_z(k, to, only_middle):
        return send(mine.at[k, 0], mine.at[k, 0], mine_recv.at[k, 0], to, only_middle)

    def column_step(i):
        k = levels[i]
        arrived(mine.at[k, 0], mine_recv.at[k, 0])
        if i == 1:
            along_z(k, pair_peer, True)
        share_column(i)

    def plane_step(i):
        k = levels[i]
        if i in (0, 3):
            arrived(rows(k, 1, 1), mine_recv.at[k, 1])
            send(rows(k, 1, 1), rows(k, 3, 1), half_recv.at[k, 1], y_peer)
            arrived(rows(k, 2, 0), mine_recv.at[k, 2])
            send(rows(k, 2, 0), rows(k, 3, 0), half_recv.at[k, 0], x_peer)
        else:
            arrived(mine.at[k, 1], mine_recv.at[k, 1])
            arrived(mine.at[k, 2], mine_recv.at[k, 2])

    def plane_rest(i):
        k = levels[i]
        arrived(rows(k, 1, 0), rest_recv.at[k, 0])
        arrived(rows(k, 2, 1), rest_recv.at[k, 1])

    def diagonal_along_z(k, to, only_middle):
        send(mine.at[k, 3], mine.at[k, 3], whole_recv.at[k], to, only_middle)

    def diagonal_step(i):
        k = levels[i]
        if i in (0, 3):
            for half in (0, 1):
                arrived(rows(k, 3, half), half_recv.at[k, half])
        else:
            arrived(mine.at[k, 3], whole_recv.at[k])
        if i == 0:
            diagonal_along_z(k, pair_peer, False)
            diagonal_along_z(k, mirror_peer, True)
        if i == 1:
            diagonal_along_z(k, pair_peer, True)

    def project_queries(first, last):
        zeros = jnp.zeros((2 * tokens, ROTARY_WIDTH), jnp.bfloat16)
        both = jnp.concatenate([queries_ref[0], queries_ref[1]], axis=0)
        for h in range(first, last):
            plain = both[:, h * HEAD_WIDTH:h * HEAD_WIDTH + PLAIN_WIDTH]
            rotary = both[:, h * HEAD_WIDTH + PLAIN_WIDTH:(h + 1) * HEAD_WIDTH]
            latent = jnp.dot(
                plain, key_half[h], preferred_element_type=jnp.float32
            ).astype(jnp.bfloat16)
            low = jnp.concatenate([rotary, zeros], axis=1)
            high = jnp.concatenate([zeros, rotary], axis=1)
            for c in (0, 1):
                there = slice(c * core_rows + h * tokens, c * core_rows + (h + 1) * tokens)
                of = slice(c * tokens, (c + 1) * tokens)
                query_latent[core, there, :] = latent[of]
                query_rotary[0, there, :] = low[of]
                query_rotary[1, there, :] = high[of]

    score_scale = HEAD_WIDTH ** (-0.5)
    group_slots = slots * Z_CHIPS * Y_CHIPS * X_CHIPS

    def attend(state, blocks, part_of=None):
        if part_of is None:
            here = pl.ds(0, flat_rows)
            flat_row = lax.broadcasted_iota(jnp.int32, (flat_rows, 1), 0)
            query_place = prior_ref[0] + flat_row // core_rows * tokens + flat_row % tokens
        else:
            here = pl.ds(pl.multiple_of(part_of * core_rows, core_rows), core_rows)
            flat_row = lax.broadcasted_iota(jnp.int32, (core_rows, 1), 0)
            query_place = prior_ref[0] + part_of * tokens + flat_row % tokens
        blocks = [(levels[i], p) for i, p in blocks]
        bases = []
        for k, p in blocks:
            source = chip(k, 1 - y if p in (2, 3) else y, 1 - x if p in (1, 3) else x)
            bases.append(core * group_slots + source * slots)
        count = len(blocks)
        width = count * half_slots

        def latent_of(part):
            return jnp.concatenate(
                [
                    jnp.concatenate(
                        [
                            mine[k, p, pl.ds(c * slots + part * half_slots, half_slots), :]
                            for c in range(tiles)
                        ],
                        axis=1,
                    )
                    for k, p in blocks
                ],
                axis=0,
            )

        latents = jnp.concatenate([latent_of(0), latent_of(1)], axis=0)
        rotary = jnp.concatenate(
            [mine[k, p, pl.ds(tiles * slots, half_slots), :] for k, p in blocks], axis=0
        )
        column = lax.broadcasted_iota(jnp.int32, (1, 2 * width), 1)
        key_place = column
        for b in range(2 * count):
            inside = (column >= b * half_slots) & (column < (b + 1) * half_slots)
            shift = bases[b % count] + (b // count) * half_slots - b * half_slots
            key_place = key_place + jnp.where(inside, shift, 0)
        contract = (((1,), (1,)), ((), ()))
        rotary_scores = [
            lax.dot_general(
                query_rotary[part, here, :], rotary, contract, preferred_element_type=jnp.float32
            )
            for part in (0, 1)
        ]
        scores = lax.dot_general(
            jnp.concatenate([query_latent[0, here, :], query_latent[1, here, :]], axis=1), latents, contract,
            preferred_element_type=jnp.float32,
        )
        scores = (scores + jnp.concatenate(rotary_scores, axis=1)) * score_scale
        visible = key_place <= query_place
        scores = jnp.where(visible, scores, -1e30)
        peak = jnp.max(scores, axis=1, keepdims=True)
        if state is not None:
            peak = jnp.maximum(peak, state[0])
        probs = jnp.where(visible, jnp.exp(scores - peak), 0.0)
        total = jnp.sum(probs, axis=1, keepdims=True)
        weighted = jnp.dot(
            probs.astype(jnp.bfloat16), latents, preferred_element_type=jnp.float32
        )
        if state is None:
            numerator[here, :] = weighted
        else:
            shrink = jnp.exp(state[0] - peak)
            total = total + state[1] * shrink
            numerator[here, :] = numerator[here, :] * shrink + weighted
        return peak, total

    along_z(z, pair_peer, False)
    own_mirrored = along_z(z, mirror_peer, True)
    share_column(0)
    send(queries_hbm, queries_ref.at[core], core_recv.at[0], core_peer)
    local[1].wait()
    local[2].wait()
    arrived(queries_ref.at[1 - core], core_recv.at[0])
    project_queries(0, heads // 2)
    sends.append(middle_sends.pop(0))
    pl.when(jnp.logical_not(middle))(own_mirrored.start)
    column_step(1)
    plane_step(0)

    @pl.when(middle)
    def _():
        arrived(mine.at[levels[2], 0], mine_recv.at[levels[2], 0])

    along_z(levels[2], mirror_peer, True)
    project_queries(heads // 2, heads)
    send(query_latent.at[core], query_latent.at[core], core_recv.at[1], core_peer)

    @pl.when(jnp.logical_not(middle))
    def _():
        arrived(mine.at[levels[2], 0], mine_recv.at[levels[2], 0])

    share_column(2)
    send(value_hbm, value_panel.at[core], core_recv.at[2], core_peer)
    diagonal_step(0)
    plane_rest(0)
    arrived(query_latent.at[1 - core], core_recv.at[1])
    column_step(3)
    diagonal_step(1)
    plane_step(1)
    state = attend(None, [(i, p) for i in (0, 1) for p in range(4)])
    plane_step(2)
    plane_step(3)
    state = attend(state, [(2, 0), (2, 1), (2, 2), (3, 0)])
    plane_rest(3)
    diagonal_step(2)
    diagonal_step(3)
    pick = core == 0
    low = [value[:core_rows] for value in state]
    high = [value[core_rows:] for value in state]
    last = [(2, 3), (3, 1), (3, 2), (3, 3)]
    their_state = [jnp.where(pick, b, a) for a, b in zip(low, high)]
    our_state = [jnp.where(pick, a, b) for a, b in zip(low, high)]
    peak, total = attend(their_state, last, 1 - core)
    lane = lax.broadcasted_iota(jnp.int32, (core_rows, LANES), 1)
    own_stats[...] = jnp.where(lane < LANES // 2, peak, total)
    theirs = pl.ds(pl.multiple_of((1 - core) * core_rows, core_rows), core_rows)
    ours = pl.ds(pl.multiple_of(core * core_rows, core_rows), core_rows)
    own_part[...] = numerator[theirs, :].astype(jnp.bfloat16)
    send(own_part, peer_part, core_recv.at[4], core_peer)
    send(own_stats, peer_stats, core_recv.at[3], core_peer)
    our_peak, our_total = attend(our_state, last, core)

    local[3].wait()
    arrived(value_panel.at[1 - core], core_recv.at[2])
    arrived(peer_stats, core_recv.at[3])
    their_peak = peer_stats[:, 0:1]
    their_total = peer_stats[:, LANES // 2:LANES // 2 + 1]
    joint_peak = jnp.maximum(our_peak, their_peak)
    our_weight = jnp.exp(our_peak - joint_peak)
    their_weight = jnp.exp(their_peak - joint_peak)
    joint_total = our_total * our_weight + their_total * their_weight
    our_weight = our_weight / joint_total
    their_weight = their_weight / joint_total
    arrived(peer_part, core_recv.at[4])
    averaged = (
        numerator[ours, :] * our_weight + peer_part[...].astype(jnp.float32) * their_weight
    ).astype(jnp.bfloat16)
    for h in range(heads):
        here = slice(h * tokens, (h + 1) * tokens)
        result = lax.dot_general(
            averaged[here], jnp.concatenate([value_panel[0, h], value_panel[1, h]], axis=1),
            (((1,), (1,)), ((), ())), preferred_element_type=jnp.float32,
        )
        out_ref[:, h * VALUE_WIDTH:(h + 1) * VALUE_WIDTH] = result.astype(jnp.bfloat16)
    for copy in sends:
        copy.wait_send()

    @pl.when(middle)
    def _():
        for copy in middle_sends:
            copy.wait_send()


def per_device_fused(queries, cache, key_up_weight, value_up_weight, prior_len):
    heads = key_up_weight.shape[0]
    tokens = queries.shape[0]
    slots = cache.shape[0]
    block_rows = slots * cache.shape[1] // LANES
    core_rows = heads * tokens
    hbm = pl.BlockSpec(memory_space=pltpu.HBM)
    dma = pltpu.SemaphoreType.DMA
    vmem = pltpu.VMEM
    return pl.pallas_call(
        fused_kernel,
        out_shape=jax.ShapeDtypeStruct((tokens, heads * VALUE_WIDTH), jnp.bfloat16),
        in_specs=[hbm, hbm, hbm, hbm, pl.BlockSpec(memory_space=pltpu.SMEM)],
        out_specs=pl.BlockSpec(memory_space=pltpu.VMEM),
        scratch_shapes=[
            vmem((2,) + queries.shape, jnp.bfloat16),
            vmem(cache.shape, jnp.bfloat16),
            vmem((4, 4, block_rows, LANES), jnp.bfloat16),
            vmem(key_up_weight.shape, jnp.bfloat16),
            vmem((2,) + value_up_weight.shape, jnp.bfloat16),
            vmem((2, 2 * core_rows, LATENT_WIDTH // 2), jnp.bfloat16),
            vmem((2, 2 * core_rows, LANES), jnp.bfloat16),
            vmem((2 * core_rows, LATENT_WIDTH), jnp.float32),
            vmem((core_rows, LATENT_WIDTH), jnp.bfloat16),
            vmem((core_rows, LATENT_WIDTH), jnp.bfloat16),
            vmem((core_rows, LANES), jnp.float32),
            vmem((core_rows, LANES), jnp.float32),
            dma((4, 3)), dma((4, 2)), dma((4, 2)), dma((4,)), dma((40,)), dma((5,)), dma((4,)),
        ],
        compiler_params=pltpu.CompilerParams(
            collective_id=0, has_side_effects=True, vmem_limit_bytes=(64 * 1024 - 10375) * 1024
        ),
    )(queries, cache, key_up_weight, value_up_weight, prior_len)


def solution(mesh):
    in_specs = (
        P("ctx", "head"),
        P(("ctx", "head"), None),
        P("head", None, "ctx"),
        P("head", None, "ctx"),
        P(),
    )
    out_specs = P("ctx", "head")
    chips = Z_CHIPS * Y_CHIPS * X_CHIPS
    body = per_device_fused if mesh.shape["ctx"] == 2 and mesh.shape["head"] == chips else per_device
    return jax.shard_map(
        body, mesh=mesh, in_specs=in_specs, out_specs=out_specs, check_vma=False
    )
```
